256 devices in a mesh: section: 4 (over z_hi), dp: 8 (over y, core), tensor: 8 (over x, z_lo).
Axes of the slice: x: 4, y: 4, z: 8 (z_hi: 4, z_lo: 2; z = z_hi * 2 + z_lo), core: 2. Of those that a mesh axis runs over, the one named last changes fastest.
Arguments:
- enc_out: bfloat16 [8, 512, 4096], P('dp', 'section'), may hold values from -6 to 6
- key_weight: bfloat16 [4, 4096, 4096], P('section', None, 'tensor'), may hold values from -0.09375 to 0.09375
- value_weight: bfloat16 [4, 4096, 4096], P('section', None, 'tensor'), may hold values from -0.09375 to 0.09375
- queries: bfloat16 [4, 8, 512, 4096], P('section', 'dp', None, 'tensor'), may hold values from -1024 to 1024
- ctx_grad: bfloat16 [4, 8, 512, 4096], P('section', 'dp', None, 'tensor'), may hold values from -12 to 12
- src_pad: int32 [8], P('dp'), may hold values from 0 to 384, as said below
- tgt_pad: int32 [8], P('dp'), may hold values from 0 to 256, as said below
Outputs:
- context: bfloat16 [4, 8, 512, 4096], P('section', 'dp', None, 'tensor')
- enc_grad: bfloat16 [8, 512, 4096], P('dp', 'section')
- key_weight_grad: bfloat16 [4, 4096, 4096], P('section', 'dp', 'tensor')
- value_weight_grad: bfloat16 [4, 4096, 4096], P('section', 'dp', 'tensor')
The draws below stay inside these ranges and needn't reach their ends.
Inputs may be any that keep to these rules, and one draw needn't show every extreme that they name: `src_pad`: some sequence has no source padding and some has the most. `tgt_pad`: some sequence has no target padding and some has the most.
All inputs are finite; a program needn't handle non-finite values.
Results may differ from the reference program's by a relative error of at most 0.023.
The reference program's roundings to bfloat16 on the way (of `key_rows`, `value_rows`, `weights_low`, `grad_in`, `score_grad`, `value_act` and `key_act`) count: a program that leaves them out, or rounds other values in their place, can miss the bound.
Values may be sent and summed in bfloat16 or wider, within the bound.
No kernel may reach another device: no remote copies, remote signals or barrier semaphores. Data moves between devices by JAX's collectives and lax.ppermute only.
A program may use at most 128 MiB of HBM per device.

```python
import jax
import jax.numpy as jnp

D = 4096
HEADS = 16
HEAD = 256
SRC = 512
TGT = 512
SECTIONS = 4
BATCH = 8
HD = 4096


def encoder_rows(base_key):
    sub_key = jax.random.fold_in(base_key, 11)
    return jnp.clip(jax.random.normal(sub_key, (BATCH, SRC, D), jnp.float32), -6.0, 6.0)


def key_matrix(base_key):
    sub_key = jax.random.fold_in(base_key, 12)
    normal_draw = jax.random.normal(sub_key, (SECTIONS, D, HEADS * HEAD), jnp.float32)
    return jnp.clip(normal_draw, -6.0, 6.0) * D ** (-0.5)


def draw_enc_out(key, part):
    base_key = key
    return encoder_rows(base_key).astype(jnp.bfloat16)


def draw_key_weight(key, part):
    base_key = key
    return key_matrix(base_key).astype(jnp.bfloat16)


def draw_queries(key, part):
    key = jax.random.fold_in(key, 23)
    full_shape = (SECTIONS, BATCH, TGT, HEADS * HEAD)
    query_draw = jax.random.normal(key, full_shape, jnp.float32)
    return query_draw.astype(jnp.bfloat16)


def padding_draw(key, largest):
    first_key, second_key = jax.random.split(key)
    values = jax.random.randint(first_key, (BATCH,), 0, largest + 1)
    shuffled = jax.random.permutation(second_key, BATCH)
    values = values.at[shuffled[0]].set(0).at[shuffled[1]].set(largest)
    return values.astype(jnp.int32)


def draw_src_pad(key, part):
    key = jax.random.fold_in(key, 24)
    return padding_draw(key, SRC - SRC // 4)


def draw_tgt_pad(key, part):
    key = jax.random.fold_in(key, 25)
    return padding_draw(key, TGT // 2)


def block_scale(stream_key, extent, shards, smallest, high):
    factor_of, own = 1.0, jax.random.fold_in(stream_key, 6)
    for position, shards_of in shards:
        heights = jnp.exp(jax.random.uniform(jax.random.fold_in(own, position), (shards_of,), jnp.float32, smallest / len(shards), high / len(shards)))
        factor_of = factor_of * jnp.repeat(heights, extent[position] // shards_of).reshape([-1 if axis == position else 1 for axis in range(len(extent))])
    return factor_of


def gaussian(own_key, dims, scale, limit, pieces=(), held_as=jnp.bfloat16):
    result = jax.random.normal(own_key, dims, jnp.float32) * scale
    if len(pieces) > 0:
        result = block_scale(own_key, dims, pieces, -0.22, 0.18) * result
    return jnp.clip(result, min=-limit, max=limit).astype(held_as)


def setup_inputs(seed: int = 0) -> dict:
    arg_keys = jax.random.split(jax.random.key(seed), 8)
    enc_out = draw_enc_out(jax.random.fold_in(arg_keys[7], 71), 0)
    key_weight = draw_key_weight(jax.random.fold_in(arg_keys[7], 71), 0)
    value_weight = gaussian(arg_keys[2], (SECTIONS, D, HD), D ** -0.5, 0.09375, ((0, 4), (2, 8)))
    queries = draw_queries(jax.random.fold_in(arg_keys[7], 71), 0)
    ctx_grad = gaussian(arg_keys[4], (SECTIONS, BATCH, TGT, HD), 2.0, 12.0, ((0, 4), (1, 8), (3, 8)))
    src_pad = draw_src_pad(jax.random.fold_in(arg_keys[7], 71), 0)
    tgt_pad = draw_tgt_pad(jax.random.fold_in(arg_keys[7], 71), 0)
    return {"enc_out": enc_out, "key_weight": key_weight, "value_weight": value_weight, "queries": queries, "ctx_grad": ctx_grad, "src_pad": src_pad, "tgt_pad": tgt_pad}


masked_score = -1.0e30


def softmax_rows(scores):
    highest = jnp.max(scores, axis=-1, keepdims=True)
    shifted = jnp.exp(scores - highest)
    return shifted / jnp.sum(shifted, axis=-1, keepdims=True)


def reference(enc_out, key_weight, value_weight, queries, ctx_grad, src_pad, tgt_pad):
    score_scale = HEAD ** -0.5
    key_valid = jnp.arange(SRC)[None, :] < (SRC - src_pad)[:, None]
    target_live = jnp.arange(TGT)[None, :] < (TGT - tgt_pad)[:, None]
    enc_flat = enc_out.reshape(BATCH * SRC, D)
    enc_total = jnp.zeros((BATCH * SRC, D), jnp.float32)
    contexts = []
    key_grads = []
    value_grads = []
    for section_index in range(SECTIONS):
        key_proj = key_weight[section_index]
        value_proj = value_weight[section_index]
        key_rows = jnp.dot(enc_flat, key_proj, preferred_element_type=jnp.float32).astype(jnp.bfloat16)
        value_rows = jnp.dot(enc_flat, value_proj, preferred_element_type=jnp.float32).astype(jnp.bfloat16)
        key_heads = key_rows.reshape(BATCH, SRC, HEADS, HEAD).astype(jnp.float32)
        value_heads = value_rows.reshape(BATCH, SRC, HEADS, HEAD).astype(jnp.float32)
        query_heads = queries[section_index].reshape(BATCH, TGT, HEADS, HEAD).astype(jnp.float32)
        scores = jnp.einsum("bthe,bshe->bhts", query_heads, key_heads) * score_scale
        scores = jnp.where(key_valid[:, None, None, :], scores, masked_score)
        soft_weights = softmax_rows(scores)
        weights_low = soft_weights.astype(jnp.bfloat16)
        context = jnp.einsum("bhts,bshe->bthe", weights_low.astype(jnp.float32), value_heads).astype(jnp.bfloat16)
        contexts.append(context.reshape(BATCH, TGT, HD))
        grad_in = jnp.where(target_live[:, :, None], ctx_grad[section_index], jnp.zeros((), jnp.bfloat16))
        grad_heads = grad_in.reshape(BATCH, TGT, HEADS, HEAD).astype(jnp.float32)
        prob_grad = jnp.einsum("bthe,bshe->bhts", grad_heads, value_heads)
        prob_dot = jnp.sum(soft_weights * prob_grad, axis=-1, keepdims=True)
        score_grad = (soft_weights * (prob_grad - prob_dot) * score_scale).astype(jnp.bfloat16)
        value_act = jnp.einsum("bhts,bthe->bshe", weights_low.astype(jnp.float32), grad_heads).astype(jnp.bfloat16)
        key_act = jnp.einsum("bhts,bthe->bshe", score_grad.astype(jnp.float32), query_heads).astype(jnp.bfloat16)
        value_act = value_act.reshape(BATCH * SRC, HD)
        key_act = key_act.reshape(BATCH * SRC, HD)
        enc_total = enc_total + jnp.dot(key_act, key_proj.T, preferred_element_type=jnp.float32)
        enc_total = enc_total + jnp.dot(value_act, value_proj.T, preferred_element_type=jnp.float32)
        key_grads.append(jnp.dot(enc_flat.T, key_act, preferred_element_type=jnp.float32).astype(jnp.bfloat16))
        value_grads.append(jnp.dot(enc_flat.T, value_act, preferred_element_type=jnp.float32).astype(jnp.bfloat16))
    enc_grad = enc_total.reshape(BATCH, SRC, D).astype(jnp.bfloat16)
    return (jnp.stack(contexts), enc_grad, jnp.stack(key_grads), jnp.stack(value_grads))
```

```python
import jax
import jax.numpy as jnp
from jax import lax
from jax.sharding import PartitionSpec as P

HEAD = 256
XS = 4
masked_score = -1e30
f32 = jnp.float32
bf16 = jnp.bfloat16


def dot(a, b):
    return jnp.dot(a, b, preferred_element_type=f32)


def dot_t(a, b):
    return lax.dot_general(a, b, (((1,), (1,)), ((), ())), preferred_element_type=f32)


def t_dot(a, b):
    return lax.dot_general(a, b, (((0,), (0,)), ((), ())), preferred_element_type=f32)


def shift_section(v, k, n):
    return lax.ppermute(v, "section", [(i, (i + k) % n) for i in range(n)])


def shift_x(v, k, n):
    lo = n // XS
    return lax.ppermute(
        v,
        "tensor",
        [(x * lo + l, ((x + k) % XS) * lo + l) for x in range(XS) for l in range(lo)],
    )


def swap_lo(v, n):
    return lax.ppermute(v, "tensor", [(i, i ^ 1) for i in range(n)])


def make_shards(mesh):
    n_sec = mesh.shape["section"]
    n_ten = mesh.shape["tensor"]

    def shards(enc_out, key_weight, value_weight, queries, ctx_grad, src_pad, tgt_pad):
        blk = enc_out.shape[1]
        width = enc_out.shape[2]
        quarter = width // XS
        key_proj = key_weight[0]
        value_proj = value_weight[0]
        local_width = key_proj.shape[1]
        heads_here = local_width // HEAD
        target_count = queries.shape[2]
        total_src = n_sec * blk
        score_scale = HEAD ** (-0.5)
        x = lax.axis_index("tensor") // (n_ten // XS)
        s = lax.axis_index("section")
        enc = enc_out[0]

        def col_quarter(m):
            return lax.dynamic_slice(enc, (0, ((x - m) % XS) * quarter), (blk, quarter))

        own = [col_quarter(m) for m in range(XS)]
        sec = [shift_section(own[0], k, n_sec) for k in range(1, n_sec)]
        g0 = jnp.concatenate(sec, axis=0)
        half = g0.shape[0] // 2
        g1 = shift_x(g0, 1, n_ten)
        g3 = shift_x(g0, -1, n_ten)
        g2a = shift_x(g1[:half], 1, n_ten)
        g2b = shift_x(g3[half:], -1, n_ten)
        g2 = jnp.concatenate([g2a, g2b], axis=0)
        rows = [jnp.concatenate([o, g], axis=0) for o, g in zip(own, (g0, g1, g2, g3))]

        w_rel = []
        for m in range(XS):
            at = ((x - m) % XS) * quarter
            w_rel.append(
                jnp.concatenate(
                    [
                        lax.dynamic_slice(key_proj, (at, 0), (quarter, local_width)),
                        lax.dynamic_slice(value_proj, (at, 0), (quarter, local_width)),
                    ],
                    axis=1,
                )
            )
        acc = dot(rows[0], w_rel[0])
        for m in (1, 3, 2):
            acc = acc + dot(rows[m], w_rel[m])
        kv = acc.astype(bf16)
        key_heads = kv[:, :local_width].reshape(total_src, heads_here, HEAD)
        value_heads = kv[:, local_width:].reshape(total_src, heads_here, HEAD)
        query_heads = queries[0, 0].reshape(target_count, heads_here, HEAD)

        j = jnp.arange(total_src)
        source = ((s - j // blk) % n_sec) * blk + j % blk
        key_valid = source < total_src - src_pad[0]
        scores = (
            jnp.einsum("the,she->hts", query_heads, key_heads, preferred_element_type=f32)
            * score_scale
        )
        scores = jnp.where(key_valid[None, None, :], scores, masked_score)
        highest = jnp.max(scores, axis=-1, keepdims=True)
        shifted = jnp.exp(scores - highest)
        soft_weights = shifted / jnp.sum(shifted, axis=-1, keepdims=True)
        weights_low = soft_weights.astype(bf16)
        context = jnp.einsum("hts,she->the", weights_low, value_heads, preferred_element_type=f32)
        context = context.astype(bf16).reshape(1, 1, target_count, local_width)
        target_live = jnp.arange(target_count) < target_count - tgt_pad[0]
        grad_in = jnp.where(target_live[:, None], ctx_grad[0, 0], jnp.zeros((), bf16))
        grad_heads = grad_in.reshape(target_count, heads_here, HEAD)
        value_act = jnp.einsum("hts,the->she", weights_low, grad_heads, preferred_element_type=f32)
        value_act = value_act.astype(bf16).reshape(total_src, local_width)
        prob_grad = jnp.einsum("the,she->hts", grad_heads, value_heads, preferred_element_type=f32)
        prob_dot = jnp.sum(soft_weights * prob_grad, axis=-1, keepdims=True)
        score_grad = (soft_weights * (prob_grad - prob_dot) * score_scale).astype(bf16)
        key_act = jnp.einsum("hts,the->she", score_grad, query_heads, preferred_element_type=f32)
        key_act = key_act.astype(bf16).reshape(total_src, local_width)

        stacked = jnp.stack(rows)
        enc_full = jnp.concatenate(
            [lax.dynamic_index_in_dim(stacked, (x - q) % XS, 0, False) for q in range(XS)], axis=1
        )

        def weight_grad(act):
            part = t_dot(enc_full, act).astype(bf16)
            return lax.psum_scatter(part, "dp", scatter_dimension=0, tiled=True)[None]

        value_weight_grad = weight_grad(value_act)
        key_weight_grad = weight_grad(key_act)

        act = jnp.concatenate([key_act, value_act], axis=1)
        chunks = 2
        cols = quarter // chunks
        top = total_src // 2
        finals = []
        for c in range(chunks):
            part = [dot_t(act, w_rel[m][c * cols : (c + 1) * cols]) for m in range(XS)]
            far = part[2].astype(bf16)
            got_a = shift_x(far[:top], -1, n_ten).astype(f32)
            got_b = shift_x(far[top:], 1, n_ten).astype(f32)
            near1 = jnp.concatenate([part[1][:top] + got_a, part[1][top:]], axis=0)
            near3 = jnp.concatenate([part[3][:top], part[3][top:] + got_b], axis=0)
            got1 = shift_x(near1.astype(bf16), -1, n_ten).astype(f32)
            got3 = shift_x(near3.astype(bf16), 1, n_ten).astype(f32)
            total = part[0] + got1 + got3
            low = total.astype(bf16)
            mine = total[:blk]
            for k in range(1, n_sec):
                mine = mine + shift_section(low[k * blk : (k + 1) * blk], -k, n_sec).astype(f32)
            mine = mine.astype(bf16)
            other = swap_lo(mine, n_ten)
            finals.append((mine.astype(f32) + other.astype(f32)).astype(bf16))
        final = jnp.concatenate(finals, axis=1)
        gathered = [final] + [shift_x(final, k, n_ten) for k in range(1, XS)]
        stacked_out = jnp.stack(gathered)
        enc_grad = jnp.concatenate(
            [lax.dynamic_index_in_dim(stacked_out, (x - q) % XS, 0, False) for q in range(XS)],
            axis=1,
        )[None]
        return (context, enc_grad, key_weight_grad, value_weight_grad)

    return shards


def solution(mesh):
    return jax.shard_map(
        make_shards(mesh),
        mesh=mesh,
        in_specs=(
            P("dp", "section", None),
            P("section", None, "tensor"),
            P("section", None, "tensor"),
            P("section", "dp", None, "tensor"),
            P("section", "dp", None, "tensor"),
            P("dp"),
            P("dp"),
        ),
        out_specs=(
            P("section", "dp", None, "tensor"),
            P("dp", "section", None),
            P("section", "dp", "tensor"),
            P("section", "dp", "tensor"),
        ),
        check_vma=False,
    )
```

```python
import jax
import jax.numpy as jnp
from jax import lax
from jax.experimental import pallas as pl
from jax.experimental.pallas import tpu as pltpu
from jax.sharding import PartitionSpec as P

HEAD = 256
XS = 4
masked_score = -1e30
f32 = jnp.float32
bf16 = jnp.bfloat16


def dot(a, b):
    return jnp.dot(a, b, preferred_element_type=f32)


def dot_t(a, b):
    return lax.dot_general(a, b, (((1,), (1,)), ((), ())), preferred_element_type=f32)


def t_dot(a, b):
    return lax.dot_general(a, b, (((0,), (0,)), ((), ())), preferred_element_type=f32)


def shift_section(v, k, n):
    return lax.ppermute(v, "section", [(i, (i + k) % n) for i in range(n)])


def shift_x(v, k, n):
    lo = n // XS
    return lax.ppermute(
        v,
        "tensor",
        [(x * lo + l, ((x + k) % XS) * lo + l) for x in range(XS) for l in range(lo)],
    )


def swap_lo(v, n):
    return lax.ppermute(v, "tensor", [(i, i ^ 1) for i in range(n)])


def shift_y(v, k, n):
    return lax.ppermute(
        v, "dp", [(y * 2 + c, ((y + k) % (n // 2)) * 2 + c) for y in range(n // 2) for c in range(2)]
    )


def swap_core(v, n):
    return lax.ppermute(v, "dp", [(i, i ^ 1) for i in range(n)])


def attention_kernel(blk, n_sec, info, k_ref, v_ref, q_ref, g_ref, ctx_ref, ka_ref, va_ref):
    scale = HEAD ** (-0.5)
    total, targets = k_ref.shape[0], q_ref.shape[0]
    sec, src_live, tgt_live = info[0], info[1], info[2]
    k, v, q = k_ref[...], v_ref[...], q_ref[...]
    row = lax.broadcasted_iota(jnp.int32, (total, 1), 0)
    block = row // blk
    place = lax.rem(sec - block + n_sec, n_sec) * blk + (row - block * blk)
    scores = dot_t(k, q) * scale
    scores = jnp.where(place < src_live, scores, masked_score)
    highest = jnp.max(scores, axis=0, keepdims=True)
    shifted = jnp.exp(scores - highest)
    weights = shifted * (1.0 / jnp.sum(shifted, axis=0, keepdims=True))
    low = weights.astype(bf16)
    ctx_ref[...] = t_dot(low, v).astype(bf16)
    target = lax.broadcasted_iota(jnp.int32, (targets, 1), 0)
    g = jnp.where(target < tgt_live, g_ref[...].astype(f32), 0.0).astype(bf16)
    va_ref[...] = dot(low, g).astype(bf16)
    prob = dot_t(v, g)
    prob_dot = jnp.sum(weights * prob, axis=0, keepdims=True)
    grad = (weights * (prob - prob_dot) * scale).astype(bf16)
    ka_ref[...] = dot(grad, q).astype(bf16)


def attention(kv, q, g, info, blk, n_sec):
    total, targets, width = kv.shape[0], q.shape[0], q.shape[1]
    heads = width // HEAD

    def rows(n, off):
        return pl.BlockSpec((n, HEAD), lambda h, info: (0, h + off))

    ctx, ka, va = pl.pallas_call(
        lambda *refs: attention_kernel(blk, n_sec, *refs),
        grid_spec=pltpu.PrefetchScalarGridSpec(
            num_scalar_prefetch=1,
            grid=(heads,),
            in_specs=[rows(total, 0), rows(total, heads), rows(targets, 0), rows(targets, 0)],
            out_specs=[rows(targets, 0), rows(total, 0), rows(total, 0)],
        ),
        out_shape=[
            jax.ShapeDtypeStruct((targets, width), bf16),
            jax.ShapeDtypeStruct((total, width), bf16),
            jax.ShapeDtypeStruct((total, width), bf16),
        ],
        compiler_params=pltpu.CompilerParams(vmem_limit_bytes=32 * 1024 * 1024),
        cost_estimate=pl.CostEstimate(
            flops=12 * total * targets * width, bytes_accessed=4 * 1024 * 1024, transcendentals=total * targets * heads
        ),
    )(info, kv, kv, q, g)
    return ctx, ka, va


def spread(far, near_up, near_down, keep, shift):
    half = far.shape[0] // 2
    low = far.astype(bf16)
    got_up = shift(low[:half], 1).astype(f32)
    got_down = shift(low[half:], -1).astype(f32)
    up = jnp.concatenate([near_up[:half] + got_up, near_up[half:]], axis=0)
    down = jnp.concatenate([near_down[:half], near_down[half:] + got_down], axis=0)
    from_below = shift(up.astype(bf16), 1).astype(f32)
    from_above = shift(down.astype(bf16), -1).astype(f32)
    return keep + from_below + from_above


def make_shards(mesh):
    n_sec = mesh.shape["section"]
    n_ten = mesh.shape["tensor"]

    def shards(enc_out, key_weight, value_weight, queries, ctx_grad, src_pad, tgt_pad):
        blk = enc_out.shape[1]
        width = enc_out.shape[2]
        quarter = width // XS
        key_proj = key_weight[0]
        value_proj = value_weight[0]
        local_width = key_proj.shape[1]
        heads_here = local_width // HEAD
        target_count = queries.shape[2]
        total_src = n_sec * blk
        score_scale = HEAD ** (-0.5)
        x = lax.axis_index("tensor") // (n_ten // XS)
        s = lax.axis_index("section")
        enc = enc_out[0]

        def col_quarter(m):
            return lax.dynamic_slice(enc, (0, ((x - m) % XS) * quarter), (blk, quarter))

        own = [col_quarter(m) for m in range(XS)]
        sec = [shift_section(own[0], k, n_sec) for k in range(1, n_sec)]
        g0 = jnp.concatenate(sec, axis=0)
        half = g0.shape[0] // 2
        g1 = shift_x(g0, 1, n_ten)
        g3 = shift_x(g0, -1, n_ten)
        g2a = shift_x(g1[:half], 1, n_ten)
        g2b = shift_x(g3[half:], -1, n_ten)
        g2 = jnp.concatenate([g2a, g2b], axis=0)
        rows = [jnp.concatenate([o, g], axis=0) for o, g in zip(own, (g0, g1, g2, g3))]

        w_rel = []
        for m in range(XS):
            at = ((x - m) % XS) * quarter
            w_rel.append(
                jnp.concatenate(
                    [
                        lax.dynamic_slice(key_proj, (at, 0), (quarter, local_width)),
                        lax.dynamic_slice(value_proj, (at, 0), (quarter, local_width)),
                    ],
                    axis=1,
                )
            )
        acc = dot(rows[0], w_rel[0])
        for m in (1, 3, 2):
            acc = acc + dot(rows[m], w_rel[m])
        kv = acc.astype(bf16)
        info = jnp.stack([s, total_src - src_pad[0], target_count - tgt_pad[0]]).astype(jnp.int32)
        context, key_act, value_act = attention(kv, queries[0, 0], ctx_grad[0, 0], info, blk, n_sec)
        context = context[None, None]
        act = jnp.concatenate([key_act, value_act], axis=1)

        def x_step(v, k):
            return shift_x(v, k, n_ten)

        cols = quarter // 2
        part_low = 2
        sub = cols // part_low
        lo = lax.axis_index("tensor") % part_low
        own_b = [lax.dynamic_slice(w, (cols + lo * sub, 0), (sub, 2 * local_width)) for w in w_rel]
        other_b = [lax.dynamic_slice(w, (cols + (1 - lo) * sub, 0), (sub, 2 * local_width)) for w in w_rel]
        sent_b = dot_t(act, jnp.concatenate(other_b, axis=0)).astype(bf16)
        got_b = swap_lo(sent_b, n_ten)
        part_a = [dot_t(act, w[:cols]) for w in w_rel]
        total_a = spread(part_a[2], part_a[3], part_a[1], part_a[0], x_step)
        sum_b = dot_t(act, jnp.concatenate(own_b, axis=0)) + got_b.astype(f32)
        part_b = [sum_b[:, m * sub : (m + 1) * sub] for m in range(XS)]
        total_b = spread(part_b[2], part_b[3], part_b[1], part_b[0], x_step)

        def over_sections(total):
            low = total.astype(bf16)
            mine = total[:blk]
            for k in range(1, n_sec):
                mine = mine + shift_section(low[k * blk : (k + 1) * blk], -k, n_sec).astype(f32)
            return mine.astype(bf16)

        mine_a = over_sections(total_a)
        mine_b = over_sections(total_b)
        other = swap_lo(jnp.concatenate([mine_a, mine_b], axis=1), n_ten)
        final_a = (mine_a.astype(f32) + other[:, :cols].astype(f32)).astype(bf16)
        low_b = jnp.where(lo == 0, mine_b, other[:, cols:])
        high_b = jnp.where(lo == 0, other[:, cols:], mine_b)
        final = jnp.concatenate([final_a, low_b, high_b], axis=1)
        gathered = [final] + [shift_x(final, k, n_ten) for k in range(1, XS)]
        stacked_out = jnp.stack(gathered)
        enc_grad = jnp.concatenate(
            [lax.dynamic_index_in_dim(stacked_out, (x - q) % XS, 0, False) for q in range(XS)],
            axis=1,
        )[None]

        n_dp = mesh.shape["dp"]
        y = lax.axis_index("dp") // 2
        core = lax.axis_index("dp") % 2
        half_cols = quarter // 2
        stacked = jnp.stack(rows)

        def enc_half(i, c):
            at = (x - y - i) % XS
            return lax.dynamic_slice(stacked, (at, 0, c * half_cols), (1, total_src, half_cols))[0]

        sent = jnp.concatenate([enc_half(i, 1 - core) for i in range(4)], axis=1)
        kept = jnp.concatenate([enc_half(i, core) for i in range(4)], axis=1)
        enc_pair = jnp.concatenate([kept, swap_core(sent, n_dp)], axis=0)
        act_pair = jnp.concatenate([act, swap_core(act, n_dp)], axis=0)
        pieces = [
            t_dot(enc_pair[:, i * half_cols : (i + 1) * half_cols], act_pair) for i in (0, 1, 2, 3)
        ]
        weight_grads = spread(
            pieces[2], pieces[1], pieces[3], pieces[0], lambda v, k: shift_y(v, k, n_dp)
        ).astype(bf16)
        key_weight_grad = weight_grads[None, :, :local_width]
        value_weight_grad = weight_grads[None, :, local_width:]
        return (context, enc_grad, key_weight_grad, value_weight_grad)

    return shards


def solution(mesh):
    return jax.shard_map(
        make_shards(mesh),
        mesh=mesh,
        in_specs=(
            P("dp", "section", None),
            P("section", None, "tensor"),
            P("section", None, "tensor"),
            P("section", "dp", None, "tensor"),
            P("section", "dp", None, "tensor"),
            P("dp"),
            P("dp"),
        ),
        out_specs=(
            P("section", "dp", None, "tensor"),
            P("dp", "section", None),
            P("section", "dp", "tensor"),
            P("section", "dp", "tensor"),
        ),
        check_vma=False,
    )
```

```python
import jax
import jax.numpy as jnp
from jax import lax
from jax.experimental import pallas as pl
from jax.experimental.pallas import tpu as pltpu
from jax.sharding import PartitionSpec as P

HEAD = 256
XS = 4
UNIT = 256
masked_score = -1e30
f32 = jnp.float32
bf16 = jnp.bfloat16
X, SEC, LO, Y, CORE, SRC_LIVE, TGT_LIVE = range(7)


def dot(a, b):
    return jnp.dot(a, b, preferred_element_type=f32)


def dot_t(a, b):
    return lax.dot_general(a, b, (((1,), (1,)), ((), ())), preferred_element_type=f32)


def t_dot(a, b):
    return lax.dot_general(a, b, (((0,), (0,)), ((), ())), preferred_element_type=f32)


def mod4(v):
    return lax.rem(v + 8, 4)


def params(mib):
    return pltpu.CompilerParams(vmem_limit_bytes=mib * 1024 * 1024)


def whole(a):
    return pl.BlockSpec(a.shape, lambda i, info: (0,) * a.ndim)


ANYWHERE = pl.BlockSpec(memory_space=pl.ANY)


def join_rows(parts, info):
    rows = sum(p.shape[0] for p in parts)
    out = jax.ShapeDtypeStruct((rows, parts[0].shape[1]), bf16)

    def body(info, *refs):
        at = 0
        for ref in refs[:-1]:
            refs[-1][at : at + ref.shape[0], :] = ref[...]
            at += ref.shape[0]

    return pl.pallas_call(
        body,
        grid_spec=pltpu.PrefetchScalarGridSpec(
            num_scalar_prefetch=1, grid=(1,), in_specs=[whole(p) for p in parts], out_specs=whole(out)
        ),
        out_shape=out,
        compiler_params=params(8),
    )(info, *parts)


def project(m, enc, parts, wk, wv, acc, info, last, n_sec):
    blk, width = enc.shape
    quarter = width // XS
    total = n_sec * blk
    cols = wk.shape[1]
    heads = cols // HEAD
    half = quarter // 2
    step = 64

    def body(info, enc_ref, *refs):
        n = len(parts)
        part_refs, wk_ref, wv_ref = refs[:n], refs[n], refs[n + 1]
        acc_ref = refs[n + 2] if acc is not None else None
        out_ref, rows_ref, half_ref = refs[-3:]

        @pl.when(pl.program_id(0) == 0)
        def _():
            sec = info[SEC]
            rows_ref[pl.ds(pl.multiple_of(sec * blk, blk), blk), :] = enc_ref[...]
            at = 0
            for ref in part_refs:
                for u in range(ref.shape[0] // step):
                    k, off = 1 + at // blk, at % blk
                    to = lax.rem(sec - k + n_sec, n_sec) * blk + off
                    rows_ref[pl.ds(pl.multiple_of(to, step), step), :] = ref[u * step : (u + 1) * step, :]
                    at += step
            other = pl.multiple_of((1 - info[CORE]) * half, half)
            half_ref[...] = rows_ref[:, pl.ds(other, half)]

        rows = rows_ref[...]
        k_part = dot(rows, wk_ref[...])
        v_part = dot(rows, wv_ref[...])
        if acc_ref is not None:
            k_part = k_part + acc_ref[:, :HEAD]
            v_part = v_part + acc_ref[:, HEAD:]
        out_ref[:, :HEAD] = k_part.astype(out_ref.dtype)
        out_ref[:, HEAD:] = v_part.astype(out_ref.dtype)

    def at_quarter(info):
        return mod4(info[X] - m)

    weight = pl.BlockSpec((quarter, HEAD), lambda h, info: (at_quarter(info), h))
    pair = pl.BlockSpec((total, 2 * HEAD), lambda h, info: (0, h))
    out_shape = [
        jax.ShapeDtypeStruct((total, 2 * cols), bf16 if last else f32),
        jax.ShapeDtypeStruct((total, quarter), bf16),
        jax.ShapeDtypeStruct((total, half), bf16),
    ]
    return pl.pallas_call(
        body,
        grid_spec=pltpu.PrefetchScalarGridSpec(
            num_scalar_prefetch=1,
            grid=(heads,),
            in_specs=[pl.BlockSpec((blk, quarter), lambda h, info: (0, at_quarter(info)))]
            + [whole(p) for p in parts]
            + [weight, weight]
            + ([pair] if acc is not None else []),
            out_specs=[pair, whole(out_shape[1]), whole(out_shape[2])],
        ),
        out_shape=out_shape,
        compiler_params=params(24),
        cost_estimate=pl.CostEstimate(
            flops=4 * total * quarter * cols, bytes_accessed=6 * 1024 * 1024, transcendentals=0
        ),
    )(info, enc, *parts, wk, wv, *([acc] if acc is not None else []))


def attention(kv, q, g, info):
    total, targets, width = kv.shape[0], q.shape[0], q.shape[1]
    heads = width // HEAD
    scale = HEAD ** (-0.5)

    def body(info, kv_ref, q_ref, g_ref, ctx_ref, act_ref):
        k, v, q = kv_ref[:, :HEAD], kv_ref[:, HEAD:], q_ref[...]
        place = lax.broadcasted_iota(jnp.int32, (total, 1), 0)
        scores = dot_t(k, q) * scale
        scores = jnp.where(place < info[SRC_LIVE], scores, masked_score)
        highest = jnp.max(scores, axis=0, keepdims=True)
        shifted = jnp.exp(scores - highest)
        weights = shifted * (1.0 / jnp.sum(shifted, axis=0, keepdims=True))
        low = weights.astype(bf16)
        target = lax.broadcasted_iota(jnp.int32, (targets, 1), 0)
        g = jnp.where(target < info[TGT_LIVE], g_ref[...].astype(f32), 0.0).astype(bf16)
        prob = dot_t(v, g)
        prob_dot = jnp.sum(weights * prob, axis=0, keepdims=True)
        grad = (weights * (prob - prob_dot) * scale).astype(bf16)
        act_ref[:, :HEAD] = dot(grad, q).astype(bf16)
        act_ref[:, HEAD:] = dot(low, g).astype(bf16)
        ctx_ref[...] = t_dot(low, v).astype(bf16)

    def cols(n, w):
        return pl.BlockSpec((n, w), lambda h, info: (0, h))

    return pl.pallas_call(
        body,
        grid_spec=pltpu.PrefetchScalarGridSpec(
            num_scalar_prefetch=1,
            grid=(heads,),
            in_specs=[cols(total, 2 * HEAD), cols(targets, HEAD), cols(targets, HEAD)],
            out_specs=[cols(targets, HEAD), cols(total, 2 * HEAD)],
        ),
        out_shape=[
            jax.ShapeDtypeStruct((targets, width), bf16),
            jax.ShapeDtypeStruct((total, 2 * width), bf16),
        ],
        compiler_params=params(20),
        cost_estimate=pl.CostEstimate(
            flops=12 * total * targets * width, bytes_accessed=4 * 1024 * 1024, transcendentals=total * targets * heads
        ),
    )(info, kv, q, g)


def partial_grad(act, wk, wv, info, units, dtype, after=(), add=None):
    total, cols = act.shape[0], wk.shape[1]
    heads = cols // HEAD
    n = len(units)

    def unit(i, info):
        at = units[0](info)
        for j in range(1, n):
            at = jnp.where(i == j, units[j](info), at)
        return at

    def body(info, act_ref, wk_ref, wv_ref, *refs):
        out_ref = refs[-1]
        sums = None
        for h in range(heads):
            for j, w_ref in enumerate((wk_ref, wv_ref)):
                at = (2 * h + j) * HEAD
                term = dot_t(act_ref[:, at : at + HEAD], w_ref[:, h * HEAD : (h + 1) * HEAD])
                sums = term if sums is None else sums + term
        if add is not None:
            sums = sums + refs[0][...].astype(f32)
        out_ref[...] = sums.astype(dtype)

    weight = pl.BlockSpec((UNIT, cols), lambda i, info: (unit(i, info), 0))
    block = pl.BlockSpec((total, UNIT), lambda i, info: (0, i))
    return pl.pallas_call(
        body,
        grid_spec=pltpu.PrefetchScalarGridSpec(
            num_scalar_prefetch=1,
            grid=(n,),
            in_specs=[whole(act), weight, weight]
            + ([block] if add is not None else [])
            + [ANYWHERE] * len(after),
            out_specs=block,
        ),
        out_shape=jax.ShapeDtypeStruct((total, n * UNIT), dtype),
        compiler_params=params(12),
        cost_estimate=pl.CostEstimate(
            flops=4 * total * n * UNIT * cols, bytes_accessed=2 * 1024 * 1024, transcendentals=0
        ),
    )(info, act, wk, wv, *([add] if add is not None else []), *after)


def pair_grads(rows, halves, act, act_other, info, after):
    total, quarter = rows[0].shape
    half = quarter // 2
    n = len(rows)

    def body(info, *refs):
        row_refs, half_refs, act_ref, other_ref, out_ref = refs[:n], refs[n : 2 * n], refs[2 * n], refs[2 * n + 1], refs[-1]
        for m in range(n):
            piece = t_dot(row_refs[m][...], act_ref[...]) + t_dot(half_refs[m][...], other_ref[...])
            out_ref[mod4(info[X] - info[Y] - m)] = piece.astype(bf16)

    out = jax.ShapeDtypeStruct((n, half, act.shape[1]), bf16)
    return pl.pallas_call(
        body,
        grid_spec=pltpu.PrefetchScalarGridSpec(
            num_scalar_prefetch=1,
            grid=(1,),
            in_specs=[pl.BlockSpec((total, half), lambda i, info: (0, info[CORE]))] * n
            + [whole(h) for h in halves]
            + [whole(act), whole(act_other)]
            + [ANYWHERE] * len(after),
            out_specs=whole(out),
        ),
        out_shape=out,
        compiler_params=params(28),
        cost_estimate=pl.CostEstimate(
            flops=4 * n * total * half * act.shape[1], bytes_accessed=8 * 1024 * 1024, transcendentals=0
        ),
    )(info, *rows, *halves, act, act_other, *after)


def spread(far, near_up, near_down, keep, shift):
    half = far.shape[0] // 2
    got_up = shift(far[:half], 1).astype(f32)
    got_down = shift(far[half:], -1).astype(f32)
    up = jnp.concatenate([near_up[:half].astype(f32) + got_up, near_up[half:].astype(f32)], axis=0)
    down = jnp.concatenate([near_down[:half].astype(f32), near_down[half:].astype(f32) + got_down], axis=0)
    from_below = shift(up.astype(bf16), 1).astype(f32)
    from_above = shift(down.astype(bf16), -1).astype(f32)
    return keep.astype(f32) + from_below + from_above


def make_shards(mesh):
    n_sec, n_dp, n_ten = mesh.shape["section"], mesh.shape["dp"], mesh.shape["tensor"]
    lows, cores = n_ten // XS, 2

    def shift_section(v, k):
        return lax.ppermute(v, "section", [(i, (i + k) % n_sec) for i in range(n_sec)])

    def shift_x(v, k):
        pairs = [(x * lows + l, ((x + k) % XS) * lows + l) for x in range(XS) for l in range(lows)]
        return lax.ppermute(v, "tensor", pairs)

    def swap_lo(v):
        return lax.ppermute(v, "tensor", [(i, i ^ 1) for i in range(n_ten)])

    def shift_y(v, k):
        ys = n_dp // cores
        pairs = [(y * cores + c, ((y + k) % ys) * cores + c) for y in range(ys) for c in range(cores)]
        return lax.ppermute(v, "dp", pairs)

    def swap_core(v):
        return lax.ppermute(v, "dp", [(i, i ^ 1) for i in range(n_dp)])

    def shards(enc_out, key_weight, value_weight, queries, ctx_grad, src_pad, tgt_pad):
        enc, wk, wv = enc_out[0], key_weight[0], value_weight[0]
        blk, width = enc.shape
        quarter = width // XS
        local_width = wk.shape[1]
        total_src = n_sec * blk
        ten, dp = lax.axis_index("tensor"), lax.axis_index("dp")
        x, lo = ten // lows, ten % lows
        sec = lax.axis_index("section")
        info = jnp.stack(
            [
                x,
                sec,
                lo,
                dp // cores,
                dp % cores,
                total_src - src_pad[0],
                queries.shape[2] - tgt_pad[0],
            ]
        ).astype(jnp.int32)

        mine = lax.dynamic_slice(enc, (0, x * quarter), (blk, quarter))
        g0 = join_rows([shift_section(mine, k) for k in range(1, n_sec)], info)
        mid = g0.shape[0] // 2
        g1 = shift_x(g0, 1)
        g3 = shift_x(g0, -1)
        g2a = shift_x(g1[:mid], 1)
        g2b = shift_x(g3[mid:], -1)
        parts = ([g0], [g1], [g2a, g2b], [g3])
        rows, halves = [None] * XS, [None] * XS
        acc = None
        for m in (0, 1, 3, 2):
            acc, rows[m], halves[m] = project(m, enc, parts[m], wk, wv, acc, info, m == 2, n_sec)
        halves = [swap_core(h) for h in halves]

        context, act = attention(acc, queries[0, 0], ctx_grad[0, 0], info)
        context = context[None, None]
        act_other = swap_core(act)

        per = quarter // UNIT
        a_units = per // 2

        def unit(m, j, side=None):
            def at(info):
                u = mod4(info[X] - m) * per + j
                if side is None:
                    return u
                return u + (info[LO] if side else 1 - info[LO])

            return at

        far_a = partial_grad(act, wk, wv, info, [unit(2, j) for j in range(a_units)], bf16)
        sent_b = partial_grad(
            act, wk, wv, info, [unit(m, a_units, False) for m in (2, 3, 1, 0)], bf16, (far_a,)
        )
        got_b = swap_lo(sent_b)
        near_a = partial_grad(
            act, wk, wv, info, [unit(m, j) for m in (3, 1, 0) for j in range(a_units)], f32, (sent_b,)
        )
        pieces = pair_grads(rows, halves, act, act_other, info, (near_a,))
        sum_b = partial_grad(
            act, wk, wv, info, [unit(m, a_units, True) for m in (2, 3, 1, 0)], f32, (pieces,), got_b
        )
        cols = a_units * UNIT
        total_a = spread(far_a, near_a[:, :cols], near_a[:, cols : 2 * cols], near_a[:, 2 * cols :], shift_x)
        part_b = [sum_b[:, j * UNIT : (j + 1) * UNIT] for j in range(XS)]
        total_b = spread(part_b[0].astype(bf16), part_b[1], part_b[2], part_b[3], shift_x)

        def over_sections(total):
            low = total.astype(bf16).reshape(n_sec, blk, total.shape[1])
            terms = lax.all_to_all(low, "section", 0, 0, tiled=True)
            return jnp.sum(terms.astype(f32), axis=0).astype(bf16)

        mine_a = over_sections(total_a)
        mine_b = over_sections(total_b)
        other = swap_lo(jnp.concatenate([mine_a, mine_b], axis=1))
        final_a = (mine_a.astype(f32) + other[:, :cols].astype(f32)).astype(bf16)
        low_b = jnp.where(lo == 0, mine_b, other[:, cols:])
        high_b = jnp.where(lo == 0, other[:, cols:], mine_b)
        final = jnp.concatenate([final_a, low_b, high_b], axis=1)
        gathered = jnp.stack([final] + [shift_x(final, k) for k in range(1, XS)])
        enc_grad = jnp.concatenate(
            [lax.dynamic_index_in_dim(gathered, (x - q) % XS, 0, False) for q in range(XS)], axis=1
        )[None]

        weight_grads = spread(pieces[2], pieces[1], pieces[3], pieces[0], shift_y)
        weight_grads = weight_grads.astype(bf16).reshape(quarter // cores, local_width // HEAD, 2, HEAD)
        key_weight_grad = weight_grads[:, :, 0].reshape(1, quarter // cores, local_width)
        value_weight_grad = weight_grads[:, :, 1].reshape(1, quarter // cores, local_width)
        return (context, enc_grad, key_weight_grad, value_weight_grad)

    return shards


def solution(mesh):
    return jax.shard_map(
        make_shards(mesh),
        mesh=mesh,
        in_specs=(
            P("dp", "section", None),
            P("section", None, "tensor"),
            P("section", None, "tensor"),
            P("section", "dp", None, "tensor"),
            P("section", "dp", None, "tensor"),
            P("dp"),
            P("dp"),
        ),
        out_specs=(
            P("section", "dp", None, "tensor"),
            P("dp", "section", None),
            P("section", "dp", "tensor"),
            P("section", "dp", "tensor"),
        ),
        check_vma=False,
    )
```

```python
import jax
import jax.numpy as jnp
from jax import lax
from jax.experimental import pallas as pl
from jax.experimental.pallas import tpu as pltpu
from jax.sharding import Mesh
from jax.sharding import PartitionSpec as P

HEAD = 256
XS = 4
UNIT = 256
masked_score = -1e30
f32 = jnp.float32
bf16 = jnp.bfloat16
X, SEC, LO, Y, CORE, SRC_LIVE, TGT_LIVE = range(7)


def dot(a, b):
    return jnp.dot(a, b, preferred_element_type=f32)


def dot_t(a, b):
    return lax.dot_general(a, b, (((1,), (1,)), ((), ())), preferred_element_type=f32)


def t_dot(a, b):
    return lax.dot_general(a, b, (((0,), (0,)), ((), ())), preferred_element_type=f32)


def mod4(v):
    return lax.rem(v + 8, 4)


def params(mib):
    return pltpu.CompilerParams(vmem_limit_bytes=mib * 1024 * 1024)


def whole(a):
    return pl.BlockSpec(a.shape, lambda i, info: (0,) * a.ndim)


ANYWHERE = pl.BlockSpec(memory_space=pl.ANY)


def join_rows(parts, info):
    rows = sum(p.shape[0] for p in parts)
    out = jax.ShapeDtypeStruct((rows, parts[0].shape[1]), bf16)

    def body(info, *refs):
        at = 0
        for ref in refs[:-1]:
            refs[-1][at : at + ref.shape[0], :] = ref[...]
            at += ref.shape[0]

    return pl.pallas_call(
        body,
        grid_spec=pltpu.PrefetchScalarGridSpec(
            num_scalar_prefetch=1, grid=(1,), in_specs=[whole(p) for p in parts], out_specs=whole(out)
        ),
        out_shape=out,
        compiler_params=params(8),
    )(info, *parts)


def project(m, enc, parts, wk, wv, acc, info, last, n_sec, after=()):
    blk, width = enc.shape
    quarter = width // XS
    total = n_sec * blk
    cols = wk.shape[1]
    heads = cols // HEAD
    half = quarter // 2
    step = 64

    def body(info, enc_ref, *refs):
        n = len(parts)
        part_refs, wk_ref, wv_ref = refs[:n], refs[n], refs[n + 1]
        acc_ref = refs[n + 2] if acc is not None else None
        out_ref, rows_ref, half_ref = refs[-3:]

        @pl.when(pl.program_id(0) == 0)
        def _():
            sec = info[SEC]
            rows_ref[pl.ds(pl.multiple_of(sec * blk, blk), blk), :] = enc_ref[...]
            at = 0
            for ref in part_refs:
                for u in range(ref.shape[0] // step):
                    k, off = 1 + at // blk, at % blk
                    to = lax.rem(sec - k + n_sec, n_sec) * blk + off
                    rows_ref[pl.ds(pl.multiple_of(to, step), step), :] = ref[u * step : (u + 1) * step, :]
                    at += step
            other = pl.multiple_of((1 - info[CORE]) * half, half)
            half_ref[...] = rows_ref[:, pl.ds(other, half)]

        rows = rows_ref[...]
        k_part = dot(rows, wk_ref[...])
        v_part = dot(rows, wv_ref[...])
        if acc_ref is not None:
            k_part = k_part + acc_ref[:, :HEAD]
            v_part = v_part + acc_ref[:, HEAD:]
        out_ref[:, :HEAD] = k_part.astype(out_ref.dtype)
        out_ref[:, HEAD:] = v_part.astype(out_ref.dtype)

    def at_quarter(info):
        return mod4(info[X] - m)

    weight = pl.BlockSpec((quarter, HEAD), lambda h, info: (at_quarter(info), h))
    pair = pl.BlockSpec((total, 2 * HEAD), lambda h, info: (0, h))
    out_shape = [
        jax.ShapeDtypeStruct((total, 2 * cols), bf16 if last else f32),
        jax.ShapeDtypeStruct((total, quarter), bf16),
        jax.ShapeDtypeStruct((total, half), bf16),
    ]
    return pl.pallas_call(
        body,
        grid_spec=pltpu.PrefetchScalarGridSpec(
            num_scalar_prefetch=1,
            grid=(heads,),
            in_specs=[pl.BlockSpec((blk, quarter), lambda h, info: (0, at_quarter(info)))]
            + [whole(p) for p in parts]
            + [weight, weight]
            + ([pair] if acc is not None else [])
            + [ANYWHERE] * len(after),
            out_specs=[pair, whole(out_shape[1]), whole(out_shape[2])],
        ),
        out_shape=out_shape,
        compiler_params=params(24),
        cost_estimate=pl.CostEstimate(
            flops=4 * total * quarter * cols, bytes_accessed=6 * 1024 * 1024, transcendentals=0
        ),
    )(info, enc, *parts, wk, wv, *([acc] if acc is not None else []), *after)


def attention(kv, q, g, info):
    total, targets, width = kv.shape[0], q.shape[0], q.shape[1]
    heads = width // HEAD
    scale = HEAD ** (-0.5)

    def body(info, kv_ref, q_ref, g_ref, ctx_ref, act_ref):
        k, v, q = kv_ref[:, :HEAD], kv_ref[:, HEAD:], q_ref[...]
        place = lax.broadcasted_iota(jnp.int32, (total, 1), 0)
        scores = dot_t(k, q) * scale
        scores = jnp.where(place < info[SRC_LIVE], scores, masked_score)
        highest = jnp.max(scores, axis=0, keepdims=True)
        shifted = jnp.exp(scores - highest)
        weights = shifted * (1.0 / jnp.sum(shifted, axis=0, keepdims=True))
        low = weights.astype(bf16)
        target = lax.broadcasted_iota(jnp.int32, (targets, 1), 0)
        g = jnp.where(target < info[TGT_LIVE], g_ref[...].astype(f32), 0.0).astype(bf16)
        prob = dot_t(v, g)
        prob_dot = jnp.sum(weights * prob, axis=0, keepdims=True)
        grad = (weights * (prob - prob_dot) * scale).astype(bf16)
        act_ref[:, :HEAD] = dot(grad, q).astype(bf16)
        act_ref[:, HEAD:] = dot(low, g).astype(bf16)
        ctx_ref[...] = t_dot(low, v).astype(bf16)

    def cols(n, w):
        return pl.BlockSpec((n, w), lambda h, info: (0, h))

    return pl.pallas_call(
        body,
        grid_spec=pltpu.PrefetchScalarGridSpec(
            num_scalar_prefetch=1,
            grid=(heads,),
            in_specs=[cols(total, 2 * HEAD), cols(targets, HEAD), cols(targets, HEAD)],
            out_specs=[cols(targets, HEAD), cols(total, 2 * HEAD)],
        ),
        out_shape=[
            jax.ShapeDtypeStruct((targets, width), bf16),
            jax.ShapeDtypeStruct((total, 2 * width), bf16),
        ],
        compiler_params=params(20),
        cost_estimate=pl.CostEstimate(
            flops=12 * total * targets * width, bytes_accessed=4 * 1024 * 1024, transcendentals=total * targets * heads
        ),
    )(info, kv, q, g)


def partial_grad(act, wk, wv, info, units, after=(), split=False, adds=None, n_sec=1):
    total, cols = act.shape[0], wk.shape[1]
    heads = cols // HEAD
    n = len(units)
    blk = total // n_sec

    def unit(i, info):
        at = units[0](info)
        for j in range(1, n):
            at = jnp.where(i == j, units[j](info), at)
        return at

    def body(info, act_ref, wk_ref, wv_ref, *refs):
        sums = None
        for h in range(heads):
            for j, w_ref in enumerate((wk_ref, wv_ref)):
                at = (2 * h + j) * HEAD
                term = dot_t(act_ref[:, at : at + HEAD], w_ref[:, h * HEAD : (h + 1) * HEAD])
                sums = term if sums is None else sums + term
        if adds is not None:
            sums = sums + refs[0][...].astype(f32) + refs[1][...].astype(f32)
            for k in range(n_sec):
                refs[-1][k, 0] = sums[k * blk : (k + 1) * blk].astype(bf16)
        elif split:
            refs[-2][...] = sums[: total // 2].astype(bf16)
            refs[-1][...] = sums[total // 2 :].astype(bf16)
        else:
            refs[-1][...] = sums

    weight = pl.BlockSpec((UNIT, cols), lambda i, info: (unit(i, info), 0))
    block = pl.BlockSpec((total, UNIT), lambda i, info: (0, i))
    if adds is not None:
        out_specs = pl.BlockSpec((n_sec, 1, blk, UNIT), lambda i, info: (0, i, 0, 0))
        out_shape = jax.ShapeDtypeStruct((n_sec, n, blk, UNIT), bf16)
    elif split:
        out_specs = [pl.BlockSpec((total // 2, UNIT), lambda i, info: (0, i))] * 2
        out_shape = [jax.ShapeDtypeStruct((total // 2, n * UNIT), bf16)] * 2
    else:
        out_specs, out_shape = block, jax.ShapeDtypeStruct((total, n * UNIT), f32)
    more = [] if adds is None else list(adds)
    return pl.pallas_call(
        body,
        grid_spec=pltpu.PrefetchScalarGridSpec(
            num_scalar_prefetch=1,
            grid=(n,),
            in_specs=[whole(act), weight, weight] + [block] * len(more) + [ANYWHERE] * len(after),
            out_specs=out_specs,
        ),
        out_shape=out_shape,
        compiler_params=params(12),
        cost_estimate=pl.CostEstimate(
            flops=4 * total * n * UNIT * cols, bytes_accessed=2 * 1024 * 1024, transcendentals=0
        ),
    )(info, act, wk, wv, *more, *after)


def pair_grads(rows, halves, act, act_other, info, after):
    total, quarter = rows[0].shape
    half = quarter // 2
    n = len(rows)

    def body(info, *refs):
        row_refs, half_refs, act_ref, other_ref = refs[:n], refs[n : 2 * n], refs[2 * n], refs[2 * n + 1]
        out_ref, top_ref, low_ref = refs[-3:]
        for m in range(n):
            piece = t_dot(row_refs[m][...], act_ref[...]) + t_dot(half_refs[m][...], other_ref[...])
            piece = piece.astype(bf16)
            slot = mod4(info[X] - info[Y] - m)
            out_ref[slot] = piece

            @pl.when(slot == 2)
            def _():
                top_ref[...] = piece[: half // 2]
                low_ref[...] = piece[half // 2 :]

    out = [
        jax.ShapeDtypeStruct((n, half, act.shape[1]), bf16),
        jax.ShapeDtypeStruct((half // 2, act.shape[1]), bf16),
        jax.ShapeDtypeStruct((half // 2, act.shape[1]), bf16),
    ]
    return pl.pallas_call(
        body,
        grid_spec=pltpu.PrefetchScalarGridSpec(
            num_scalar_prefetch=1,
            grid=(1,),
            in_specs=[pl.BlockSpec((total, half), lambda i, info: (0, info[CORE]))] * n
            + [whole(h) for h in halves]
            + [whole(act), whole(act_other)]
            + [ANYWHERE] * len(after),
            out_specs=[whole(o) for o in out],
        ),
        out_shape=out,
        compiler_params=params(28),
        cost_estimate=pl.CostEstimate(
            flops=4 * n * total * half * act.shape[1], bytes_accessed=8 * 1024 * 1024, transcendentals=0
        ),
    )(info, *rows, *halves, act, act_other, *after)


def small(body, ins, outs, info, after=()):
    ins = [i if isinstance(i, tuple) else (i, whole(i)) for i in ins]
    n = len(ins)

    def run(info, *refs):
        body(info, *refs[:n], *refs[n + len(after) :])

    return pl.pallas_call(
        run,
        grid_spec=pltpu.PrefetchScalarGridSpec(
            num_scalar_prefetch=1,
            grid=(1,),
            in_specs=[s for _, s in ins] + [ANYWHERE] * len(after),
            out_specs=[whole(o) for o in outs],
        ),
        out_shape=outs,
        compiler_params=params(24),
        cost_estimate=pl.CostEstimate(flops=1024 * 1024, bytes_accessed=1024 * 1024, transcendentals=0),
    )(info, *[a for a, _ in ins], *after)


def add_near(up, down, got_up, got_down, rows, cols, info, after=()):
    half = rows // 2

    def body(info, up_ref, down_ref, got_up_ref, got_down_ref, up_out, down_out):
        up_out[:half] = (up_ref[:half].astype(f32) + got_up_ref[...].astype(f32)).astype(bf16)
        up_out[half:] = up_ref[half:].astype(bf16)
        down_out[:half] = down_ref[:half].astype(bf16)
        down_out[half:] = (down_ref[half:].astype(f32) + got_down_ref[...].astype(f32)).astype(bf16)

    out = jax.ShapeDtypeStruct((rows, cols), bf16)
    return small(body, [up, down, got_up, got_down], [out, out], info, after)


def make_shards(n_sec, n_dp, lows):
    cores = 2

    def shift_section(v, k):
        return lax.ppermute(v, "section", [(i, (i + k) % n_sec) for i in range(n_sec)])

    def shift_x(v, k):
        return lax.ppermute(v, "x", [(i, (i + k) % XS) for i in range(XS)])

    def shift_y(v, k):
        ys = n_dp // cores
        pairs = [(y * cores + c, ((y + k) % ys) * cores + c) for y in range(ys) for c in range(cores)]
        return lax.ppermute(v, "dp", pairs)

    def swap_core(v):
        return lax.ppermute(v, "dp", [(i, i ^ 1) for i in range(n_dp)])

    def shards(enc_out, key_weight, value_weight, queries, ctx_grad, src_pad, tgt_pad):
        enc, wk, wv = enc_out[0], key_weight[0], value_weight[0]
        blk, width = enc.shape
        quarter = width // XS
        local_width = wk.shape[1]
        total_src = n_sec * blk
        dp = lax.axis_index("dp")
        x, lo, sec = lax.axis_index("x"), lax.axis_index("low"), lax.axis_index("section")
        info = jnp.stack(
            [
                x,
                sec,
                lo,
                dp // cores,
                dp % cores,
                total_src - src_pad[0],
                queries.shape[2] - tgt_pad[0],
            ]
        ).astype(jnp.int32)

        mine = lax.dynamic_slice(enc, (0, x * quarter), (blk, quarter))
        g0 = join_rows([shift_section(mine, k) for k in range(1, n_sec)], info)
        mid = g0.shape[0] // 2
        g1 = shift_x(g0, 1)
        g3 = shift_x(g0, -1)
        rows, halves = [None] * XS, [None] * XS
        acc, rows[0], halves[0] = project(0, enc, [g0], wk, wv, None, info, False, n_sec)
        part = jax.ShapeDtypeStruct((mid, quarter), bf16)

        def cut(info, g1_ref, g3_ref, top_ref, low_ref):
            top_ref[...] = g1_ref[:mid]
            low_ref[...] = g3_ref[mid:]

        top, low = small(cut, [g1, g3], [part, part], info, (acc,))
        g2a = shift_x(top, 1)
        g2b = shift_x(low, -1)
        for m, parts in ((1, [g1]), (3, [g3]), (2, [g2a, g2b])):
            acc, rows[m], halves[m] = project(m, enc, parts, wk, wv, acc, info, m == 2, n_sec, (top,))
        halves = [swap_core(h) for h in halves]

        context, act = attention(acc, queries[0, 0], ctx_grad[0, 0], info)
        context = context[None, None]
        act_other = swap_core(act)

        per = quarter // UNIT
        span = per // 2
        cols = span * UNIT

        def units(quarters, part):
            return [
                lambda info, m=m, j=j: mod4(info[X] - m) * per + part * span + j
                for m in quarters
                for j in range(span)
            ]

        def grad(quarters, part, after=(), **more):
            return partial_grad(act, wk, wv, info, units(quarters, part), after, n_sec=n_sec, **more)

        def steer(near, got, after=()):
            up = pl.BlockSpec((total_src, cols), lambda i, info: (0, 0))
            down = pl.BlockSpec((total_src, cols), lambda i, info: (0, 1))
            return add_near((near, up), (near, down), *got, total_src, cols, info, after)

        far_a = grad((2,), 0, split=True)
        got_a = shift_x(far_a[0], 1), shift_x(far_a[1], -1)
        far_b = grad((2,), 1, far_a, split=True)
        got_b = shift_x(far_b[0], 1), shift_x(far_b[1], -1)
        near_a = grad((3, 1), 0, far_b)
        out_a = steer(near_a, got_a)
        in_a = shift_x(out_a[0], 1), shift_x(out_a[1], -1)

        pieces, far_top, far_low = pair_grads(rows, halves, act, act_other, info, out_a)
        got_y = shift_y(far_top, 1), shift_y(far_low, -1)

        near_b = grad((3, 1), 1, (far_top,))
        out_b = steer(near_b, got_b)
        in_b = shift_x(out_b[0], 1), shift_x(out_b[1], -1)
        total_a = grad((0,), 0, out_b, adds=in_a)

        def over_sections(total):
            flat = total.reshape(n_sec * lows, blk, UNIT)
            return lax.all_to_all(flat, ("section", "low"), 0, 0, tiled=True)

        terms_a = over_sections(total_a)
        wide = pieces.shape[2]

        def piece(i):
            return pieces, pl.BlockSpec((None, cols, wide), lambda _, info: (i, 0, 0))

        out_y = add_near(piece(1), piece(3), *got_y, cols, wide, info, (total_a,))
        in_y = shift_y(out_y[0], 1), shift_y(out_y[1], -1)
        total_b = grad((0,), 1, out_y, adds=in_b)
        terms_b = over_sections(total_b)

        ends = XS * lows
        copies = jax.ShapeDtypeStruct((ends, blk, 2 * UNIT), bf16)

        def collect(info, a_ref, b_ref, out_ref):
            for j, ref in enumerate((a_ref, b_ref)):
                sums = jnp.sum(ref[...].astype(f32), axis=0).astype(bf16)
                for e in range(ends):
                    out_ref[e, :, j * UNIT : (j + 1) * UNIT] = sums

        (spread_out,) = small(collect, [terms_a, terms_b], [copies], info)
        gathered = lax.all_to_all(spread_out, ("x", "low"), 0, 0, tiled=True)

        def finish_y(info, keep_ref, below_ref, above_ref, key_ref, value_ref):
            sums = keep_ref[...].astype(f32) + below_ref[...].astype(f32) + above_ref[...].astype(f32)
            sums = sums.astype(bf16)
            for h in range(local_width // HEAD):
                at = 2 * h * HEAD
                key_ref[:, h * HEAD : (h + 1) * HEAD] = sums[:, at : at + HEAD]
                value_ref[:, h * HEAD : (h + 1) * HEAD] = sums[:, at + HEAD : at + 2 * HEAD]

        shard = jax.ShapeDtypeStruct((cols, local_width), bf16)
        key_weight_grad, value_weight_grad = small(
            finish_y, [piece(0), *in_y], [shard, shard], info, (spread_out,)
        )
        key_weight_grad, value_weight_grad = key_weight_grad[None], value_weight_grad[None]

        def place(info, ref, out_ref):
            for e in range(ends):
                for j in range(2):
                    at = (e // lows) * quarter + j * cols + (e % lows) * UNIT
                    out_ref[:, at : at + UNIT] = ref[e, :, j * UNIT : (j + 1) * UNIT]

        (enc_grad,) = small(place, [gathered], [jax.ShapeDtypeStruct((blk, width), bf16)], info)
        enc_grad = enc_grad[None]
        return (context, enc_grad, key_weight_grad, value_weight_grad)

    return shards


def solution(mesh):
    n_sec, n_dp, n_ten = (mesh.shape[name] for name in ("section", "dp", "tensor"))
    lows = n_ten // XS
    fine = Mesh(mesh.devices.reshape(n_sec, n_dp, XS, lows), ("section", "dp", "x", "low"))
    heads = ("x", "low")
    return jax.shard_map(
        make_shards(n_sec, n_dp, lows),
        mesh=fine,
        in_specs=(
            P("dp", "section", None),
            P("section", None, heads),
            P("section", None, heads),
            P("section", "dp", None, heads),
            P("section", "dp", None, heads),
            P("dp"),
            P("dp"),
        ),
        out_specs=(
            P("section", "dp", None, heads),
            P("dp", "section", None),
            P("section", "dp", heads),
            P("section", "dp", heads),
        ),
        check_vma=False,
    )
```

```python
import jax
import jax.numpy as jnp
from jax import lax
from jax.experimental import pallas as pl
from jax.experimental.pallas import tpu as pltpu
from jax.sharding import Mesh
from jax.sharding import PartitionSpec as P

HEAD = 256
XS = 4
UNIT = 256
masked_score = -1e30
f32 = jnp.float32
bf16 = jnp.bfloat16
X, SEC, LO, Y, CORE, SRC_LIVE, TGT_LIVE = range(7)


def dot(a, b):
    return jnp.dot(a, b, preferred_element_type=f32)


def dot_t(a, b):
    return lax.dot_general(a, b, (((1,), (1,)), ((), ())), preferred_element_type=f32)


def t_dot(a, b):
    return lax.dot_general(a, b, (((0,), (0,)), ((), ())), preferred_element_type=f32)


def mod4(v):
    return lax.rem(v + 8, 4)


def params(mib):
    return pltpu.CompilerParams(vmem_limit_bytes=mib * 1024 * 1024)


def whole(a):
    return pl.BlockSpec(a.shape, lambda i, info: (0,) * a.ndim)


ANYWHERE = pl.BlockSpec(memory_space=pl.ANY)
LIGHT = pl.CostEstimate(flops=1, bytes_accessed=1, transcendentals=0)


def project(m, enc, parts, wk, wv, acc, info, last, n_sec, after=()):
    blk, width = enc.shape
    quarter = width // XS
    total = n_sec * blk
    cols = wk.shape[1]
    heads = cols // HEAD

    def body(info, enc_ref, *refs):
        n = len(parts)
        part_refs, wk_ref, wv_ref = refs[:n], refs[n], refs[n + 1]
        acc_ref = refs[n + 2] if acc is not None else None
        out_ref, rows_ref = refs[-2:]

        @pl.when(pl.program_id(0) == 0)
        def _():
            rows_ref[pl.ds(pl.multiple_of(info[SEC] * blk, blk), blk), :] = enc_ref[...]
            for ref, (_, pieces) in zip(part_refs, parts):
                for at, count, block, off in pieces:
                    to = block_of(info, block, n_sec) * blk + off
                    rows_ref[pl.ds(pl.multiple_of(to, count), count), :] = ref[at : at + count, :]

        rows = rows_ref[...]
        k_part = dot(rows, wk_ref[...])
        v_part = dot(rows, wv_ref[...])
        if acc_ref is not None:
            k_part = k_part + acc_ref[:, :HEAD]
            v_part = v_part + acc_ref[:, HEAD:]
        out_ref[:, :HEAD] = k_part.astype(out_ref.dtype)
        out_ref[:, HEAD:] = v_part.astype(out_ref.dtype)

    def at_quarter(info):
        return mod4(info[X] - m)

    weight = pl.BlockSpec((quarter, HEAD), lambda h, info: (at_quarter(info), h))
    pair = pl.BlockSpec((total, 2 * HEAD), lambda h, info: (0, h))
    out_shape = [
        jax.ShapeDtypeStruct((total, 2 * cols), bf16 if last else f32),
        jax.ShapeDtypeStruct((total, quarter), bf16),
    ]
    return pl.pallas_call(
        body,
        grid_spec=pltpu.PrefetchScalarGridSpec(
            num_scalar_prefetch=1,
            grid=(heads,),
            in_specs=[pl.BlockSpec((blk, quarter), lambda h, info: (0, at_quarter(info)))]
            + [whole(p) for p, _ in parts]
            + [weight, weight]
            + ([pair] if acc is not None else [])
            + [ANYWHERE] * len(after),
            out_specs=[pair, whole(out_shape[1])],
        ),
        out_shape=out_shape,
        compiler_params=params(24),
        cost_estimate=LIGHT,
    )(info, enc, *[p for p, _ in parts], wk, wv, *([acc] if acc is not None else []), *after)


def attention(kv, q, g, info, after):
    total, targets, width = kv.shape[0], q.shape[0], q.shape[1]
    heads = width // HEAD
    scale = HEAD ** (-0.5)

    def body(info, kv_ref, q_ref, g_ref, *refs):
        ctx_ref, act_ref = refs[-2:]
        k, v, q = kv_ref[:, :HEAD], kv_ref[:, HEAD:], q_ref[...]
        place = lax.broadcasted_iota(jnp.int32, (total, 1), 0)
        scores = dot_t(k, q) * scale
        scores = jnp.where(place < info[SRC_LIVE], scores, masked_score)
        highest = jnp.max(scores, axis=0, keepdims=True)
        shifted = jnp.exp(scores - highest)
        weights = shifted * (1.0 / jnp.sum(shifted, axis=0, keepdims=True))
        low = weights.astype(bf16)
        target = lax.broadcasted_iota(jnp.int32, (targets, 1), 0)
        g = jnp.where(target < info[TGT_LIVE], g_ref[...].astype(f32), 0.0).astype(bf16)
        prob = dot_t(v, g)
        prob_dot = jnp.sum(weights * prob, axis=0, keepdims=True)
        grad = (weights * (prob - prob_dot) * scale).astype(bf16)
        act_ref[:, :HEAD] = dot(grad, q).astype(bf16)
        act_ref[:, HEAD:] = dot(low, g).astype(bf16)
        ctx_ref[...] = t_dot(low, v).astype(bf16)

    def cols(n, w):
        return pl.BlockSpec((n, w), lambda h, info: (0, h))

    return pl.pallas_call(
        body,
        grid_spec=pltpu.PrefetchScalarGridSpec(
            num_scalar_prefetch=1,
            grid=(heads,),
            in_specs=[cols(total, 2 * HEAD), cols(targets, HEAD), cols(targets, HEAD)] + [ANYWHERE] * len(after),
            out_specs=[cols(targets, HEAD), cols(total, 2 * HEAD)],
        ),
        out_shape=[
            jax.ShapeDtypeStruct((targets, width), bf16),
            jax.ShapeDtypeStruct((total, 2 * width), bf16),
        ],
        compiler_params=params(20),
        cost_estimate=LIGHT,
    )(info, kv, q, g, *after)


def block_of(info, which, n_sec):
    back = (0, 1 + 2 * info[LO], 3 - 2 * info[LO], 2)[which]
    return lax.rem(info[SEC] - back + n_sec, n_sec)


def partial_grad(act, wk, wv, info, quarters, dtype, after=(), first=None):
    total, cols = act.shape[0], wk.shape[1]
    width = wk.shape[0]
    heads = cols // HEAD
    per = width // XS // UNIT
    n = per * len(quarters)

    def unit(i, info):
        quarter = i // per
        m = quarters[0]
        for j, other in enumerate(quarters[1:]):
            m = jnp.where(quarter == j + 1, other, m)
        return mod4(info[X] - m) * per + i % per

    def body(info, act_ref, wk_ref, wv_ref, *refs):
        sums = None
        for h in range(heads):
            for j, w_ref in enumerate((wk_ref, wv_ref)):
                at = (2 * h + j) * HEAD
                term = dot_t(act_ref[:, at : at + HEAD], w_ref[:, h * HEAD : (h + 1) * HEAD])
                sums = term if sums is None else sums + term
        if first is None:
            refs[-1][...] = sums.astype(dtype)
        else:
            out_ref, up_ref, down_ref = refs[-3:]
            out_ref[...] = sums.astype(dtype)
            n_sec, blk = first
            at = block_of(info, 3, n_sec) * blk
            up_ref[...] = out_ref[pl.ds(pl.multiple_of(at, blk), blk // 2), :]
            down_ref[...] = out_ref[pl.ds(pl.multiple_of(at + blk // 2, blk // 2), blk // 2), :]

    weight = pl.BlockSpec((UNIT, cols), lambda i, info: (unit(i, info), 0))
    block = pl.BlockSpec((total, UNIT), lambda i, info: (0, i))
    out_specs, out_shape = [block], [jax.ShapeDtypeStruct((total, n * UNIT), dtype)]
    if first is not None:
        rows = first[1] // 2
        out_specs += [pl.BlockSpec((rows, UNIT), lambda i, info: (0, i))] * 2
        out_shape += [jax.ShapeDtypeStruct((rows, n * UNIT), dtype)] * 2
    return pl.pallas_call(
        body,
        grid_spec=pltpu.PrefetchScalarGridSpec(
            num_scalar_prefetch=1,
            grid=(n,),
            in_specs=[whole(act), weight, weight] + [ANYWHERE] * len(after),
            out_specs=out_specs,
        ),
        out_shape=out_shape,
        compiler_params=params(12),
        cost_estimate=LIGHT,
    )(info, act, wk, wv, *after)


def pair_grads(kept, got, act, act_other, info, after):
    width = act.shape[1]
    counts = (2, 1, 1)
    half = kept.shape[1] // sum(counts)

    def body(info, kept_ref, got_ref, act_ref, other_ref, *refs):
        at = 0
        for ref, count in zip(refs[-3:], counts):
            for j in range(count):
                here = slice(at, at + half)
                term = t_dot(kept_ref[:, here], act_ref[...]) + t_dot(got_ref[:, here], other_ref[...])
                ref[j * half : (j + 1) * half, :] = term.astype(bf16)
                at += half

    out = [jax.ShapeDtypeStruct((count * half, width), bf16) for count in counts]
    return small(body, [kept, got, act, act_other], out, info, after)


def small(body, ins, outs, info, after=()):
    ins = [i if isinstance(i, tuple) else (i, whole(i)) for i in ins]
    n = len(ins)

    def run(info, *refs):
        body(info, *refs[:n], *refs[n + len(after) :])

    return pl.pallas_call(
        run,
        grid_spec=pltpu.PrefetchScalarGridSpec(
            num_scalar_prefetch=1,
            grid=(1,),
            in_specs=[s for _, s in ins] + [ANYWHERE] * len(after),
            out_specs=[whole(o) for o in outs],
        ),
        out_shape=[jax.ShapeDtypeStruct(o.shape, o.dtype) for o in outs],
        compiler_params=params(28),
        cost_estimate=LIGHT,
    )(info, *[a for a, _ in ins], *after)


def make_shards(n_sec):

    def shift_x(v, k):
        return lax.ppermute(v, "x", [(i, (i + k) % XS) for i in range(XS)])

    def swap_core(v):
        return lax.ppermute(v, "core", [(0, 1), (1, 0)])

    def swap_low(v):
        return lax.ppermute(v, "low", [(0, 1), (1, 0)])

    def cross(v):
        n = 2 * n_sec
        return lax.ppermute(v, ("section", "low"), [(z, (z + (1 if z % 2 else -1)) % n) for z in range(n)])

    def shift_y(v):
        n = 2 * XS
        return lax.ppermute(v, ("y", "core"), [(i, (i + (-2 if i % 2 else 2)) % n) for i in range(n)])

    def shards(enc_out, key_weight, value_weight, queries, ctx_grad, src_pad, tgt_pad):
        enc, wk, wv = enc_out[0], key_weight[0], value_weight[0]
        blk, width = enc.shape
        quarter = width // XS
        local_width = wk.shape[1]
        total_src = n_sec * blk
        x, lo, sec = lax.axis_index("x"), lax.axis_index("low"), lax.axis_index("section")
        info = jnp.stack(
            [
                x,
                sec,
                lo,
                lax.axis_index("y"),
                lax.axis_index("core"),
                total_src - src_pad[0],
                queries.shape[2] - tgt_pad[0],
            ]
        ).astype(jnp.int32)

        mine = lax.dynamic_slice(enc, (0, x * quarter), (blk, quarter))
        mid = blk // 2

        def both(up, down):
            return shift_x(up, 1), shift_x(down, -1)

        def with_half(block, up, down, after=()):
            out = jax.ShapeDtypeStruct((blk + mid, quarter), bf16)

            def body(info, block_ref, up_ref, down_ref, up_out, down_out):
                up_out[:blk] = block_ref[...]
                up_out[blk:] = up_ref[:mid]
                down_out[:blk] = block_ref[...]
                down_out[blk:] = down_ref[mid:blk]

            return small(body, [block, up, down], [out, out], info, after)

        b1 = cross(mine)
        b2 = swap_low(b1)
        u1, d1 = both(b1, b1)
        b3 = cross(b2)
        u2, d2 = both(*with_half(b2, u1, d1))
        out3 = with_half(b3, u2, d2)
        u3, d3 = both(*out3)
        rows = [None] * XS
        acc, rows[0] = project(
            0, enc, [(b, [(0, blk, i + 1, 0)]) for i, b in enumerate((b1, b2, b3))], wk, wv, None, info, False, n_sec, out3
        )

        def cut(info, up_ref, down_ref, up_out, down_out):
            up_out[...] = up_ref[:mid]
            down_out[...] = down_ref[mid:blk]

        out4 = small(cut, [u3, d3], [jax.ShapeDtypeStruct((mid, quarter), bf16)] * 2, info, (acc,))
        u4, d4 = both(*out4)
        for m, got in ((1, (u1, u2, u3)), (3, (d1, d2, d3))):
            acc, rows[m] = project(
                m, enc, [(g, [(0, blk, i + 1, 0)]) for i, g in enumerate(got)], wk, wv, acc, info, False, n_sec, out4
            )
        last = [(u2, [(blk, mid, 1, 0)]), (d2, [(blk, mid, 1, mid)]), (u3, [(blk, mid, 2, 0)]), (d3, [(blk, mid, 2, mid)])]
        last += [(u4, [(0, mid, 3, 0)]), (d4, [(0, mid, 3, mid)])]
        acc, rows[2] = project(2, enc, last, wk, wv, acc, info, True, n_sec)

        half = quarter // 2

        def pack(info, *refs):
            core = info[CORE]
            row_refs, (kept_ref, sent_ref) = refs[:XS], refs[XS:]
            for m, ref in enumerate(row_refs):
                step = mod4(info[X] - info[Y] - m)
                for out_ref, side in ((kept_ref, core), (sent_ref, 1 - core)):

                    @pl.when(step == 1 + 2 * side)
                    def _():
                        out_ref[:, :quarter] = ref[...]

                    for place, at in ((2, quarter), (0, quarter + half)):

                        @pl.when(step == place)
                        def _():
                            out_ref[:, at : at + half] = ref[:, pl.ds(pl.multiple_of(side * half, half), half)]

        packed = jax.ShapeDtypeStruct((total_src, 2 * quarter), bf16)
        kept, sent = small(pack, rows, [packed, packed], info)
        got = swap_core(sent)

        context, act = attention(acc, queries[0, 0], ctx_grad[0, 0], info, (sent,))
        context = context[None, None]
        act_other = swap_core(act)

        far, up, down = partial_grad(act, wk, wv, info, (2,), bf16, first=(n_sec, blk))
        up, down = both(up, down)
        (near,) = partial_grad(act, wk, wv, info, (3, 1), f32, (far,))
        (keep,) = partial_grad(act, wk, wv, info, (0,), f32, (near,))
        def stage(done, sent, following, up, down, carried, after=(), through=None):
            ins, outs = [up, down], []
            if done is not None:
                ins.append((keep, pl.BlockSpec((blk, quarter), lambda i, info: (block_of(info, done, n_sec), 0))))
                outs.append(jax.ShapeDtypeStruct((blk, quarter), bf16))
            if carried is not None:
                ins.append(carried)
            if sent is not None:
                ins.append((near, pl.BlockSpec((blk, 2 * quarter), lambda i, info: (block_of(info, sent, n_sec), 0))))
                size = blk if following is None else blk + mid
                outs += [jax.ShapeDtypeStruct((size, quarter), bf16)] * 2
            if following is not None:
                ins.append((far, pl.BlockSpec((blk, quarter), lambda i, info: (block_of(info, following, n_sec), 0))))

            if through is not None:
                ins.append(through)
                outs.append(through)

            def body(info, *refs):
                refs = list(refs)
                if through is not None:
                    refs.pop()[...] = refs.pop(len(ins) - 1)[...]
                up_ref, down_ref = refs.pop(0), refs.pop(0)
                if done is not None:
                    sums = refs.pop(0)[...] + up_ref[:blk].astype(f32) + down_ref[:blk].astype(f32)
                    if carried is not None:
                        sums = sums + refs.pop(0)[...].astype(f32)
                near_ref = refs.pop(0) if sent is not None else None
                far_ref = refs.pop(0) if following is not None else None
                if done is not None:
                    refs.pop(0)[...] = sums.astype(bf16)
                if sent is not None:
                    up_out, down_out = refs
                    at = blk if done is not None else 0
                    half_up, half_down = up_ref[at : at + mid].astype(f32), down_ref[at : at + mid].astype(f32)
                    up_out[:mid] = (near_ref[:mid, :quarter] + half_up).astype(bf16)
                    up_out[mid:blk] = near_ref[mid:, :quarter].astype(bf16)
                    down_out[:mid] = near_ref[:mid, quarter:].astype(bf16)
                    down_out[mid:blk] = (near_ref[mid:, quarter:] + half_down).astype(bf16)
                    if following is not None:
                        up_out[blk:] = far_ref[:mid]
                        down_out[blk:] = far_ref[mid:]

            return small(body, ins, outs, info, after)

        out = stage(None, 3, 2, up, down, None)
        up, down = both(*out)
        near_y, far_y, keep_y = pair_grads(kept, got, act, act_other, info, out)
        total, up, down, far_y = stage(3, 2, 1, up, down, None, through=far_y)
        got_y = shift_y(far_y)
        (up, down), carried = both(up, down), cross(total)
        total, up, down = stage(2, 1, 0, up, down, carried)
        (up, down), carried = both(up, down), swap_low(total)
        def add_y(info, near_ref, got_ref, out_ref):
            out_ref[...] = near_ref[...]
            at = pl.ds(pl.multiple_of(info[CORE] * half, half), half)
            out_ref[at, :] = (near_ref[at, :].astype(f32) + got_ref[...].astype(f32)).astype(bf16)

        (out_y,) = small(add_y, [near_y, got_y], [near_y], info, (total,))
        in_y = shift_y(out_y)
        total, up, down = stage(1, 0, None, up, down, carried, (out_y,))
        (up, down), carried = both(up, down), cross(total)
        (mine,) = stage(0, None, None, up, down, carried)
        other = swap_low(mine)
        part = mine

        def add_two(info, one_ref, two_ref, out_ref):
            out_ref[...] = (one_ref[...].astype(f32) + two_ref[...].astype(f32)).astype(bf16)

        (final,) = small(add_two, [mine, other], [part], info)
        gathered = [final] + [shift_x(final, k) for k in range(1, XS)]

        def halve(info, in_ref, out_ref):
            out_ref[...] = in_ref[pl.ds(pl.multiple_of((1 - info[CORE]) * half, half), half), :]

        (away_y,) = small(halve, [in_y], [keep_y], info, (final,))
        home_y = swap_core(away_y)

        def place(info, *refs):
            for k in range(XS):
                at = mod4(info[X] - k) * quarter
                refs[-1][:, pl.ds(pl.multiple_of(at, quarter), quarter)] = refs[k][...]

        (enc_grad,) = small(place, gathered, [jax.ShapeDtypeStruct((blk, width), bf16)], info, (away_y,))
        enc_grad = enc_grad[None]

        def finish(info, keep_ref, in_ref, home_ref, key_ref, value_ref):
            at = pl.ds(pl.multiple_of(info[CORE] * half, half), half)
            sums = keep_ref[...].astype(f32) + in_ref[at, :].astype(f32) + home_ref[...].astype(f32)
            sums = sums.astype(bf16)
            for h in range(local_width // HEAD):
                at = 2 * h * HEAD
                key_ref[:, h * HEAD : (h + 1) * HEAD] = sums[:, at : at + HEAD]
                value_ref[:, h * HEAD : (h + 1) * HEAD] = sums[:, at + HEAD : at + 2 * HEAD]

        shard = jax.ShapeDtypeStruct((half, local_width), bf16)
        key_weight_grad, value_weight_grad = small(finish, [keep_y, in_y, home_y], [shard, shard], info)
        key_weight_grad, value_weight_grad = key_weight_grad[None], value_weight_grad[None]
        return (context, enc_grad, key_weight_grad, value_weight_grad)

    return shards


def solution(mesh):
    n_sec, n_dp, n_ten = (mesh.shape[name] for name in ("section", "dp", "tensor"))
    fine = Mesh(
        mesh.devices.reshape(n_sec, n_dp // 2, 2, XS, n_ten // XS), ("section", "y", "core", "x", "low")
    )
    dp, heads = ("y", "core"), ("x", "low")
    return jax.shard_map(
        make_shards(n_sec),
        mesh=fine,
        in_specs=(
            P(dp, "section", None),
            P("section", None, heads),
            P("section", None, heads),
            P("section", dp, None, heads),
            P("section", dp, None, heads),
            P(dp),
            P(dp),
        ),
        out_specs=(
            P("section", dp, None, heads),
            P(dp, "section", None),
            P("section", dp, heads),
            P("section", dp, heads),
        ),
        check_vma=False,
    )
```

```python
import jax
import jax.numpy as jnp
from jax import lax
from jax.experimental import pallas as pl
from jax.experimental.pallas import tpu as pltpu
from jax.sharding import Mesh
from jax.sharding import PartitionSpec as P

HEAD = 256
XS = 4
UNIT = 512
masked_score = -1e30
f32 = jnp.float32
bf16 = jnp.bfloat16
X, SEC, LO, Y, CORE, SRC_LIVE, TGT_LIVE = range(7)


def dot(a, b):
    return jnp.dot(a, b, preferred_element_type=f32)


def dot_t(a, b):
    return lax.dot_general(a, b, (((1,), (1,)), ((), ())), preferred_element_type=f32)


def t_dot(a, b):
    return lax.dot_general(a, b, (((0,), (0,)), ((), ())), preferred_element_type=f32)


def mod4(v):
    return lax.rem(v + 8, 4)


def params(mib):
    return pltpu.CompilerParams(vmem_limit_bytes=mib * 1024 * 1024)


def whole(a):
    return pl.BlockSpec(a.shape, lambda i, info: (0,) * a.ndim)


ANYWHERE = pl.BlockSpec(memory_space=pl.ANY)
LIGHT = pl.CostEstimate(flops=1, bytes_accessed=1, transcendentals=0)


def project(quarters, enc, wk, wv, acc, info, n_sec, after=(), queries=None):
    blk, width = enc.shape
    quarter = width // XS
    total = n_sec * blk
    cols = wk.shape[1]
    heads = cols // HEAD
    parts = [part for _, some in quarters for part in some]
    extra = ([] if acc is None else [acc]) + list(queries or ())
    n = len(quarters)

    def body(info, *refs):
        refs = list(refs)
        enc_refs = [refs.pop(0) for _ in quarters]
        part_refs = [refs.pop(0) for _ in parts]
        weight_refs = [refs.pop(0) for _ in range(2 * n)]
        acc_ref = refs.pop(0) if acc is not None else None
        rows_refs = refs[-n:]

        @pl.when(pl.program_id(0) == 0)
        def _():
            left = list(part_refs)
            for rows_ref, enc_ref, (_, some) in zip(rows_refs, enc_refs, quarters):
                rows_ref[pl.ds(pl.multiple_of(info[SEC] * blk, blk), blk), :] = enc_ref[...]
                for _, pieces in some:
                    ref = left.pop(0)
                    for at, count, block, off in pieces:
                        to = block_of(info, block, n_sec) * blk + off
                        rows_ref[pl.ds(pl.multiple_of(to, count), count), :] = ref[at : at + count, :]

        sums = [None if acc_ref is None else acc_ref[:, j * HEAD : (j + 1) * HEAD] for j in range(2)]
        for i, rows_ref in enumerate(rows_refs):
            rows = rows_ref[...]
            for j in range(2):
                term = dot(rows, weight_refs[2 * i + j][...])
                sums[j] = term if sums[j] is None else sums[j] + term
        if queries is None:
            refs[-n - 1][:, :HEAD] = sums[0]
            refs[-n - 1][:, HEAD:] = sums[1]
        else:
            k, v = (one.astype(bf16) for one in sums)
            attend(k, v, refs[0][...], refs[1][...], info, refs[-n - 2], refs[-n - 1])

    def head(rows, count):
        return pl.BlockSpec((rows, count * HEAD), lambda h, info: (0, h))

    def enc_block(m):
        return pl.BlockSpec((blk, quarter), lambda h, info: (0, mod4(info[X] - m)))

    def weight(m):
        return pl.BlockSpec((quarter, HEAD), lambda h, info: (mod4(info[X] - m), h))

    rows_out = jax.ShapeDtypeStruct((total, quarter), bf16)
    if queries is None:
        targets = 0
        out_shape, out_specs = [jax.ShapeDtypeStruct((total, 2 * cols), f32)], [head(total, 2)]
    else:
        targets = queries[0].shape[0]
        out_shape = [
            jax.ShapeDtypeStruct((targets, cols), bf16),
            jax.ShapeDtypeStruct((total, 2 * cols), bf16),
        ]
        out_specs = [head(targets, 1), head(total, 2)]
    return pl.pallas_call(
        body,
        grid_spec=pltpu.PrefetchScalarGridSpec(
            num_scalar_prefetch=1,
            grid=(heads,),
            in_specs=[enc_block(m) for m, _ in quarters]
            + [whole(p) for p, _ in parts]
            + [weight(m) for m, _ in quarters for _ in range(2)]
            + ([] if acc is None else [head(total, 2)])
            + ([] if queries is None else [head(targets, 1)] * 2)
            + [ANYWHERE] * len(after),
            out_specs=out_specs + [whole(rows_out)] * n,
        ),
        out_shape=out_shape + [rows_out] * n,
        compiler_params=params(24),
        cost_estimate=LIGHT,
    )(info, *[enc] * n, *[p for p, _ in parts], *[wk, wv] * n, *extra, *after)


def attend(k, v, q, g, info, ctx_ref, act_ref):
    scale = HEAD ** (-0.5)
    place = lax.broadcasted_iota(jnp.int32, (k.shape[0], 1), 0)
    scores = dot_t(k, q) * scale
    scores = jnp.where(place < info[SRC_LIVE], scores, masked_score)
    highest = jnp.max(scores, axis=0, keepdims=True)
    shifted = jnp.exp(scores - highest)
    weights = shifted * (1.0 / jnp.sum(shifted, axis=0, keepdims=True))
    low = weights.astype(bf16)
    target = lax.broadcasted_iota(jnp.int32, (q.shape[0], 1), 0)
    g = jnp.where(target < info[TGT_LIVE], g.astype(f32), 0.0).astype(bf16)
    prob = dot_t(v, g)
    prob_dot = jnp.sum(weights * prob, axis=0, keepdims=True)
    grad = (weights * (prob - prob_dot) * scale).astype(bf16)
    act_ref[:, :HEAD] = dot(grad, q).astype(bf16)
    act_ref[:, HEAD:] = dot(low, g).astype(bf16)
    ctx_ref[...] = t_dot(low, v).astype(bf16)


def block_of(info, which, n_sec):
    back = (0, 1 + 2 * info[LO], 3 - 2 * info[LO], 2)[which]
    return lax.rem(info[SEC] - back + n_sec, n_sec)


def partial_grad(act, wk, wv, info, quarters, dtype, after=(), first=None):
    total, cols = act.shape[0], wk.shape[1]
    width = wk.shape[0]
    heads = cols // HEAD
    per = width // XS // UNIT
    n = per * len(quarters)

    def unit(i, info):
        quarter = i // per
        m = quarters[0]
        for j, other in enumerate(quarters[1:]):
            m = jnp.where(quarter == j + 1, other, m)
        return mod4(info[X] - m) * per + i % per

    def body(info, act_ref, wk_ref, wv_ref, *refs):
        sums = None
        for h in range(heads):
            for j, w_ref in enumerate((wk_ref, wv_ref)):
                at = (2 * h + j) * HEAD
                term = dot_t(act_ref[:, at : at + HEAD], w_ref[:, h * HEAD : (h + 1) * HEAD])
                sums = term if sums is None else sums + term
        if first is None:
            refs[-1][...] = sums.astype(dtype)
        else:
            out_ref, up_ref, down_ref = refs[-3:]
            out_ref[...] = sums.astype(dtype)
            n_sec, blk = first
            at = block_of(info, 3, n_sec) * blk
            up_ref[...] = out_ref[pl.ds(pl.multiple_of(at, blk), blk // 2), :]
            down_ref[...] = out_ref[pl.ds(pl.multiple_of(at + blk // 2, blk // 2), blk // 2), :]

    weight = pl.BlockSpec((UNIT, cols), lambda i, info: (unit(i, info), 0))
    block = pl.BlockSpec((total, UNIT), lambda i, info: (0, i))
    out_specs, out_shape = [block], [jax.ShapeDtypeStruct((total, n * UNIT), dtype)]
    if first is not None:
        rows = first[1] // 2
        out_specs += [pl.BlockSpec((rows, UNIT), lambda i, info: (0, i))] * 2
        out_shape += [jax.ShapeDtypeStruct((rows, n * UNIT), dtype)] * 2
    return pl.pallas_call(
        body,
        grid_spec=pltpu.PrefetchScalarGridSpec(
            num_scalar_prefetch=1,
            grid=(n,),
            in_specs=[whole(act), weight, weight] + [ANYWHERE] * len(after),
            out_specs=out_specs,
        ),
        out_shape=out_shape,
        compiler_params=params(12),
        cost_estimate=LIGHT,
    )(info, act, wk, wv, *after)


def pair_grads(kept, got, act, act_other, info, after):
    width = act.shape[1]
    counts = (2, 1, 1)
    half = kept.shape[1] // sum(counts)

    def body(info, kept_ref, got_ref, act_ref, other_ref, *refs):
        at = 0
        for ref, count in zip(refs[-3:], counts):
            for j in range(count):
                here = slice(at, at + half)
                term = t_dot(kept_ref[:, here], act_ref[...]) + t_dot(got_ref[:, here], other_ref[...])
                ref[j * half : (j + 1) * half, :] = term.astype(bf16)
                at += half

    out = [jax.ShapeDtypeStruct((count * half, width), bf16) for count in counts]
    return small(body, [kept, got, act, act_other], out, info, after)


def small(body, ins, outs, info, after=()):
    ins = [i if isinstance(i, tuple) else (i, whole(i)) for i in ins]
    n = len(ins)

    def run(info, *refs):
        body(info, *refs[:n], *refs[n + len(after) :])

    return pl.pallas_call(
        run,
        grid_spec=pltpu.PrefetchScalarGridSpec(
            num_scalar_prefetch=1,
            grid=(1,),
            in_specs=[s for _, s in ins] + [ANYWHERE] * len(after),
            out_specs=[whole(o) for o in outs],
        ),
        out_shape=[jax.ShapeDtypeStruct(o.shape, o.dtype) for o in outs],
        compiler_params=params(28),
        cost_estimate=LIGHT,
    )(info, *[a for a, _ in ins], *after)


def make_shards(n_sec):

    def shift_x(v, k):
        return lax.ppermute(v, "x", [(i, (i + k) % XS) for i in range(XS)])

    def swap_core(v):
        return lax.ppermute(v, "core", [(0, 1), (1, 0)])

    def swap_low(v):
        return lax.ppermute(v, "low", [(0, 1), (1, 0)])

    def cross(v):
        n = 2 * n_sec
        return lax.ppermute(v, ("section", "low"), [(z, (z + (1 if z % 2 else -1)) % n) for z in range(n)])

    def shift_y(v, change=False):
        n = 2 * XS
        pairs = [(i, (i + (-2 if i % 2 else 2)) % n) for i in range(n)]
        return lax.ppermute(v, ("y", "core"), [(i, j ^ 1 if change else j) for i, j in pairs])

    def shards(enc_out, key_weight, value_weight, queries, ctx_grad, src_pad, tgt_pad):
        enc, wk, wv = enc_out[0], key_weight[0], value_weight[0]
        blk, width = enc.shape
        quarter = width // XS
        local_width = wk.shape[1]
        total_src = n_sec * blk
        x, lo, sec = lax.axis_index("x"), lax.axis_index("low"), lax.axis_index("section")
        info = jnp.stack(
            [
                x,
                sec,
                lo,
                lax.axis_index("y"),
                lax.axis_index("core"),
                total_src - src_pad[0],
                queries.shape[2] - tgt_pad[0],
            ]
        ).astype(jnp.int32)

        mine = lax.dynamic_slice(enc, (0, x * quarter), (blk, quarter))
        mid = blk // 2

        def both(up, down):
            return shift_x(up, 1), shift_x(down, -1)

        def with_half(block, up, down, after=()):
            out = jax.ShapeDtypeStruct((blk + mid, quarter), bf16)

            def body(info, block_ref, up_ref, down_ref, up_out, down_out):
                up_out[:blk] = block_ref[...]
                up_out[blk:] = up_ref[:mid]
                down_out[:blk] = block_ref[...]
                down_out[blk:] = down_ref[mid:blk]

            return small(body, [block, up, down], [out, out], info, after)

        b1 = cross(mine)
        b2 = swap_low(b1)
        u1, d1 = both(b1, b1)
        b3 = cross(b2)
        u2, d2 = both(*with_half(b2, u1, d1))
        out3 = with_half(b3, u2, d2)
        u3, d3 = both(*out3)
        rows = [None] * XS

        def parts(*got):
            return [(g, [(0, blk, i + 1, 0)]) for i, g in enumerate(got)]

        acc, rows[0] = project([(0, parts(b1, b2, b3))], enc, wk, wv, None, info, n_sec, out3)

        def cut(info, up_ref, down_ref, up_out, down_out):
            up_out[...] = up_ref[:mid]
            down_out[...] = down_ref[mid:blk]

        out4 = small(cut, [u3, d3], [jax.ShapeDtypeStruct((mid, quarter), bf16)] * 2, info, (acc,))
        u4, d4 = both(*out4)
        beside = [(1, parts(u1, u2, u3)), (3, parts(d1, d2, d3))]
        acc, rows[1], rows[3] = project(beside, enc, wk, wv, acc, info, n_sec, out4)
        last = [(u2, [(blk, mid, 1, 0)]), (d2, [(blk, mid, 1, mid)]), (u3, [(blk, mid, 2, 0)]), (d3, [(blk, mid, 2, mid)])]
        last += [(u4, [(0, mid, 3, 0)]), (d4, [(0, mid, 3, mid)])]
        asked = (queries[0, 0], ctx_grad[0, 0])
        context, act, rows[2] = project([(2, last)], enc, wk, wv, acc, info, n_sec, queries=asked)
        context = context[None, None]
        act_other = swap_core(act)

        half = quarter // 2

        def pack(own, after=()):
            def body(info, *refs):
                side = info[CORE] if own else 1 - info[CORE]
                for m, ref in enumerate(refs[:-1]):
                    step = mod4(info[X] - info[Y] - m)

                    @pl.when(step == 1 + 2 * side)
                    def _():
                        refs[-1][:, :quarter] = ref[...]

                    for place, at in ((2, quarter), (0, quarter + half)):

                        @pl.when(step == place)
                        def _():
                            refs[-1][:, at : at + half] = ref[:, pl.ds(pl.multiple_of(side * half, half), half)]

            return small(body, rows, [jax.ShapeDtypeStruct((total_src, 2 * quarter), bf16)], info, after)[0]

        sent = pack(False)
        got = swap_core(sent)

        far, up, down = partial_grad(act, wk, wv, info, (2,), bf16, first=(n_sec, blk))
        up, down = both(up, down)
        (near,) = partial_grad(act, wk, wv, info, (3, 1), f32, (far,))
        kept = pack(True, (near,))
        (keep,) = partial_grad(act, wk, wv, info, (0,), f32, (near,))
        def stage(done, sent, following, up, down, carried, after=(), through=None):
            ins, outs = [up, down], []
            if done is not None:
                ins.append((keep, pl.BlockSpec((blk, quarter), lambda i, info: (block_of(info, done, n_sec), 0))))
                outs.append(jax.ShapeDtypeStruct((blk, quarter), bf16))
            if carried is not None:
                ins.append(carried)
            if sent is not None:
                ins.append((near, pl.BlockSpec((blk, 2 * quarter), lambda i, info: (block_of(info, sent, n_sec), 0))))
                size = blk if following is None else blk + mid
                outs += [jax.ShapeDtypeStruct((size, quarter), bf16)] * 2
            if following is not None:
                ins.append((far, pl.BlockSpec((blk, quarter), lambda i, info: (block_of(info, following, n_sec), 0))))

            if through is not None:
                ins.append(through)
                outs.append(through)

            def body(info, *refs):
                refs = list(refs)
                if through is not None:
                    refs.pop()[...] = refs.pop(len(ins) - 1)[...]
                up_ref, down_ref = refs.pop(0), refs.pop(0)
                if done is not None:
                    sums = refs.pop(0)[...] + up_ref[:blk].astype(f32) + down_ref[:blk].astype(f32)
                    if carried is not None:
                        sums = sums + refs.pop(0)[...].astype(f32)
                near_ref = refs.pop(0) if sent is not None else None
                far_ref = refs.pop(0) if following is not None else None
                if done is not None:
                    refs.pop(0)[...] = sums.astype(bf16)
                if sent is not None:
                    up_out, down_out = refs
                    at = blk if done is not None else 0
                    half_up, half_down = up_ref[at : at + mid].astype(f32), down_ref[at : at + mid].astype(f32)
                    up_out[:mid] = (near_ref[:mid, :quarter] + half_up).astype(bf16)
                    up_out[mid:blk] = near_ref[mid:, :quarter].astype(bf16)
                    down_out[:mid] = near_ref[:mid, quarter:].astype(bf16)
                    down_out[mid:blk] = (near_ref[mid:, quarter:] + half_down).astype(bf16)
                    if following is not None:
                        up_out[blk:] = far_ref[:mid]
                        down_out[blk:] = far_ref[mid:]

            return small(body, ins, outs, info, after)

        out = stage(None, 3, 2, up, down, None)
        up, down = both(*out)
        near_y, far_y, keep_y = pair_grads(kept, got, act, act_other, info, out)
        total, up, down, far_y = stage(3, 2, 1, up, down, None, through=far_y)
        got_y = shift_y(far_y)
        (up, down), carried = both(up, down), cross(total)
        total, up, down = stage(2, 1, 0, up, down, carried)
        (up, down), carried = both(up, down), swap_low(total)
        total, up, down = stage(1, 0, None, up, down, carried)

        def add_y(info, near_ref, got_ref, same_ref, other_ref):
            here = pl.ds(pl.multiple_of(info[CORE] * half, half), half)
            there = pl.ds(pl.multiple_of((1 - info[CORE]) * half, half), half)
            same_ref[...] = (near_ref[here, :].astype(f32) + got_ref[...].astype(f32)).astype(bf16)
            other_ref[...] = near_ref[there, :]

        same_y, other_y = small(add_y, [near_y, got_y], [keep_y, keep_y], info, (total,))
        in_y = shift_y(same_y), shift_y(other_y, True)
        (up, down), carried = both(up, down), cross(total)
        (mine,) = stage(0, None, None, up, down, carried)
        other = swap_low(mine)
        part = mine

        def add_two(info, one_ref, two_ref, out_ref):
            out_ref[...] = (one_ref[...].astype(f32) + two_ref[...].astype(f32)).astype(bf16)

        (final,) = small(add_two, [mine, other], [part], info)
        gathered = [final] + [shift_x(final, k) for k in range(1, XS)]

        def finish(info, keep_ref, one_ref, two_ref, key_ref, value_ref):
            sums = keep_ref[...].astype(f32) + one_ref[...].astype(f32) + two_ref[...].astype(f32)
            sums = sums.astype(bf16)
            for h in range(local_width // HEAD):
                at = 2 * h * HEAD
                key_ref[:, h * HEAD : (h + 1) * HEAD] = sums[:, at : at + HEAD]
                value_ref[:, h * HEAD : (h + 1) * HEAD] = sums[:, at + HEAD : at + 2 * HEAD]

        shard = jax.ShapeDtypeStruct((half, local_width), bf16)
        key_weight_grad, value_weight_grad = small(finish, [keep_y, *in_y], [shard, shard], info)
        key_weight_grad, value_weight_grad = key_weight_grad[None], value_weight_grad[None]
        def place(info, *refs):
            for k in range(XS):
                at = mod4(info[X] - k) * quarter
                refs[-1][:, pl.ds(pl.multiple_of(at, quarter), quarter)] = refs[k][...]

        (enc_grad,) = small(place, gathered, [jax.ShapeDtypeStruct((blk, width), bf16)], info, (key_weight_grad,))
        enc_grad = enc_grad[None]

        return (context, enc_grad, key_weight_grad, value_weight_grad)

    return shards


def solution(mesh):
    n_sec, n_dp, n_ten = (mesh.shape[name] for name in ("section", "dp", "tensor"))
    fine = Mesh(
        mesh.devices.reshape(n_sec, n_dp // 2, 2, XS, n_ten // XS), ("section", "y", "core", "x", "low")
    )
    dp, heads = ("y", "core"), ("x", "low")
    return jax.shard_map(
        make_shards(n_sec),
        mesh=fine,
        in_specs=(
            P(dp, "section", None),
            P("section", None, heads),
            P("section", None, heads),
            P("section", dp, None, heads),
            P("section", dp, None, heads),
            P(dp),
            P(dp),
        ),
        out_specs=(
            P("section", dp, None, heads),
            P(dp, "section", None),
            P("section", dp, heads),
            P("section", dp, heads),
        ),
        check_vma=False,
    )
```

```python
import jax
import jax.numpy as jnp
from jax import lax
from jax.experimental import pallas as pl
from jax.experimental.pallas import tpu as pltpu
from jax.sharding import Mesh
from jax.sharding import PartitionSpec as P

HEAD = 256
XS = 4
UNIT = 512
masked_score = -1e30
f32 = jnp.float32
bf16 = jnp.bfloat16
X, SEC, LO, Y, CORE, SRC_LIVE, TGT_LIVE = range(7)


def dot(a, b):
    return jnp.dot(a, b, preferred_element_type=f32)


def dot_t(a, b):
    return lax.dot_general(a, b, (((1,), (1,)), ((), ())), preferred_element_type=f32)


def t_dot(a, b):
    return lax.dot_general(a, b, (((0,), (0,)), ((), ())), preferred_element_type=f32)


def mod4(v):
    return lax.rem(v + 8, 4)


def params(mib):
    return pltpu.CompilerParams(vmem_limit_bytes=mib * 1024 * 1024)


def whole(a):
    return pl.BlockSpec(a.shape, lambda i, info: (0,) * a.ndim)


ANYWHERE = pl.BlockSpec(memory_space=pl.ANY)
LIGHT = pl.CostEstimate(flops=1, bytes_accessed=1, transcendentals=0)


def project(quarters, enc, wk, wv, acc, info, n_sec, after=(), queries=None):
    blk, width = enc.shape
    quarter = width // XS
    total = n_sec * blk
    cols = wk.shape[1]
    heads = cols // HEAD
    parts = [part for _, some in quarters for part in some]
    extra = ([] if acc is None else [acc]) + list(queries or ())
    n = len(quarters)

    def body(info, *refs):
        refs = list(refs)
        enc_refs = [refs.pop(0) for _ in quarters]
        part_refs = [refs.pop(0) for _ in parts]
        weight_refs = [refs.pop(0) for _ in range(2 * n)]
        acc_ref = refs.pop(0) if acc is not None else None
        rows_refs = refs[-n:]

        @pl.when(pl.program_id(0) == 0)
        def _():
            left = list(part_refs)
            for rows_ref, enc_ref, (_, some) in zip(rows_refs, enc_refs, quarters):
                rows_ref[pl.ds(pl.multiple_of(info[SEC] * blk, blk), blk), :] = enc_ref[...]
                for _, pieces in some:
                    ref = left.pop(0)
                    for at, count, block, off in pieces:
                        to = block_of(info, block, n_sec) * blk + off
                        rows_ref[pl.ds(pl.multiple_of(to, count), count), :] = ref[at : at + count, :]

        sums = [None if acc_ref is None else acc_ref[:, j * HEAD : (j + 1) * HEAD] for j in range(2)]
        for i, rows_ref in enumerate(rows_refs):
            rows = rows_ref[...]
            for j in range(2):
                term = dot(rows, weight_refs[2 * i + j][...])
                sums[j] = term if sums[j] is None else sums[j] + term
        if queries is None:
            refs[-n - 1][:, :HEAD] = sums[0]
            refs[-n - 1][:, HEAD:] = sums[1]
        else:
            k, v = (one.astype(bf16) for one in sums)
            attend(k, v, refs[0][...], refs[1][...], info, refs[-n - 2], refs[-n - 1])

    def head(rows, count):
        return pl.BlockSpec((rows, count * HEAD), lambda h, info: (0, h))

    def enc_block(m):
        return pl.BlockSpec((blk, quarter), lambda h, info: (0, mod4(info[X] - m)))

    def weight(m):
        return pl.BlockSpec((quarter, HEAD), lambda h, info: (mod4(info[X] - m), h))

    rows_out = jax.ShapeDtypeStruct((total, quarter), bf16)
    if queries is None:
        targets = 0
        out_shape, out_specs = [jax.ShapeDtypeStruct((total, 2 * cols), f32)], [head(total, 2)]
    else:
        targets = queries[0].shape[0]
        out_shape = [
            jax.ShapeDtypeStruct((targets, cols), bf16),
            jax.ShapeDtypeStruct((total, 2 * cols), bf16),
        ]
        out_specs = [head(targets, 1), head(total, 2)]
    return pl.pallas_call(
        body,
        grid_spec=pltpu.PrefetchScalarGridSpec(
            num_scalar_prefetch=1,
            grid=(heads,),
            in_specs=[enc_block(m) for m, _ in quarters]
            + [whole(p) for p, _ in parts]
            + [weight(m) for m, _ in quarters for _ in range(2)]
            + ([] if acc is None else [head(total, 2)])
            + ([] if queries is None else [head(targets, 1)] * 2)
            + [ANYWHERE] * len(after),
            out_specs=out_specs + [whole(rows_out)] * n,
        ),
        out_shape=out_shape + [rows_out] * n,
        compiler_params=params(24),
        cost_estimate=LIGHT,
    )(info, *[enc] * n, *[p for p, _ in parts], *[wk, wv] * n, *extra, *after)


def attend(k, v, q, g, info, ctx_ref, act_ref):
    scale = HEAD ** (-0.5)
    place = lax.broadcasted_iota(jnp.int32, (k.shape[0], 1), 0)
    scores = dot_t(k, q) * scale
    scores = jnp.where(place < info[SRC_LIVE], scores, masked_score)
    highest = jnp.max(scores, axis=0, keepdims=True)
    shifted = jnp.exp(scores - highest)
    weights = shifted * (1.0 / jnp.sum(shifted, axis=0, keepdims=True))
    low = weights.astype(bf16)
    target = lax.broadcasted_iota(jnp.int32, (q.shape[0], 1), 0)
    g = jnp.where(target < info[TGT_LIVE], g.astype(f32), 0.0).astype(bf16)
    prob = dot_t(v, g)
    prob_dot = jnp.sum(weights * prob, axis=0, keepdims=True)
    grad = (weights * (prob - prob_dot) * scale).astype(bf16)
    act_ref[:, :HEAD] = dot(grad, q).astype(bf16)
    act_ref[:, HEAD:] = dot(low, g).astype(bf16)
    ctx_ref[...] = t_dot(low, v).astype(bf16)


def block_of(info, which, n_sec):
    back = (0, 1 + 2 * info[LO], 3 - 2 * info[LO], 2)[which]
    return lax.rem(info[SEC] - back + n_sec, n_sec)


def partial_grad(act, wk, wv, info, quarters, dtype, after=(), first=None):
    total, cols = act.shape[0], wk.shape[1]
    width = wk.shape[0]
    heads = cols // HEAD
    per = width // XS // UNIT
    n = per * len(quarters)

    def unit(i, info):
        quarter = i // per
        m = quarters[0]
        for j, other in enumerate(quarters[1:]):
            m = jnp.where(quarter == j + 1, other, m)
        return mod4(info[X] - m) * per + i % per

    def body(info, act_ref, wk_ref, wv_ref, *refs):
        sums = None
        for h in range(heads):
            for j, w_ref in enumerate((wk_ref, wv_ref)):
                at = (2 * h + j) * HEAD
                term = dot_t(act_ref[:, at : at + HEAD], w_ref[:, h * HEAD : (h + 1) * HEAD])
                sums = term if sums is None else sums + term
        if first is None:
            refs[-1][...] = sums.astype(dtype)
        else:
            out_ref, up_ref, down_ref = refs[-3:]
            out_ref[...] = sums.astype(dtype)
            n_sec, blk, blocks = first
            mid = blk // 2
            for i, which in enumerate(blocks):
                at = block_of(info, which, n_sec) * blk
                up_ref[i * mid : (i + 1) * mid, :] = out_ref[pl.ds(pl.multiple_of(at, blk), mid), :]
                down_ref[i * mid : (i + 1) * mid, :] = out_ref[pl.ds(pl.multiple_of(at + mid, mid), mid), :]

    weight = pl.BlockSpec((UNIT, cols), lambda i, info: (unit(i, info), 0))
    block = pl.BlockSpec((total, UNIT), lambda i, info: (0, i))
    out_specs, out_shape = [block], [jax.ShapeDtypeStruct((total, n * UNIT), dtype)]
    if first is not None:
        rows = first[1] // 2 * len(first[2])
        out_specs += [pl.BlockSpec((rows, UNIT), lambda i, info: (0, i))] * 2
        out_shape += [jax.ShapeDtypeStruct((rows, n * UNIT), dtype)] * 2
    return pl.pallas_call(
        body,
        grid_spec=pltpu.PrefetchScalarGridSpec(
            num_scalar_prefetch=1,
            grid=(n,),
            in_specs=[whole(act), weight, weight] + [ANYWHERE] * len(after),
            out_specs=out_specs,
        ),
        out_shape=out_shape,
        compiler_params=params(12),
        cost_estimate=LIGHT,
    )(info, act, wk, wv, *after)


def pair_grads(kept, got, act, act_other, info, blocks, after=()):
    width = act.shape[1]
    half = kept.shape[1] // XS

    def body(info, kept_ref, got_ref, act_ref, other_ref, *refs):
        for ref, group in zip(refs, blocks):
            for j, at in enumerate(group):
                here = slice(at * half, (at + 1) * half)
                term = t_dot(kept_ref[:, here], act_ref[...]) + t_dot(got_ref[:, here], other_ref[...])
                ref[j * half : (j + 1) * half, :] = term.astype(bf16)

    out = [jax.ShapeDtypeStruct((len(group) * half, width), bf16) for group in blocks]
    return small(body, [kept, got, act, act_other], out, info, after)


def small(body, ins, outs, info, after=()):
    ins = [i if isinstance(i, tuple) else (i, whole(i)) for i in ins]
    n = len(ins)

    def run(info, *refs):
        body(info, *refs[:n], *refs[n + len(after) :])

    return pl.pallas_call(
        run,
        grid_spec=pltpu.PrefetchScalarGridSpec(
            num_scalar_prefetch=1,
            grid=(1,),
            in_specs=[s for _, s in ins] + [ANYWHERE] * len(after),
            out_specs=[whole(o) for o in outs],
        ),
        out_shape=[jax.ShapeDtypeStruct(o.shape, o.dtype) for o in outs],
        compiler_params=params(28),
        cost_estimate=LIGHT,
    )(info, *[a for a, _ in ins], *after)


def make_shards(n_sec):

    def shift_x(v, k):
        return lax.ppermute(v, "x", [(i, (i + k) % XS) for i in range(XS)])

    def swap_core(v):
        return lax.ppermute(v, "core", [(0, 1), (1, 0)])

    def swap_low(v):
        return lax.ppermute(v, "low", [(0, 1), (1, 0)])

    def cross(v):
        n = 2 * n_sec
        return lax.ppermute(v, ("section", "low"), [(z, (z + (1 if z % 2 else -1)) % n) for z in range(n)])

    def jump(v, k):
        n = 2 * n_sec
        return lax.ppermute(v, ("section", "low"), [(z, (z + (-2 * k if z % 2 else 2 * k)) % n) for z in range(n)])

    def shift_y(v, change=False):
        n = 2 * XS
        pairs = [(i, (i + (-2 if i % 2 else 2)) % n) for i in range(n)]
        return lax.ppermute(v, ("y", "core"), [(i, j ^ 1 if change else j) for i, j in pairs])

    def shards(enc_out, key_weight, value_weight, queries, ctx_grad, src_pad, tgt_pad):
        enc, wk, wv = enc_out[0], key_weight[0], value_weight[0]
        blk, width = enc.shape
        quarter = width // XS
        local_width = wk.shape[1]
        total_src = n_sec * blk
        x, lo, sec = lax.axis_index("x"), lax.axis_index("low"), lax.axis_index("section")
        info = jnp.stack(
            [
                x,
                sec,
                lo,
                lax.axis_index("y"),
                lax.axis_index("core"),
                total_src - src_pad[0],
                queries.shape[2] - tgt_pad[0],
            ]
        ).astype(jnp.int32)

        mine = lax.dynamic_slice(enc, (0, x * quarter), (blk, quarter))
        mid = blk // 2

        def both(up, down):
            return shift_x(up, 1), shift_x(down, -1)

        def with_halves(block, ups, downs, after=()):
            out = jax.ShapeDtypeStruct((blk + mid * len(ups), quarter), bf16)

            def body(info, block_ref, *refs):
                up_out, down_out = refs[-2:]
                up_out[:blk] = block_ref[...]
                down_out[:blk] = block_ref[...]
                for i in range(len(ups)):
                    at = blk + i * mid
                    up_out[at : at + mid] = refs[i][:mid]
                    down_out[at : at + mid] = refs[len(ups) + i][mid:blk]

            return small(body, [block, *ups, *downs], [out, out], info, after)

        b1, b2 = cross(mine), jump(mine, -1)
        u1, d1 = both(b1, b1)
        u2, d2 = both(b2, b2)
        b3 = cross(b2)
        out3 = with_halves(b3, (u1, u2), (d1, d2))
        u3, d3 = both(*out3)
        rows = [None] * XS

        def parts(*got):
            return [(g, [(0, blk, i + 1, 0)]) for i, g in enumerate(got)]

        acc, rows[0] = project([(0, parts(b1, b2, b3))], enc, wk, wv, None, info, n_sec, out3)

        def cut(info, up_ref, down_ref, up_out, down_out):
            up_out[...] = up_ref[:mid]
            down_out[...] = down_ref[mid:blk]

        out4 = small(cut, [u3, d3], [jax.ShapeDtypeStruct((mid, quarter), bf16)] * 2, info, (acc,))
        u4, d4 = both(*out4)
        beside = [(1, parts(u1, u2, u3)), (3, parts(d1, d2, d3))]
        acc, rows[1], rows[3] = project(beside, enc, wk, wv, acc, info, n_sec, out4)
        last = [(u3, [(blk, mid, 1, 0), (blk + mid, mid, 2, 0)]), (d3, [(blk, mid, 1, mid), (blk + mid, mid, 2, mid)])]
        last += [(u4, [(0, mid, 3, 0)]), (d4, [(0, mid, 3, mid)])]
        asked = (queries[0, 0], ctx_grad[0, 0])
        context, act, rows[2] = project([(2, last)], enc, wk, wv, acc, info, n_sec, queries=asked)
        context = context[None, None]
        act_other = swap_core(act)

        half = quarter // 2

        def pack(own, after=()):
            def body(info, *refs):
                side = info[CORE] if own else 1 - info[CORE]
                for m, ref in enumerate(refs[:-1]):
                    step = mod4(info[X] - info[Y] - m)

                    @pl.when(step == 1 + 2 * side)
                    def _():
                        refs[-1][:, :quarter] = ref[...]

                    for place, at in ((2, quarter), (0, quarter + half)):

                        @pl.when(step == place)
                        def _():
                            refs[-1][:, at : at + half] = ref[:, pl.ds(pl.multiple_of(side * half, half), half)]

            return small(body, rows, [jax.ShapeDtypeStruct((total_src, 2 * quarter), bf16)], info, after)[0]

        sent = pack(False)
        got = swap_core(sent)

        far, up, down = partial_grad(act, wk, wv, info, (2,), bf16, first=(n_sec, blk, (3, 0)))
        halves = both(up, down)
        (near,) = partial_grad(act, wk, wv, info, (3, 1), bf16, (far,))
        kept = pack(True, (near,))
        (far_y,) = pair_grads(kept, got, act, act_other, info, [(2,)], (near,))
        (keep,) = partial_grad(act, wk, wv, info, (0,), f32, (near,))

        def rows_of(v, which):
            return v, pl.BlockSpec((blk, v.shape[1]), lambda i, info: (block_of(info, which, n_sec), 0))

        def stage(done, sent, ahead, after=(), through=()):
            ins, outs = [], []
            for which, (up, down), _, more in done:
                ins += [rows_of(keep, which), up, down, *more]
                outs.append(jax.ShapeDtypeStruct((blk, quarter), bf16))
            for which, (up, down), _ in sent:
                ins += [rows_of(near, which), up, down]
            ins += [rows_of(far, which) for which in ahead] + list(through)
            size = blk * len(sent) + mid * len(ahead)
            outs += [jax.ShapeDtypeStruct((size, quarter), bf16)] * (2 if size else 0) + list(through)

            def body(info, *refs):
                refs, out_refs = list(refs[: len(ins)]), list(refs[len(ins) :])
                for _, _, at, more in done:
                    sums = refs.pop(0)[...]
                    for _ in range(2):
                        sums = sums + refs.pop(0)[at : at + blk].astype(f32)
                    for _ in more:
                        sums = sums + refs.pop(0)[...].astype(f32)
                    out_refs.pop(0)[...] = sums.astype(bf16)
                to = 0
                if size:
                    up_out, down_out = out_refs.pop(0), out_refs.pop(0)
                for _, _, at in sent:
                    near_ref, up_ref, down_ref = (refs.pop(0) for _ in range(3))
                    half_up, half_down = up_ref[at : at + mid].astype(f32), down_ref[at : at + mid].astype(f32)
                    up_out[to : to + mid] = (near_ref[:mid, :quarter].astype(f32) + half_up).astype(bf16)
                    up_out[to + mid : to + blk] = near_ref[mid:, :quarter]
                    down_out[to : to + mid] = near_ref[:mid, quarter:]
                    down_out[to + mid : to + blk] = (near_ref[mid:, quarter:].astype(f32) + half_down).astype(bf16)
                    to += blk
                for _ in ahead:
                    far_ref = refs.pop(0)
                    up_out[to : to + mid] = far_ref[:mid]
                    down_out[to : to + mid] = far_ref[mid:]
                    to += mid
                for ref, out_ref in zip(refs, out_refs):
                    out_ref[...] = ref[...]

            return small(body, ins, outs, info, after)

        up, down, far_y = stage([], [(3, halves, 0)], [2, 1], through=[far_y])
        got_y = shift_y(far_y)
        near_y, keep_y = pair_grads(kept, got, act, act_other, info, [(0, 1), (3,)], (up,))
        side = both(up, down)
        total3, up, down = stage([(3, side, 0, [])], [(2, side, blk), (1, side, blk + mid)], [])
        carried = cross(total3)
        side = both(up, down)
        total2, total1, up, down = stage([(2, side, 0, [carried]), (1, side, blk, [])], [(0, halves, mid)], [])

        def add_y(info, near_ref, got_ref, same_ref, other_ref):
            here = pl.ds(pl.multiple_of(info[CORE] * half, half), half)
            there = pl.ds(pl.multiple_of((1 - info[CORE]) * half, half), half)
            same_ref[...] = (near_ref[here, :].astype(f32) + got_ref[...].astype(f32)).astype(bf16)
            other_ref[...] = near_ref[there, :]

        same_y, other_y = small(add_y, [near_y, got_y], [keep_y, keep_y], info, (total1,))
        same_y = shift_y(same_y)
        side = both(up, down)
        carried = [cross(total1), jump(total2, 1)]
        mine, other_y = stage([(0, side, 0, carried)], [], [], through=[other_y])
        in_y = same_y, shift_y(other_y, True)
        other = swap_low(mine)
        part = mine

        def add_two(info, one_ref, two_ref, out_ref):
            out_ref[...] = (one_ref[...].astype(f32) + two_ref[...].astype(f32)).astype(bf16)

        (final,) = small(add_two, [mine, other], [part], info)
        below, above = both(final, final)
        half_part = jax.ShapeDtypeStruct((mid, quarter), bf16)
        passed = small(cut, [below, above], [half_part, half_part], info)
        top, low = both(*passed)

        def finish(info, keep_ref, one_ref, two_ref, key_ref, value_ref):
            sums = keep_ref[...].astype(f32) + one_ref[...].astype(f32) + two_ref[...].astype(f32)
            sums = sums.astype(bf16)
            for h in range(local_width // HEAD):
                at = 2 * h * HEAD
                key_ref[:, h * HEAD : (h + 1) * HEAD] = sums[:, at : at + HEAD]
                value_ref[:, h * HEAD : (h + 1) * HEAD] = sums[:, at + HEAD : at + 2 * HEAD]

        shard = jax.ShapeDtypeStruct((half, local_width), bf16)
        key_weight_grad, value_weight_grad = small(finish, [keep_y, *in_y], [shard, shard], info, (passed[0],))

        def place(info, *refs):
            for ref, k in zip(refs[:-1], (0, 1, 3)):
                at = mod4(info[X] - k) * quarter
                refs[-1][:, pl.ds(pl.multiple_of(at, quarter), quarter)] = ref[...]

        whole_rows = jax.ShapeDtypeStruct((blk, width), bf16)
        (enc_grad,) = small(place, [final, below, above], [whole_rows], info, (key_weight_grad,))

        def place_last(info, top_ref, low_ref, _, out_ref):
            out_ref[:mid] = top_ref[...]
            out_ref[mid:] = low_ref[...]

        enc_grad = pl.pallas_call(
            place_last,
            grid_spec=pltpu.PrefetchScalarGridSpec(
                num_scalar_prefetch=1,
                grid=(1,),
                in_specs=[whole(half_part), whole(half_part), ANYWHERE],
                out_specs=pl.BlockSpec((blk, quarter), lambda i, info: (0, mod4(info[X] - 2))),
            ),
            out_shape=whole_rows,
            input_output_aliases={3: 0},
            compiler_params=params(8),
            cost_estimate=LIGHT,
        )(info, top, low, enc_grad)
        enc_grad = enc_grad[None]

        return (context, enc_grad, key_weight_grad[None], value_weight_grad[None])

    return shards


def solution(mesh):
    n_sec, n_dp, n_ten = (mesh.shape[name] for name in ("section", "dp", "tensor"))
    fine = Mesh(
        mesh.devices.reshape(n_sec, n_dp // 2, 2, XS, n_ten // XS), ("section", "y", "core", "x", "low")
    )
    dp, heads = ("y", "core"), ("x", "low")
    return jax.shard_map(
        make_shards(n_sec),
        mesh=fine,
        in_specs=(
            P(dp, "section", None),
            P("section", None, heads),
            P("section", None, heads),
            P("section", dp, None, heads),
            P("section", dp, None, heads),
            P(dp),
            P(dp),
        ),
        out_specs=(
            P("section", dp, None, heads),
            P(dp, "section", None),
            P("section", dp, heads),
            P("section", dp, heads),
        ),
        check_vma=False,
    )
```

```python
import jax
import jax.numpy as jnp
from jax import lax
from jax.experimental import pallas as pl
from jax.experimental.pallas import tpu as pltpu
from jax.sharding import Mesh
from jax.sharding import PartitionSpec as P

HEAD = 256
XS = 4
UNIT = 512
masked_score = -1e30
f32 = jnp.float32
bf16 = jnp.bfloat16
X, SEC, LO, Y, CORE, SRC_LIVE, TGT_LIVE = range(7)


def dot(a, b):
    return jnp.dot(a, b, preferred_element_type=f32)


def dot_t(a, b):
    return lax.dot_general(a, b, (((1,), (1,)), ((), ())), preferred_element_type=f32)


def t_dot(a, b):
    return lax.dot_general(a, b, (((0,), (0,)), ((), ())), preferred_element_type=f32)


def mod4(v):
    return lax.rem(v + 8, 4)


def params(mib):
    return pltpu.CompilerParams(vmem_limit_bytes=mib * 1024 * 1024)


def whole(a):
    return pl.BlockSpec(a.shape, lambda i, info: (0,) * a.ndim)


ANYWHERE = pl.BlockSpec(memory_space=pl.ANY)
LIGHT = pl.CostEstimate(flops=1, bytes_accessed=1, transcendentals=0)


def project(quarters, enc, wk, wv, acc, info, n_sec, after=(), queries=None):
    blk, width = enc.shape
    quarter = width // XS
    total = n_sec * blk
    cols = wk.shape[1]
    heads = cols // HEAD
    parts = [part for _, some in quarters for part in some]
    extra = ([] if acc is None else [acc]) + list(queries or ())
    n = len(quarters)

    def body(info, *refs):
        refs = list(refs)
        enc_refs = [refs.pop(0) for _ in quarters]
        part_refs = [refs.pop(0) for _ in parts]
        weight_refs = [refs.pop(0) for _ in range(2 * n)]
        acc_ref = refs.pop(0) if acc is not None else None
        rows_refs = refs[-n:]

        @pl.when(pl.program_id(0) == 0)
        def _():
            left = list(part_refs)
            for rows_ref, enc_ref, (_, some) in zip(rows_refs, enc_refs, quarters):
                rows_ref[pl.ds(pl.multiple_of(info[SEC] * blk, blk), blk), :] = enc_ref[...]
                for _, pieces in some:
                    ref = left.pop(0)
                    for at, count, block, off in pieces:
                        to = block_of(info, block, n_sec) * blk + off
                        rows_ref[pl.ds(pl.multiple_of(to, count), count), :] = ref[at : at + count, :]

        sums = [None if acc_ref is None else acc_ref[:, j * HEAD : (j + 1) * HEAD] for j in range(2)]
        for i, rows_ref in enumerate(rows_refs):
            rows = rows_ref[...]
            for j in range(2):
                term = dot(rows, weight_refs[2 * i + j][...])
                sums[j] = term if sums[j] is None else sums[j] + term
        if queries is None:
            refs[-n - 1][:, :HEAD] = sums[0]
            refs[-n - 1][:, HEAD:] = sums[1]
        else:
            k, v = (one.astype(bf16) for one in sums)
            attend(k, v, refs[0][...], refs[1][...], info, refs[-n - 2], refs[-n - 1])

    def head(rows, count):
        return pl.BlockSpec((rows, count * HEAD), lambda h, info: (0, h))

    def enc_block(m):
        return pl.BlockSpec((blk, quarter), lambda h, info: (0, mod4(info[X] - m)))

    def weight(m):
        return pl.BlockSpec((quarter, HEAD), lambda h, info: (mod4(info[X] - m), h))

    rows_out = jax.ShapeDtypeStruct((total, quarter), bf16)
    if queries is None:
        targets = 0
        out_shape, out_specs = [jax.ShapeDtypeStruct((total, 2 * cols), f32)], [head(total, 2)]
    else:
        targets = queries[0].shape[0]
        out_shape = [
            jax.ShapeDtypeStruct((targets, cols), bf16),
            jax.ShapeDtypeStruct((total, 2 * cols), bf16),
        ]
        out_specs = [head(targets, 1), head(total, 2)]
    return pl.pallas_call(
        body,
        grid_spec=pltpu.PrefetchScalarGridSpec(
            num_scalar_prefetch=1,
            grid=(heads,),
            in_specs=[enc_block(m) for m, _ in quarters]
            + [whole(p) for p, _ in parts]
            + [weight(m) for m, _ in quarters for _ in range(2)]
            + ([] if acc is None else [head(total, 2)])
            + ([] if queries is None else [head(targets, 1)] * 2)
            + [ANYWHERE] * len(after),
            out_specs=out_specs + [whole(rows_out)] * n,
        ),
        out_shape=out_shape + [rows_out] * n,
        compiler_params=params(24),
        cost_estimate=LIGHT,
    )(info, *[enc] * n, *[p for p, _ in parts], *[wk, wv] * n, *extra, *after)


def attend(k, v, q, g, info, ctx_ref, act_ref):
    scale = HEAD ** (-0.5)
    place = lax.broadcasted_iota(jnp.int32, (k.shape[0], 1), 0)
    scores = jnp.where(place < info[SRC_LIVE], dot_t(k, q), masked_score / scale)
    highest = jnp.max(scores, axis=0, keepdims=True)
    shifted = jnp.exp((scores - highest) * scale)
    weights = shifted * (1.0 / jnp.sum(shifted, axis=0, keepdims=True))
    low = weights.astype(bf16)
    target = lax.broadcasted_iota(jnp.int32, (q.shape[0], 1), 0)
    g = jnp.where(target < info[TGT_LIVE], g.astype(f32), 0.0).astype(bf16)
    prob = dot_t(v, g)
    prob_dot = jnp.sum(weights * prob, axis=0, keepdims=True)
    grad = (weights * (prob - prob_dot)).astype(bf16)
    act_ref[:, :HEAD] = (dot(grad, q) * scale).astype(bf16)
    act_ref[:, HEAD:] = dot(low, g).astype(bf16)
    ctx_ref[...] = t_dot(low, v).astype(bf16)


def block_of(info, which, n_sec):
    back = (0, 1 + 2 * info[LO], 3 - 2 * info[LO], 2)[which]
    return lax.rem(info[SEC] - back + n_sec, n_sec)


def partial_grad(act, wk, wv, info, quarters, dtype, after=(), first=None):
    total, cols = act.shape[0], wk.shape[1]
    width = wk.shape[0]
    heads = cols // HEAD
    per = width // XS // UNIT
    n = per * len(quarters)

    def unit(i, info):
        quarter = i // per
        m = quarters[0]
        for j, other in enumerate(quarters[1:]):
            m = jnp.where(quarter == j + 1, other, m)
        return mod4(info[X] - m) * per + i % per

    def body(info, act_ref, wk_ref, wv_ref, *refs):
        sums = None
        for h in range(heads):
            for j, w_ref in enumerate((wk_ref, wv_ref)):
                at = (2 * h + j) * HEAD
                term = dot_t(act_ref[:, at : at + HEAD], w_ref[:, h * HEAD : (h + 1) * HEAD])
                sums = term if sums is None else sums + term
        if first is None:
            refs[-1][...] = sums.astype(dtype)
        else:
            out_ref, up_ref, down_ref = refs[-3:]
            out_ref[...] = sums.astype(dtype)
            n_sec, blk, blocks = first
            mid = blk // 2
            for i, which in enumerate(blocks):
                at = block_of(info, which, n_sec) * blk
                up_ref[i * mid : (i + 1) * mid, :] = out_ref[pl.ds(pl.multiple_of(at, blk), mid), :]
                down_ref[i * mid : (i + 1) * mid, :] = out_ref[pl.ds(pl.multiple_of(at + mid, mid), mid), :]

    weight = pl.BlockSpec((UNIT, cols), lambda i, info: (unit(i, info), 0))
    block = pl.BlockSpec((total, UNIT), lambda i, info: (0, i))
    out_specs, out_shape = [block], [jax.ShapeDtypeStruct((total, n * UNIT), dtype)]
    if first is not None:
        rows = first[1] // 2 * len(first[2])
        out_specs += [pl.BlockSpec((rows, UNIT), lambda i, info: (0, i))] * 2
        out_shape += [jax.ShapeDtypeStruct((rows, n * UNIT), dtype)] * 2
    return pl.pallas_call(
        body,
        grid_spec=pltpu.PrefetchScalarGridSpec(
            num_scalar_prefetch=1,
            grid=(n,),
            in_specs=[whole(act), weight, weight] + [ANYWHERE] * len(after),
            out_specs=out_specs,
        ),
        out_shape=out_shape,
        compiler_params=params(12),
        cost_estimate=LIGHT,
    )(info, act, wk, wv, *after)


def pair_grads(kept, got, act, act_other, info, blocks, after=()):
    width = act.shape[1]
    half = kept.shape[1] // XS

    def body(info, kept_ref, got_ref, act_ref, other_ref, *refs):
        for ref, group in zip(refs, blocks):
            for j, at in enumerate(group):
                here = slice(at * half, (at + 1) * half)
                term = t_dot(kept_ref[:, here], act_ref[...]) + t_dot(got_ref[:, here], other_ref[...])
                ref[j * half : (j + 1) * half, :] = term.astype(bf16)

    out = [jax.ShapeDtypeStruct((len(group) * half, width), bf16) for group in blocks]
    return small(body, [kept, got, act, act_other], out, info, after)


def small(body, ins, outs, info, after=()):
    ins = [i if isinstance(i, tuple) else (i, whole(i)) for i in ins]
    n = len(ins)

    def run(info, *refs):
        body(info, *refs[:n], *refs[n + len(after) :])

    return pl.pallas_call(
        run,
        grid_spec=pltpu.PrefetchScalarGridSpec(
            num_scalar_prefetch=1,
            grid=(1,),
            in_specs=[s for _, s in ins] + [ANYWHERE] * len(after),
            out_specs=[whole(o) for o in outs],
        ),
        out_shape=[jax.ShapeDtypeStruct(o.shape, o.dtype) for o in outs],
        compiler_params=params(28),
        cost_estimate=LIGHT,
    )(info, *[a for a, _ in ins], *after)


def make_shards(n_sec):

    def shift_x(v, k):
        return lax.ppermute(v, "x", [(i, (i + k) % XS) for i in range(XS)])

    def swap_core(v):
        return lax.ppermute(v, "core", [(0, 1), (1, 0)])

    def swap_low(v):
        return lax.ppermute(v, "low", [(0, 1), (1, 0)])

    def cross(v):
        n = 2 * n_sec
        return lax.ppermute(v, ("section", "low"), [(z, (z + (1 if z % 2 else -1)) % n) for z in range(n)])

    def jump(v, k):
        n = 2 * n_sec
        return lax.ppermute(v, ("section", "low"), [(z, (z + (-2 * k if z % 2 else 2 * k)) % n) for z in range(n)])

    def shift_y(v, change=False):
        n = 2 * XS
        pairs = [(i, (i + (-2 if i % 2 else 2)) % n) for i in range(n)]
        return lax.ppermute(v, ("y", "core"), [(i, j ^ 1 if change else j) for i, j in pairs])

    def shards(enc_out, key_weight, value_weight, queries, ctx_grad, src_pad, tgt_pad):
        enc, wk, wv = enc_out[0], key_weight[0], value_weight[0]
        blk, width = enc.shape
        quarter = width // XS
        local_width = wk.shape[1]
        total_src = n_sec * blk
        x, lo, sec = lax.axis_index("x"), lax.axis_index("low"), lax.axis_index("section")
        info = jnp.stack(
            [
                x,
                sec,
                lo,
                lax.axis_index("y"),
                lax.axis_index("core"),
                total_src - src_pad[0],
                queries.shape[2] - tgt_pad[0],
            ]
        ).astype(jnp.int32)

        mine = lax.dynamic_slice(enc, (0, x * quarter), (blk, quarter))
        mid = blk // 2

        def both(up, down):
            return shift_x(up, 1), shift_x(down, -1)

        def with_halves(block, ups, downs, after=()):
            out = jax.ShapeDtypeStruct((blk + mid * len(ups), quarter), bf16)

            def body(info, block_ref, *refs):
                up_out, down_out = refs[-2:]
                up_out[:blk] = block_ref[...]
                down_out[:blk] = block_ref[...]
                for i in range(len(ups)):
                    at = blk + i * mid
                    up_out[at : at + mid] = refs[i][:mid]
                    down_out[at : at + mid] = refs[len(ups) + i][mid:blk]

            return small(body, [block, *ups, *downs], [out, out], info, after)

        b1, b2 = cross(mine), jump(mine, -1)
        u1, d1 = both(b1, b1)
        u2, d2 = both(b2, b2)
        b3 = cross(b2)
        out3 = with_halves(b3, (u1, u2), (d1, d2))
        u3, d3 = both(*out3)
        rows = [None] * XS

        def parts(*got):
            return [(g, [(0, blk, i + 1, 0)]) for i, g in enumerate(got)]

        acc, rows[0] = project([(0, parts(b1, b2, b3))], enc, wk, wv, None, info, n_sec, out3)

        def cut(info, up_ref, down_ref, up_out, down_out):
            up_out[...] = up_ref[:mid]
            down_out[...] = down_ref[mid:blk]

        out4 = small(cut, [u3, d3], [jax.ShapeDtypeStruct((mid, quarter), bf16)] * 2, info, (acc,))
        u4, d4 = both(*out4)
        beside = [(1, parts(u1, u2, u3)), (3, parts(d1, d2, d3))]
        acc, rows[1], rows[3] = project(beside, enc, wk, wv, acc, info, n_sec, out4)
        last = [(u3, [(blk, mid, 1, 0), (blk + mid, mid, 2, 0)]), (d3, [(blk, mid, 1, mid), (blk + mid, mid, 2, mid)])]
        last += [(u4, [(0, mid, 3, 0)]), (d4, [(0, mid, 3, mid)])]
        asked = (queries[0, 0], ctx_grad[0, 0])
        context, act, rows[2] = project([(2, last)], enc, wk, wv, acc, info, n_sec, queries=asked)
        context = context[None, None]
        act_other = swap_core(act)

        half = quarter // 2

        def pack(own, after=()):
            def body(info, *refs):
                side = info[CORE] if own else 1 - info[CORE]
                for m, ref in enumerate(refs[:-1]):
                    step = mod4(info[X] - info[Y] - m)

                    @pl.when(step == 1 + 2 * side)
                    def _():
                        refs[-1][:, :quarter] = ref[...]

                    for place, at in ((2, quarter), (0, quarter + half)):

                        @pl.when(step == place)
                        def _():
                            refs[-1][:, at : at + half] = ref[:, pl.ds(pl.multiple_of(side * half, half), half)]

            return small(body, rows, [jax.ShapeDtypeStruct((total_src, 2 * quarter), bf16)], info, after)[0]

        sent = pack(False)
        got = swap_core(sent)

        far, up, down = partial_grad(act, wk, wv, info, (2,), bf16, first=(n_sec, blk, (3, 0, 2)))
        halves = both(up, down)
        (near,) = partial_grad(act, wk, wv, info, (3, 1), bf16, (far,))
        kept = pack(True, (near,))
        (far_y,) = pair_grads(kept, got, act, act_other, info, [(2,)], (near,))
        (keep,) = partial_grad(act, wk, wv, info, (0,), f32, (near,))

        def rows_of(v, which):
            return v, pl.BlockSpec((blk, v.shape[1]), lambda i, info: (block_of(info, which, n_sec), 0))

        def stage(done, sent, ahead, after=(), through=()):
            ins, outs = [], []
            for which, (up, down), _, more in done:
                ins += [rows_of(keep, which), up, down, *more]
                outs.append(jax.ShapeDtypeStruct((blk, quarter), bf16))
            for which, (up, down), _ in sent:
                ins += [rows_of(near, which), up, down]
            ins += [rows_of(far, which) for which in ahead] + list(through)
            size = blk * len(sent) + mid * len(ahead)
            outs += [jax.ShapeDtypeStruct((size, quarter), bf16)] * (2 if size else 0) + list(through)

            def body(info, *refs):
                refs, out_refs = list(refs[: len(ins)]), list(refs[len(ins) :])
                for _, _, at, more in done:
                    sums = refs.pop(0)[...]
                    for _ in range(2):
                        sums = sums + refs.pop(0)[at : at + blk].astype(f32)
                    for _ in more:
                        sums = sums + refs.pop(0)[...].astype(f32)
                    out_refs.pop(0)[...] = sums.astype(bf16)
                to = 0
                if size:
                    up_out, down_out = out_refs.pop(0), out_refs.pop(0)
                for _, _, at in sent:
                    near_ref, up_ref, down_ref = (refs.pop(0) for _ in range(3))
                    half_up, half_down = up_ref[at : at + mid].astype(f32), down_ref[at : at + mid].astype(f32)
                    up_out[to : to + mid] = (near_ref[:mid, :quarter].astype(f32) + half_up).astype(bf16)
                    up_out[to + mid : to + blk] = near_ref[mid:, :quarter]
                    down_out[to : to + mid] = near_ref[:mid, quarter:]
                    down_out[to + mid : to + blk] = (near_ref[mid:, quarter:].astype(f32) + half_down).astype(bf16)
                    to += blk
                for _ in ahead:
                    far_ref = refs.pop(0)
                    up_out[to : to + mid] = far_ref[:mid]
                    down_out[to : to + mid] = far_ref[mid:]
                    to += mid
                for ref, out_ref in zip(refs, out_refs):
                    out_ref[...] = ref[...]

            return small(body, ins, outs, info, after)

        up, down, far_y = stage([], [(3, halves, 0)], [1], through=[far_y])
        got_y = shift_y(far_y)
        near_y, keep_y = pair_grads(kept, got, act, act_other, info, [(0, 1), (3,)], (up,))
        side = both(up, down)
        total3, up, down = stage([(3, side, 0, [])], [(2, halves, 2 * mid), (1, side, blk)], [])
        carried = cross(total3)
        side = both(up, down)
        total2, total1, up, down = stage([(2, side, 0, [carried]), (1, side, blk, [])], [(0, halves, mid)], [])

        def add_y(info, near_ref, got_ref, same_ref, other_ref):
            here = pl.ds(pl.multiple_of(info[CORE] * half, half), half)
            there = pl.ds(pl.multiple_of((1 - info[CORE]) * half, half), half)
            same_ref[...] = (near_ref[here, :].astype(f32) + got_ref[...].astype(f32)).astype(bf16)
            other_ref[...] = near_ref[there, :]

        same_y, other_y = small(add_y, [near_y, got_y], [keep_y, keep_y], info, (total1,))
        same_y = shift_y(same_y)
        carried = [jump(total2, 1), cross(total1)]
        side = both(up, down)
        mine, other_y = stage([(0, side, 0, carried)], [], [], through=[other_y])
        in_y = same_y, shift_y(other_y, True)
        other = swap_low(mine)
        part = mine

        def add_two(info, one_ref, two_ref, out_ref, top_ref):
            out_ref[...] = (one_ref[...].astype(f32) + two_ref[...].astype(f32)).astype(bf16)
            top_ref[...] = out_ref[:mid]

        half_part = jax.ShapeDtypeStruct((mid, quarter), bf16)
        final, top = small(add_two, [mine, other], [part, half_part], info)
        below, above = both(final, final)
        far_top = shift_x(top, 2)

        def cut_low(info, in_ref, out_ref):
            out_ref[...] = in_ref[mid:]

        (low,) = small(cut_low, [above], [half_part], info)
        far_low = shift_x(low, -1)

        def finish(info, keep_ref, one_ref, two_ref, key_ref, value_ref, end_ref):
            end_ref[...] = jnp.zeros_like(end_ref)
            sums = keep_ref[...].astype(f32) + one_ref[...].astype(f32) + two_ref[...].astype(f32)
            sums = sums.astype(bf16)
            for h in range(local_width // HEAD):
                at = 2 * h * HEAD
                key_ref[:, h * HEAD : (h + 1) * HEAD] = sums[:, at : at + HEAD]
                value_ref[:, h * HEAD : (h + 1) * HEAD] = sums[:, at + HEAD : at + 2 * HEAD]

        shard = jax.ShapeDtypeStruct((half, local_width), bf16)
        end = jax.ShapeDtypeStruct((16, 128), bf16)
        key_weight_grad, value_weight_grad, end = small(finish, [keep_y, *in_y], [shard, shard, end], info, (low,))

        def place(info, *refs):
            for ref, k in zip(refs[:-1], (0, 1, 3)):
                at = mod4(info[X] - k) * quarter
                refs[-1][:, pl.ds(pl.multiple_of(at, quarter), quarter)] = ref[...]

        whole_rows = jax.ShapeDtypeStruct((blk, width), bf16)
        (enc_grad,) = small(place, [final, below, above], [whole_rows], info, (low,))

        def place_last(info, top_ref, low_ref, _, __, out_ref):
            out_ref[:mid] = top_ref[...]
            out_ref[mid:] = low_ref[...]

        enc_grad = pl.pallas_call(
            place_last,
            grid_spec=pltpu.PrefetchScalarGridSpec(
                num_scalar_prefetch=1,
                grid=(1,),
                in_specs=[whole(half_part), whole(half_part), ANYWHERE, ANYWHERE],
                out_specs=pl.BlockSpec((blk, quarter), lambda i, info: (0, mod4(info[X] - 2))),
            ),
            out_shape=whole_rows,
            input_output_aliases={3: 0},
            compiler_params=params(8),
            cost_estimate=LIGHT,
        )(info, far_top, far_low, enc_grad, end)
        enc_grad = enc_grad[None]

        return (context, enc_grad, key_weight_grad[None], value_weight_grad[None])

    return shards


def solution(mesh):
    n_sec, n_dp, n_ten = (mesh.shape[name] for name in ("section", "dp", "tensor"))
    fine = Mesh(
        mesh.devices.reshape(n_sec, n_dp // 2, 2, XS, n_ten // XS), ("section", "y", "core", "x", "low")
    )
    dp, heads = ("y", "core"), ("x", "low")
    return jax.shard_map(
        make_shards(n_sec),
        mesh=fine,
        in_specs=(
            P(dp, "section", None),
            P("section", None, heads),
            P("section", None, heads),
            P("section", dp, None, heads),
            P("section", dp, None, heads),
            P(dp),
            P(dp),
        ),
        out_specs=(
            P("section", dp, None, heads),
            P(dp, "section", None),
            P("section", dp, heads),
            P("section", dp, heads),
        ),
        check_vma=False,
    )
```

```python
import jax
import jax.numpy as jnp
from jax import lax
from jax.experimental import pallas as pl
from jax.experimental.pallas import tpu as pltpu
from jax.sharding import Mesh
from jax.sharding import PartitionSpec as P

HEAD = 256
XS = 4
UNIT = 512
masked_score = -1e30
f32 = jnp.float32
bf16 = jnp.bfloat16
X, SEC, LO, Y, CORE, SRC_LIVE, TGT_LIVE = range(7)


def dot(a, b):
    return jnp.dot(a, b, preferred_element_type=f32)


def dot_t(a, b):
    return lax.dot_general(a, b, (((1,), (1,)), ((), ())), preferred_element_type=f32)


def t_dot(a, b):
    return lax.dot_general(a, b, (((0,), (0,)), ((), ())), preferred_element_type=f32)


def mod4(v):
    return lax.rem(v + 8, 4)


def params(mib):
    return pltpu.CompilerParams(vmem_limit_bytes=mib * 1024 * 1024)


def whole(a):
    return pl.BlockSpec(a.shape, lambda i, info: (0,) * a.ndim)


ANYWHERE = pl.BlockSpec(memory_space=pl.ANY)
LIGHT = pl.CostEstimate(flops=1, bytes_accessed=1, transcendentals=0)


def project(quarters, enc, wk, wv, acc, info, n_sec, after=(), queries=None, first=None):
    blk, width = enc.shape
    quarter = width // XS
    total = n_sec * blk
    cols = wk.shape[1]
    heads = cols // HEAD
    parts = [part for _, some in quarters for part in some]
    extra = ([] if acc is None else [acc]) + list(queries or ())
    n = len(quarters)

    def body(info, *refs):
        refs = list(refs)
        enc_refs = [refs.pop(0) for _ in quarters]
        part_refs = [refs.pop(0) for _ in parts]
        weight_refs = [refs.pop(0) for _ in range(2 * n)]
        acc_ref = refs.pop(0) if acc is not None else None
        step = pl.program_id(0)
        if queries is not None:
            far_refs = refs[-3:]
            del refs[-3:]
        rows_refs = refs[-n:]

        @pl.when(step == 0)
        def _():
            left = list(part_refs)
            for rows_ref, enc_ref, (_, some) in zip(rows_refs, enc_refs, quarters):
                rows_ref[pl.ds(pl.multiple_of(info[SEC] * blk, blk), blk), :] = enc_ref[...]
                for _, pieces in some:
                    ref = left.pop(0)
                    for at, count, block, off in pieces:
                        to = block_of(info, block, n_sec) * blk + off
                        rows_ref[pl.ds(pl.multiple_of(to, count), count), :] = ref[at : at + count, :]

        def head_sums():
            sums = [None if acc_ref is None else acc_ref[:, j * HEAD : (j + 1) * HEAD] for j in range(2)]
            for i, rows_ref in enumerate(rows_refs):
                rows = rows_ref[...]
                for j in range(2):
                    term = dot(rows, weight_refs[2 * i + j][...])
                    sums[j] = term if sums[j] is None else sums[j] + term
            return sums

        if queries is None:
            sums = head_sums()
            refs[-n - 1][:, :HEAD] = sums[0]
            refs[-n - 1][:, HEAD:] = sums[1]
            return
        q_ref, g_ref, wk_ref, wv_ref = refs[:4]
        ctx_ref, act_ref = refs[-n - 2], refs[-n - 1]

        @pl.when(step < heads)
        def _():
            k, v = (one.astype(bf16) for one in head_sums())
            at = pl.multiple_of(step * 2 * HEAD, 2 * HEAD)
            here = act_ref.at[:, pl.ds(at, 2 * HEAD)]
            attend(k, v, q_ref[...], g_ref[...], info, ctx_ref, here)

        @pl.when(step >= heads)
        def _():
            far_terms(act_ref, wk_ref, wv_ref, info, (n_sec, blk, first), *far_refs)

    def head(rows, count):
        return pl.BlockSpec((rows, count * HEAD), lambda h, info: (0, jnp.minimum(h, heads - 1)))

    def enc_block(m):
        return pl.BlockSpec((blk, quarter), lambda h, info: (0, mod4(info[X] - m)))

    def weight(m):
        return pl.BlockSpec((quarter, HEAD), lambda h, info: (mod4(info[X] - m), jnp.minimum(h, heads - 1)))

    rows_out = jax.ShapeDtypeStruct((total, quarter), bf16)
    if queries is None:
        far_shape, far_specs = [], []
        targets = 0
        out_shape, out_specs = [jax.ShapeDtypeStruct((total, 2 * cols), f32)], [head(total, 2)]
    else:
        targets = queries[0].shape[0]
        act_out = jax.ShapeDtypeStruct((total, 2 * cols), bf16)
        out_shape, out_specs = [jax.ShapeDtypeStruct((targets, cols), bf16), act_out], [head(targets, 1), whole(act_out)]
        per = quarter // UNIT

        def unit(h):
            return jnp.maximum(h - heads, 0)

        far_weight = pl.BlockSpec((UNIT, cols), lambda h, info: (mod4(info[X] - 2) * per + unit(h), 0))
        far_rows = (total, blk // 2 * len(first), blk // 2 * len(first))
        far_shape = [jax.ShapeDtypeStruct((r, quarter), bf16) for r in far_rows]
        far_specs = [pl.BlockSpec((r, UNIT), lambda h, info: (0, unit(h))) for r in far_rows]
        extra += [wk, wv]
    return pl.pallas_call(
        body,
        grid_spec=pltpu.PrefetchScalarGridSpec(
            num_scalar_prefetch=1,
            grid=(heads if queries is None else heads + per,),
            in_specs=[enc_block(m) for m, _ in quarters]
            + [whole(p) for p, _ in parts]
            + [weight(m) for m, _ in quarters for _ in range(2)]
            + ([] if acc is None else [head(total, 2)])
            + ([] if queries is None else [head(targets, 1)] * 2 + [far_weight] * 2)
            + [ANYWHERE] * len(after),
            out_specs=out_specs + [whole(rows_out)] * n + far_specs,
        ),
        out_shape=out_shape + [rows_out] * n + far_shape,
        compiler_params=params(28),
        cost_estimate=LIGHT,
    )(info, *[enc] * n, *[p for p, _ in parts], *[wk, wv] * n, *extra, *after)


def attend(k, v, q, g, info, ctx_ref, act_ref):
    scale = HEAD ** (-0.5)
    place = lax.broadcasted_iota(jnp.int32, (k.shape[0], 1), 0)
    scores = jnp.where(place < info[SRC_LIVE], dot_t(k, q), masked_score / scale)
    highest = jnp.max(scores, axis=0, keepdims=True)
    shifted = jnp.exp((scores - highest) * scale)
    weights = shifted * (1.0 / jnp.sum(shifted, axis=0, keepdims=True))
    low = weights.astype(bf16)
    target = lax.broadcasted_iota(jnp.int32, (q.shape[0], 1), 0)
    g = jnp.where(target < info[TGT_LIVE], g.astype(f32), 0.0).astype(bf16)
    prob = dot_t(v, g)
    prob_dot = jnp.sum(weights * prob, axis=0, keepdims=True)
    grad = (weights * (prob - prob_dot)).astype(bf16)
    act_ref[:, :HEAD] = (dot(grad, q) * scale).astype(bf16)
    act_ref[:, HEAD:] = dot(low, g).astype(bf16)
    ctx_ref[...] = t_dot(low, v).astype(bf16)


def block_of(info, which, n_sec):
    back = (0, 1 + 2 * info[LO], 3 - 2 * info[LO], 2)[which]
    return lax.rem(info[SEC] - back + n_sec, n_sec)


def transposed(act_ref, wk_ref, wv_ref):
    sums = None
    for h in range(wk_ref.shape[1] // HEAD):
        for j, w_ref in enumerate((wk_ref, wv_ref)):
            at = (2 * h + j) * HEAD
            term = dot_t(act_ref[:, at : at + HEAD], w_ref[:, h * HEAD : (h + 1) * HEAD])
            sums = term if sums is None else sums + term
    return sums


def far_terms(act_ref, wk_ref, wv_ref, info, first, out_ref, up_ref, down_ref):
    out_ref[...] = transposed(act_ref, wk_ref, wv_ref).astype(out_ref.dtype)
    n_sec, blk, blocks = first
    mid = blk // 2
    for i, which in enumerate(blocks):
        at = block_of(info, which, n_sec) * blk
        up_ref[i * mid : (i + 1) * mid, :] = out_ref[pl.ds(pl.multiple_of(at, blk), mid), :]
        down_ref[i * mid : (i + 1) * mid, :] = out_ref[pl.ds(pl.multiple_of(at + mid, mid), mid), :]


def partial_grad(act, wk, wv, info, quarters, dtype, after=()):
    total, cols = act.shape[0], wk.shape[1]
    width = wk.shape[0]
    per = width // XS // UNIT
    n = per * len(quarters)

    def unit(i, info):
        quarter = i // per
        m = quarters[0]
        for j, other in enumerate(quarters[1:]):
            m = jnp.where(quarter == j + 1, other, m)
        return mod4(info[X] - m) * per + i % per

    def body(info, act_ref, wk_ref, wv_ref, *refs):
        refs[-1][...] = transposed(act_ref, wk_ref, wv_ref).astype(dtype)

    weight = pl.BlockSpec((UNIT, cols), lambda i, info: (unit(i, info), 0))
    block = pl.BlockSpec((total, UNIT), lambda i, info: (0, i))
    out_specs, out_shape = [block], [jax.ShapeDtypeStruct((total, n * UNIT), dtype)]
    return pl.pallas_call(
        body,
        grid_spec=pltpu.PrefetchScalarGridSpec(
            num_scalar_prefetch=1,
            grid=(n,),
            in_specs=[whole(act), weight, weight] + [ANYWHERE] * len(after),
            out_specs=out_specs,
        ),
        out_shape=out_shape,
        compiler_params=params(12),
        cost_estimate=LIGHT,
    )(info, act, wk, wv, *after)


def pair_grads(kept, got, act, act_other, info, blocks, after=()):
    width = act.shape[1]
    half = kept.shape[1] // XS

    def body(info, kept_ref, got_ref, act_ref, other_ref, *refs):
        for ref, group in zip(refs, blocks):
            for j, at in enumerate(group):
                here = slice(at * half, (at + 1) * half)
                term = t_dot(kept_ref[:, here], act_ref[...]) + t_dot(got_ref[:, here], other_ref[...])
                ref[j * half : (j + 1) * half, :] = term.astype(bf16)

    out = [jax.ShapeDtypeStruct((len(group) * half, width), bf16) for group in blocks]
    return small(body, [kept, got, act, act_other], out, info, after)


def small(body, ins, outs, info, after=()):
    ins = [i if isinstance(i, tuple) else (i, whole(i)) for i in ins]
    n = len(ins)

    def run(info, *refs):
        body(info, *refs[:n], *refs[n + len(after) :])

    return pl.pallas_call(
        run,
        grid_spec=pltpu.PrefetchScalarGridSpec(
            num_scalar_prefetch=1,
            grid=(1,),
            in_specs=[s for _, s in ins] + [ANYWHERE] * len(after),
            out_specs=[whole(o) for o in outs],
        ),
        out_shape=[jax.ShapeDtypeStruct(o.shape, o.dtype) for o in outs],
        compiler_params=params(28),
        cost_estimate=LIGHT,
    )(info, *[a for a, _ in ins], *after)


def make_shards(n_sec):

    def shift_x(v, k):
        return lax.ppermute(v, "x", [(i, (i + k) % XS) for i in range(XS)])

    def swap_core(v):
        return lax.ppermute(v, "core", [(0, 1), (1, 0)])

    def swap_low(v):
        return lax.ppermute(v, "low", [(0, 1), (1, 0)])

    def cross(v):
        n = 2 * n_sec
        return lax.ppermute(v, ("section", "low"), [(z, (z + (1 if z % 2 else -1)) % n) for z in range(n)])

    def jump(v, k):
        n = 2 * n_sec
        return lax.ppermute(v, ("section", "low"), [(z, (z + (-2 * k if z % 2 else 2 * k)) % n) for z in range(n)])

    def shift_y(v, change=False):
        n = 2 * XS
        pairs = [(i, (i + (-2 if i % 2 else 2)) % n) for i in range(n)]
        return lax.ppermute(v, ("y", "core"), [(i, j ^ 1 if change else j) for i, j in pairs])

    def shards(enc_out, key_weight, value_weight, queries, ctx_grad, src_pad, tgt_pad):
        enc, wk, wv = enc_out[0], key_weight[0], value_weight[0]
        blk, width = enc.shape
        quarter = width // XS
        local_width = wk.shape[1]
        total_src = n_sec * blk
        x, lo, sec = lax.axis_index("x"), lax.axis_index("low"), lax.axis_index("section")
        info = jnp.stack(
            [
                x,
                sec,
                lo,
                lax.axis_index("y"),
                lax.axis_index("core"),
                total_src - src_pad[0],
                queries.shape[2] - tgt_pad[0],
            ]
        ).astype(jnp.int32)

        mine = lax.dynamic_slice(enc, (0, x * quarter), (blk, quarter))
        mid = blk // 2

        def both(up, down):
            return shift_x(up, 1), shift_x(down, -1)

        def with_halves(block, ups, downs, after=()):
            out = jax.ShapeDtypeStruct((blk + mid * len(ups), quarter), bf16)

            def body(info, block_ref, *refs):
                up_out, down_out = refs[-2:]
                up_out[:blk] = block_ref[...]
                down_out[:blk] = block_ref[...]
                for i in range(len(ups)):
                    at = blk + i * mid
                    up_out[at : at + mid] = refs[i][:mid]
                    down_out[at : at + mid] = refs[len(ups) + i][mid:blk]

            return small(body, [block, *ups, *downs], [out, out], info, after)

        b1, b2 = cross(mine), jump(mine, -1)
        u1, d1 = both(b1, b1)
        u2, d2 = both(b2, b2)
        b3 = cross(b2)
        out3 = with_halves(b3, (u1, u2), (d1, d2))
        u3, d3 = both(*out3)
        rows = [None] * XS

        def parts(*got):
            return [(g, [(0, blk, i + 1, 0)]) for i, g in enumerate(got)]

        acc, rows[0] = project([(0, parts(b1, b2, b3))], enc, wk, wv, None, info, n_sec, out3)

        def cut(info, up_ref, down_ref, up_out, down_out):
            up_out[...] = up_ref[:mid]
            down_out[...] = down_ref[mid:blk]

        out4 = small(cut, [u3, d3], [jax.ShapeDtypeStruct((mid, quarter), bf16)] * 2, info, (acc,))
        u4, d4 = both(*out4)
        beside = [(1, parts(u1, u2, u3)), (3, parts(d1, d2, d3))]
        acc, rows[1], rows[3] = project(beside, enc, wk, wv, acc, info, n_sec, out4)
        last = [(u3, [(blk, mid, 1, 0), (blk + mid, mid, 2, 0)]), (d3, [(blk, mid, 1, mid), (blk + mid, mid, 2, mid)])]
        last += [(u4, [(0, mid, 3, 0)]), (d4, [(0, mid, 3, mid)])]
        asked = (queries[0, 0], ctx_grad[0, 0])
        first = (3, 0, 2)
        context, act, rows[2], far, up, down = project(
            [(2, last)], enc, wk, wv, acc, info, n_sec, queries=asked, first=first
        )
        context = context[None, None]
        act_other = swap_core(act)

        half = quarter // 2

        def pack(own, after=()):
            def body(info, *refs):
                side = info[CORE] if own else 1 - info[CORE]
                for m, ref in enumerate(refs[:-1]):
                    step = mod4(info[X] - info[Y] - m)

                    @pl.when(step == 1 + 2 * side)
                    def _():
                        refs[-1][:, :quarter] = ref[...]

                    for place, at in ((2, quarter), (0, quarter + half)):

                        @pl.when(step == place)
                        def _():
                            refs[-1][:, at : at + half] = ref[:, pl.ds(pl.multiple_of(side * half, half), half)]

            return small(body, rows, [jax.ShapeDtypeStruct((total_src, 2 * quarter), bf16)], info, after)[0]

        sent = pack(False)
        got = swap_core(sent)

        halves = both(up, down)
        (near,) = partial_grad(act, wk, wv, info, (3, 1), bf16, (far,))
        kept = pack(True, (near,))
        (far_y,) = pair_grads(kept, got, act, act_other, info, [(2,)], (near,))
        (keep,) = partial_grad(act, wk, wv, info, (0,), f32, (near,))

        def rows_of(v, which):
            return v, pl.BlockSpec((blk, v.shape[1]), lambda i, info: (block_of(info, which, n_sec), 0))

        def stage(done, sent, ahead, after=(), through=()):
            ins, outs = [], []
            for which, (up, down), _, more in done:
                ins += [rows_of(keep, which), up, down, *more]
                outs.append(jax.ShapeDtypeStruct((blk, quarter), bf16))
            for which, (up, down), _ in sent:
                ins += [rows_of(near, which), up, down]
            ins += [rows_of(far, which) for which in ahead] + list(through)
            size = blk * len(sent) + mid * len(ahead)
            outs += [jax.ShapeDtypeStruct((size, quarter), bf16)] * (2 if size else 0) + list(through)

            def body(info, *refs):
                refs, out_refs = list(refs[: len(ins)]), list(refs[len(ins) :])
                for _, _, at, more in done:
                    sums = refs.pop(0)[...]
                    for _ in range(2):
                        sums = sums + refs.pop(0)[at : at + blk].astype(f32)
                    for _ in more:
                        sums = sums + refs.pop(0)[...].astype(f32)
                    out_refs.pop(0)[...] = sums.astype(bf16)
                to = 0
                if size:
                    up_out, down_out = out_refs.pop(0), out_refs.pop(0)
                for _, _, at in sent:
                    near_ref, up_ref, down_ref = (refs.pop(0) for _ in range(3))
                    half_up, half_down = up_ref[at : at + mid].astype(f32), down_ref[at : at + mid].astype(f32)
                    up_out[to : to + mid] = (near_ref[:mid, :quarter].astype(f32) + half_up).astype(bf16)
                    up_out[to + mid : to + blk] = near_ref[mid:, :quarter]
                    down_out[to : to + mid] = near_ref[:mid, quarter:]
                    down_out[to + mid : to + blk] = (near_ref[mid:, quarter:].astype(f32) + half_down).astype(bf16)
                    to += blk
                for _ in ahead:
                    far_ref = refs.pop(0)
                    up_out[to : to + mid] = far_ref[:mid]
                    down_out[to : to + mid] = far_ref[mid:]
                    to += mid
                for ref, out_ref in zip(refs, out_refs):
                    out_ref[...] = ref[...]

            return small(body, ins, outs, info, after)

        up, down, far_y = stage([], [(3, halves, 0)], [1], through=[far_y])
        got_y = shift_y(far_y)
        near_y, keep_y = pair_grads(kept, got, act, act_other, info, [(0, 1), (3,)], (up,))
        side = both(up, down)
        total3, up, down = stage([(3, side, 0, [])], [(2, halves, 2 * mid), (1, side, blk)], [])
        carried = cross(total3)
        side = both(up, down)
        total2, total1, up, down = stage([(2, side, 0, [carried]), (1, side, blk, [])], [(0, halves, mid)], [])

        def add_y(info, near_ref, got_ref, same_ref, other_ref):
            here = pl.ds(pl.multiple_of(info[CORE] * half, half), half)
            there = pl.ds(pl.multiple_of((1 - info[CORE]) * half, half), half)
            same_ref[...] = (near_ref[here, :].astype(f32) + got_ref[...].astype(f32)).astype(bf16)
            other_ref[...] = near_ref[there, :]

        same_y, other_y = small(add_y, [near_y, got_y], [keep_y, keep_y], info, (total1,))
        same_y = shift_y(same_y)
        carried = [jump(total2, 1), cross(total1)]
        side = both(up, down)
        mine, other_y = stage([(0, side, 0, carried)], [], [], through=[other_y])
        in_y = same_y, shift_y(other_y, True)
        other = swap_low(mine)
        part = mine

        def add_two(info, one_ref, two_ref, out_ref, top_ref):
            out_ref[...] = (one_ref[...].astype(f32) + two_ref[...].astype(f32)).astype(bf16)
            top_ref[...] = out_ref[:mid]

        half_part = jax.ShapeDtypeStruct((mid, quarter), bf16)
        final, top = small(add_two, [mine, other], [part, half_part], info)
        below, above = both(final, final)
        far_top = shift_x(top, 2)

        def cut_low(info, in_ref, out_ref):
            out_ref[...] = in_ref[mid:]

        (low,) = small(cut_low, [above], [half_part], info)
        far_low = shift_x(low, -1)

        def finish(info, keep_ref, one_ref, two_ref, key_ref, value_ref, end_ref):
            end_ref[...] = jnp.zeros_like(end_ref)
            sums = keep_ref[...].astype(f32) + one_ref[...].astype(f32) + two_ref[...].astype(f32)
            sums = sums.astype(bf16)
            for h in range(local_width // HEAD):
                at = 2 * h * HEAD
                key_ref[:, h * HEAD : (h + 1) * HEAD] = sums[:, at : at + HEAD]
                value_ref[:, h * HEAD : (h + 1) * HEAD] = sums[:, at + HEAD : at + 2 * HEAD]

        shard = jax.ShapeDtypeStruct((half, local_width), bf16)
        end = jax.ShapeDtypeStruct((16, 128), bf16)
        key_weight_grad, value_weight_grad, end = small(finish, [keep_y, *in_y], [shard, shard, end], info, (low,))

        def place(info, *refs):
            for ref, k in zip(refs[:-1], (0, 1, 3)):
                at = mod4(info[X] - k) * quarter
                refs[-1][:, pl.ds(pl.multiple_of(at, quarter), quarter)] = ref[...]

        whole_rows = jax.ShapeDtypeStruct((blk, width), bf16)
        (enc_grad,) = small(place, [final, below, above], [whole_rows], info, (low,))

        def place_last(info, top_ref, low_ref, _, __, out_ref):
            out_ref[:mid] = top_ref[...]
            out_ref[mid:] = low_ref[...]

        enc_grad = pl.pallas_call(
            place_last,
            grid_spec=pltpu.PrefetchScalarGridSpec(
                num_scalar_prefetch=1,
                grid=(1,),
                in_specs=[whole(half_part), whole(half_part), ANYWHERE, ANYWHERE],
                out_specs=pl.BlockSpec((blk, quarter), lambda i, info: (0, mod4(info[X] - 2))),
            ),
            out_shape=whole_rows,
            input_output_aliases={3: 0},
            compiler_params=params(8),
            cost_estimate=LIGHT,
        )(info, far_top, far_low, enc_grad, end)
        enc_grad = enc_grad[None]

        return (context, enc_grad, key_weight_grad[None], value_weight_grad[None])

    return shards


def solution(mesh):
    n_sec, n_dp, n_ten = (mesh.shape[name] for name in ("section", "dp", "tensor"))
    fine = Mesh(
        mesh.devices.reshape(n_sec, n_dp // 2, 2, XS, n_ten // XS), ("section", "y", "core", "x", "low")
    )
    dp, heads = ("y", "core"), ("x", "low")
    return jax.shard_map(
        make_shards(n_sec),
        mesh=fine,
        in_specs=(
            P(dp, "section", None),
            P("section", None, heads),
            P("section", None, heads),
            P("section", dp, None, heads),
            P("section", dp, None, heads),
            P(dp),
            P(dp),
        ),
        out_specs=(
            P("section", dp, None, heads),
            P(dp, "section", None),
            P("section", dp, heads),
            P("section", dp, heads),
        ),
        check_vma=False,
    )
```

```python
import jax
import jax.numpy as jnp
from jax import lax
from jax.experimental import pallas as pl
from jax.experimental.pallas import tpu as pltpu
from jax.sharding import Mesh
from jax.sharding import PartitionSpec as P

HEAD = 256
XS = 4
UNIT = 512
masked_score = -1e30
f32 = jnp.float32
bf16 = jnp.bfloat16
X, SEC, LO, Y, CORE, SRC_LIVE, TGT_LIVE = range(7)


def dot(a, b):
    return jnp.dot(a, b, preferred_element_type=f32)


def dot_t(a, b):
    return lax.dot_general(a, b, (((1,), (1,)), ((), ())), preferred_element_type=f32)


def t_dot(a, b):
    return lax.dot_general(a, b, (((0,), (0,)), ((), ())), preferred_element_type=f32)


def mod4(v):
    return lax.rem(v + 8, 4)


def params(mib):
    return pltpu.CompilerParams(vmem_limit_bytes=mib * 1024 * 1024)


def whole(a):
    return pl.BlockSpec(a.shape, lambda i, info: (0,) * a.ndim)


ANYWHERE = pl.BlockSpec(memory_space=pl.ANY)
LIGHT = pl.CostEstimate(flops=1, bytes_accessed=1, transcendentals=0)


def project(quarters, enc, wk, wv, acc, info, n_sec, after=(), queries=None, first=None):
    blk, width = enc.shape
    quarter = width // XS
    total = n_sec * blk
    cols = wk.shape[1]
    heads = cols // HEAD
    parts = [part for _, some in quarters for part in some]
    extra = ([] if acc is None else [acc]) + list(queries or ())
    n = len(quarters)

    def body(info, *refs):
        refs = list(refs)
        enc_refs = [refs.pop(0) for _ in quarters]
        part_refs = [refs.pop(0) for _ in parts]
        weight_refs = [refs.pop(0) for _ in range(2 * n)]
        acc_ref = refs.pop(0) if acc is not None else None
        step = pl.program_id(0)
        if queries is not None:
            far_refs = refs[-3:]
            del refs[-3:]
        rows_refs = refs[-n:]

        @pl.when(step == 0)
        def _():
            left = list(part_refs)
            for rows_ref, enc_ref, (_, some) in zip(rows_refs, enc_refs, quarters):
                rows_ref[pl.ds(pl.multiple_of(info[SEC] * blk, blk), blk), :] = enc_ref[...]
                for _, pieces in some:
                    ref = left.pop(0)
                    for at, count, block, off in pieces:
                        to = block_of(info, block, n_sec) * blk + off
                        rows_ref[pl.ds(pl.multiple_of(to, count), count), :] = ref[at : at + count, :]

        def head_sums():
            sums = [None if acc_ref is None else acc_ref[:, j * HEAD : (j + 1) * HEAD] for j in range(2)]
            for i, rows_ref in enumerate(rows_refs):
                rows = rows_ref[...]
                for j in range(2):
                    term = dot(rows, weight_refs[2 * i + j][...])
                    sums[j] = term if sums[j] is None else sums[j] + term
            return sums

        if queries is None:
            sums = head_sums()
            refs[-n - 1][:, :HEAD] = sums[0]
            refs[-n - 1][:, HEAD:] = sums[1]
            return
        q_ref, g_ref, wk_ref, wv_ref = refs[:4]
        ctx_ref, act_ref = refs[-n - 2], refs[-n - 1]

        @pl.when(step < heads)
        def _():
            k, v = (one.astype(bf16) for one in head_sums())
            at = pl.multiple_of(step * 2 * HEAD, 2 * HEAD)
            here = act_ref.at[:, pl.ds(at, 2 * HEAD)]
            attend(k, v, q_ref[...], g_ref[...], info, ctx_ref, here)

        @pl.when(step >= heads)
        def _():
            far_terms(act_ref, wk_ref, wv_ref, info, (n_sec, blk, first), *far_refs)

    def head(rows, count):
        return pl.BlockSpec((rows, count * HEAD), lambda h, info: (0, jnp.minimum(h, heads - 1)))

    def enc_block(m):
        return pl.BlockSpec((blk, quarter), lambda h, info: (0, mod4(info[X] - m)))

    def weight(m):
        return pl.BlockSpec((quarter, HEAD), lambda h, info: (mod4(info[X] - m), jnp.minimum(h, heads - 1)))

    rows_out = jax.ShapeDtypeStruct((total, quarter), bf16)
    if queries is None:
        far_shape, far_specs = [], []
        targets = 0
        out_shape, out_specs = [jax.ShapeDtypeStruct((total, 2 * cols), f32)], [head(total, 2)]
    else:
        targets = queries[0].shape[0]
        act_out = jax.ShapeDtypeStruct((total, 2 * cols), bf16)
        out_shape, out_specs = [jax.ShapeDtypeStruct((targets, cols), bf16), act_out], [head(targets, 1), whole(act_out)]
        per = quarter // UNIT

        def unit(h):
            return jnp.maximum(h - heads, 0)

        far_weight = pl.BlockSpec((UNIT, cols), lambda h, info: (mod4(info[X] - 2) * per + unit(h), 0))
        far_rows = (total, blk // 2 * len(first), blk // 2 * len(first))
        far_shape = [jax.ShapeDtypeStruct((r, quarter), bf16) for r in far_rows]
        far_specs = [pl.BlockSpec((r, UNIT), lambda h, info: (0, unit(h))) for r in far_rows]
        extra += [wk, wv]
    return pl.pallas_call(
        body,
        grid_spec=pltpu.PrefetchScalarGridSpec(
            num_scalar_prefetch=1,
            grid=(heads if queries is None else heads + per,),
            in_specs=[enc_block(m) for m, _ in quarters]
            + [whole(p) for p, _ in parts]
            + [weight(m) for m, _ in quarters for _ in range(2)]
            + ([] if acc is None else [head(total, 2)])
            + ([] if queries is None else [head(targets, 1)] * 2 + [far_weight] * 2)
            + [ANYWHERE] * len(after),
            out_specs=out_specs + [whole(rows_out)] * n + far_specs,
        ),
        out_shape=out_shape + [rows_out] * n + far_shape,
        compiler_params=params(28),
        cost_estimate=LIGHT,
    )(info, *[enc] * n, *[p for p, _ in parts], *[wk, wv] * n, *extra, *after)


def attend(k, v, q, g, info, ctx_ref, act_ref):
    scale = HEAD ** (-0.5)
    place = lax.broadcasted_iota(jnp.int32, (k.shape[0], 1), 0)
    scores = jnp.where(place < info[SRC_LIVE], dot_t(k, q), masked_score / scale)
    highest = jnp.max(scores, axis=0, keepdims=True)
    shifted = jnp.exp((scores - highest) * scale)
    weights = shifted * (1.0 / jnp.sum(shifted, axis=0, keepdims=True))
    low = weights.astype(bf16)
    target = lax.broadcasted_iota(jnp.int32, (q.shape[0], 1), 0)
    g = jnp.where(target < info[TGT_LIVE], g.astype(f32), 0.0).astype(bf16)
    prob = dot_t(v, g)
    prob_dot = jnp.sum(weights * prob, axis=0, keepdims=True)
    grad = (weights * (prob - prob_dot)).astype(bf16)
    act_ref[:, :HEAD] = (dot(grad, q) * scale).astype(bf16)
    act_ref[:, HEAD:] = dot(low, g).astype(bf16)
    ctx_ref[...] = t_dot(low, v).astype(bf16)


def block_of(info, which, n_sec):
    back = (0, 1 + 2 * info[LO], 3 - 2 * info[LO], 2)[which]
    return lax.rem(info[SEC] - back + n_sec, n_sec)


def transposed(act_ref, wk_ref, wv_ref):
    sums = None
    for h in range(wk_ref.shape[1] // HEAD):
        for j, w_ref in enumerate((wk_ref, wv_ref)):
            at = (2 * h + j) * HEAD
            term = dot_t(act_ref[:, at : at + HEAD], w_ref[:, h * HEAD : (h + 1) * HEAD])
            sums = term if sums is None else sums + term
    return sums


def far_terms(act_ref, wk_ref, wv_ref, info, first, out_ref, up_ref, down_ref):
    out_ref[...] = transposed(act_ref, wk_ref, wv_ref).astype(out_ref.dtype)
    n_sec, blk, blocks = first
    mid = blk // 2
    for i, which in enumerate(blocks):
        at = block_of(info, which, n_sec) * blk
        up_ref[i * mid : (i + 1) * mid, :] = out_ref[pl.ds(pl.multiple_of(at, blk), mid), :]
        down_ref[i * mid : (i + 1) * mid, :] = out_ref[pl.ds(pl.multiple_of(at + mid, mid), mid), :]


def partial_grad(act, wk, wv, info, quarters, dtype, after=()):
    total, cols = act.shape[0], wk.shape[1]
    width = wk.shape[0]
    per = width // XS // UNIT
    n = per * len(quarters)

    def unit(i, info):
        quarter = i // per
        m = quarters[0]
        for j, other in enumerate(quarters[1:]):
            m = jnp.where(quarter == j + 1, other, m)
        return mod4(info[X] - m) * per + i % per

    def body(info, act_ref, wk_ref, wv_ref, *refs):
        refs[-1][...] = transposed(act_ref, wk_ref, wv_ref).astype(dtype)

    weight = pl.BlockSpec((UNIT, cols), lambda i, info: (unit(i, info), 0))
    block = pl.BlockSpec((total, UNIT), lambda i, info: (0, i))
    out_specs, out_shape = [block], [jax.ShapeDtypeStruct((total, n * UNIT), dtype)]
    return pl.pallas_call(
        body,
        grid_spec=pltpu.PrefetchScalarGridSpec(
            num_scalar_prefetch=1,
            grid=(n,),
            in_specs=[whole(act), weight, weight] + [ANYWHERE] * len(after),
            out_specs=out_specs,
        ),
        out_shape=out_shape,
        compiler_params=params(12),
        cost_estimate=LIGHT,
    )(info, act, wk, wv, *after)


def pair_grads(kept, got, act, act_other, info, blocks, after=()):
    width = act.shape[1]
    half = kept.shape[1] // XS

    def body(info, kept_ref, got_ref, act_ref, other_ref, *refs):
        for ref, group in zip(refs, blocks):
            for j, at in enumerate(group):
                here = slice(at * half, (at + 1) * half)
                term = t_dot(kept_ref[:, here], act_ref[...]) + t_dot(got_ref[:, here], other_ref[...])
                ref[j * half : (j + 1) * half, :] = term.astype(bf16)

    out = [jax.ShapeDtypeStruct((len(group) * half, width), bf16) for group in blocks]
    return small(body, [kept, got, act, act_other], out, info, after)


def small(body, ins, outs, info, after=()):
    ins = [i if isinstance(i, tuple) else (i, whole(i)) for i in ins]
    n = len(ins)

    def run(info, *refs):
        body(info, *refs[:n], *refs[n + len(after) :])

    return pl.pallas_call(
        run,
        grid_spec=pltpu.PrefetchScalarGridSpec(
            num_scalar_prefetch=1,
            grid=(1,),
            in_specs=[s for _, s in ins] + [ANYWHERE] * len(after),
            out_specs=[whole(o) for o in outs],
        ),
        out_shape=[jax.ShapeDtypeStruct(o.shape, o.dtype) for o in outs],
        compiler_params=params(28),
        cost_estimate=LIGHT,
    )(info, *[a for a, _ in ins], *after)


def make_shards(n_sec):

    def shift_x(v, k):
        return lax.ppermute(v, "x", [(i, (i + k) % XS) for i in range(XS)])

    def swap_core(v):
        return lax.ppermute(v, "core", [(0, 1), (1, 0)])

    def swap_low(v):
        return lax.ppermute(v, "low", [(0, 1), (1, 0)])

    def cross(v):
        n = 2 * n_sec
        return lax.ppermute(v, ("section", "low"), [(z, (z + (1 if z % 2 else -1)) % n) for z in range(n)])

    def jump(v, k):
        n = 2 * n_sec
        return lax.ppermute(v, ("section", "low"), [(z, (z + (-2 * k if z % 2 else 2 * k)) % n) for z in range(n)])

    def shift_y(v, change=False):
        n = 2 * XS
        pairs = [(i, (i + (-2 if i % 2 else 2)) % n) for i in range(n)]
        return lax.ppermute(v, ("y", "core"), [(i, j ^ 1 if change else j) for i, j in pairs])

    def shards(enc_out, key_weight, value_weight, queries, ctx_grad, src_pad, tgt_pad):
        enc, wk, wv = enc_out[0], key_weight[0], value_weight[0]
        blk, width = enc.shape
        quarter = width // XS
        local_width = wk.shape[1]
        total_src = n_sec * blk
        x, lo, sec = lax.axis_index("x"), lax.axis_index("low"), lax.axis_index("section")
        info = jnp.stack(
            [
                x,
                sec,
                lo,
                lax.axis_index("y"),
                lax.axis_index("core"),
                total_src - src_pad[0],
                queries.shape[2] - tgt_pad[0],
            ]
        ).astype(jnp.int32)

        mine = lax.dynamic_slice(enc, (0, x * quarter), (blk, quarter))
        mid = blk // 2

        def both(up, down):
            return shift_x(up, 1), shift_x(down, -1)

        def with_halves(block, ups, downs):
            part = jax.ShapeDtypeStruct((mid, quarter), bf16)
            out = jax.ShapeDtypeStruct((mid + mid * len(ups), quarter), bf16)

            def body(info, block_ref, *refs):
                up_out, down_out, top_out, low_out = refs[-4:]
                top_out[...] = block_ref[:mid]
                low_out[...] = block_ref[mid:]
                up_out[:mid] = block_ref[mid:]
                down_out[:mid] = block_ref[:mid]
                for i in range(len(ups)):
                    at = mid + i * mid
                    up_out[at : at + mid] = refs[i][:mid]
                    down_out[at : at + mid] = refs[len(ups) + i][mid:blk]

            return small(body, [block, *ups, *downs], [out, out, part, part], info)

        b1, b2 = cross(mine), jump(mine, -1)
        u1, d1 = both(b1, b1)
        u2, d2 = both(b2, b2)
        b3 = cross(b2)
        out3 = with_halves(b3, (u1, u2), (d1, d2))
        ut, dt = both(*out3[2:])
        u3, d3 = both(*out3[:2])
        u4, d4 = both(ut, dt)
        rows = [None] * XS

        def parts(*got):
            return [(g, [(0, blk, i + 1, 0)]) for i, g in enumerate(got)]

        acc, rows[0] = project([(0, parts(b1, b2, b3))], enc, wk, wv, None, info, n_sec, out3)

        beside = [
            (1, parts(u1, u2) + [(ut, [(0, mid, 3, 0)]), (u3, [(0, mid, 3, mid)])]),
            (3, parts(d1, d2) + [(dt, [(0, mid, 3, mid)]), (d3, [(0, mid, 3, 0)])]),
        ]
        acc, rows[1], rows[3] = project(beside, enc, wk, wv, acc, info, n_sec)
        last = [(u3, [(mid, mid, 1, 0), (blk, mid, 2, 0)]), (d3, [(mid, mid, 1, mid), (blk, mid, 2, mid)])]
        last += [(u4, [(0, mid, 3, 0)]), (d4, [(0, mid, 3, mid)])]
        asked = (queries[0, 0], ctx_grad[0, 0])
        first = (3, 0, 2)
        context, act, rows[2], far, up, down = project(
            [(2, last)], enc, wk, wv, acc, info, n_sec, queries=asked, first=first
        )
        context = context[None, None]
        act_other = swap_core(act)

        half = quarter // 2

        def pack(own, after=()):
            def body(info, *refs):
                side = info[CORE] if own else 1 - info[CORE]
                for m, ref in enumerate(refs[:-1]):
                    step = mod4(info[X] - info[Y] - m)

                    @pl.when(step == 1 + 2 * side)
                    def _():
                        refs[-1][:, :quarter] = ref[...]

                    for place, at in ((2, quarter), (0, quarter + half)):

                        @pl.when(step == place)
                        def _():
                            refs[-1][:, at : at + half] = ref[:, pl.ds(pl.multiple_of(side * half, half), half)]

            return small(body, rows, [jax.ShapeDtypeStruct((total_src, 2 * quarter), bf16)], info, after)[0]

        sent = pack(False)
        got = swap_core(sent)

        halves = both(up, down)
        (near,) = partial_grad(act, wk, wv, info, (3, 1), bf16, (far,))
        kept = pack(True, (near,))
        (far_y,) = pair_grads(kept, got, act, act_other, info, [(2,)], (near,))
        (keep,) = partial_grad(act, wk, wv, info, (0,), f32, (near,))

        def rows_of(v, which):
            return v, pl.BlockSpec((blk, v.shape[1]), lambda i, info: (block_of(info, which, n_sec), 0))

        def stage(done, sent, ahead, after=(), through=()):
            ins, outs = [], []
            for which, (up, down), _, more in done:
                ins += [rows_of(keep, which), up, down, *more]
                outs.append(jax.ShapeDtypeStruct((blk, quarter), bf16))
            for which, (up, down), _ in sent:
                ins += [rows_of(near, which), up, down]
            ins += [rows_of(far, which) for which in ahead] + list(through)
            size = blk * len(sent) + mid * len(ahead)
            outs += [jax.ShapeDtypeStruct((size, quarter), bf16)] * (2 if size else 0) + list(through)

            def body(info, *refs):
                refs, out_refs = list(refs[: len(ins)]), list(refs[len(ins) :])
                for _, _, at, more in done:
                    sums = refs.pop(0)[...]
                    for _ in range(2):
                        sums = sums + refs.pop(0)[at : at + blk].astype(f32)
                    for _ in more:
                        sums = sums + refs.pop(0)[...].astype(f32)
                    out_refs.pop(0)[...] = sums.astype(bf16)
                to = 0
                if size:
                    up_out, down_out = out_refs.pop(0), out_refs.pop(0)
                for _, _, at in sent:
                    near_ref, up_ref, down_ref = (refs.pop(0) for _ in range(3))
                    half_up, half_down = up_ref[at : at + mid].astype(f32), down_ref[at : at + mid].astype(f32)
                    up_out[to : to + mid] = (near_ref[:mid, :quarter].astype(f32) + half_up).astype(bf16)
                    up_out[to + mid : to + blk] = near_ref[mid:, :quarter]
                    down_out[to : to + mid] = near_ref[:mid, quarter:]
                    down_out[to + mid : to + blk] = (near_ref[mid:, quarter:].astype(f32) + half_down).astype(bf16)
                    to += blk
                for _ in ahead:
                    far_ref = refs.pop(0)
                    up_out[to : to + mid] = far_ref[:mid]
                    down_out[to : to + mid] = far_ref[mid:]
                    to += mid
                for ref, out_ref in zip(refs, out_refs):
                    out_ref[...] = ref[...]

            return small(body, ins, outs, info, after)

        up, down, far_y = stage([], [(3, halves, 0)], [1], through=[far_y])
        got_y = shift_y(far_y)
        near_y, keep_y = pair_grads(kept, got, act, act_other, info, [(0, 1), (3,)], (up,))
        side = both(up, down)
        total3, up, down = stage([(3, side, 0, [])], [(2, halves, 2 * mid), (1, side, blk)], [])
        carried = cross(total3)
        side = both(up, down)
        total2, total1, up, down = stage([(2, side, 0, [carried]), (1, side, blk, [])], [(0, halves, mid)], [])

        def add_y(info, near_ref, got_ref, same_ref, other_ref):
            here = pl.ds(pl.multiple_of(info[CORE] * half, half), half)
            there = pl.ds(pl.multiple_of((1 - info[CORE]) * half, half), half)
            same_ref[...] = (near_ref[here, :].astype(f32) + got_ref[...].astype(f32)).astype(bf16)
            other_ref[...] = near_ref[there, :]

        same_y, other_y = small(add_y, [near_y, got_y], [keep_y, keep_y], info, (total1,))
        same_y = shift_y(same_y)
        carried = [jump(total2, 1), cross(total1)]
        side = both(up, down)
        mine, other_y = stage([(0, side, 0, carried)], [], [], through=[other_y])
        in_y = same_y, shift_y(other_y, True)
        other = swap_low(mine)
        part = mine

        def add_two(info, one_ref, two_ref, out_ref, top_ref):
            out_ref[...] = (one_ref[...].astype(f32) + two_ref[...].astype(f32)).astype(bf16)
            top_ref[...] = out_ref[:mid]

        half_part = jax.ShapeDtypeStruct((mid, quarter), bf16)
        final, top = small(add_two, [mine, other], [part, half_part], info)
        below, above = both(final, final)
        far_top = shift_x(top, 2)

        def cut_low(info, in_ref, out_ref):
            out_ref[...] = in_ref[mid:]

        (low,) = small(cut_low, [above], [half_part], info)
        far_low = shift_x(low, -1)

        def finish(info, keep_ref, one_ref, two_ref, key_ref, value_ref, end_ref):
            end_ref[...] = jnp.zeros_like(end_ref)
            sums = keep_ref[...].astype(f32) + one_ref[...].astype(f32) + two_ref[...].astype(f32)
            sums = sums.astype(bf16)
            for h in range(local_width // HEAD):
                at = 2 * h * HEAD
                key_ref[:, h * HEAD : (h + 1) * HEAD] = sums[:, at : at + HEAD]
                value_ref[:, h * HEAD : (h + 1) * HEAD] = sums[:, at + HEAD : at + 2 * HEAD]

        shard = jax.ShapeDtypeStruct((half, local_width), bf16)
        end = jax.ShapeDtypeStruct((16, 128), bf16)
        key_weight_grad, value_weight_grad, end = small(finish, [keep_y, *in_y], [shard, shard, end], info, (low,))

        def place(info, *refs):
            for ref, k in zip(refs[:-1], (0, 1, 3)):
                at = mod4(info[X] - k) * quarter
                refs[-1][:, pl.ds(pl.multiple_of(at, quarter), quarter)] = ref[...]

        whole_rows = jax.ShapeDtypeStruct((blk, width), bf16)
        (enc_grad,) = small(place, [final, below, above], [whole_rows], info, (low,))

        def place_last(info, top_ref, low_ref, _, __, out_ref):
            out_ref[:mid] = top_ref[...]
            out_ref[mid:] = low_ref[...]

        enc_grad = pl.pallas_call(
            place_last,
            grid_spec=pltpu.PrefetchScalarGridSpec(
                num_scalar_prefetch=1,
                grid=(1,),
                in_specs=[whole(half_part), whole(half_part), ANYWHERE, ANYWHERE],
                out_specs=pl.BlockSpec((blk, quarter), lambda i, info: (0, mod4(info[X] - 2))),
            ),
            out_shape=whole_rows,
            input_output_aliases={3: 0},
            compiler_params=params(8),
            cost_estimate=LIGHT,
        )(info, far_top, far_low, enc_grad, end)
        enc_grad = enc_grad[None]

        return (context, enc_grad, key_weight_grad[None], value_weight_grad[None])

    return shards


def solution(mesh):
    n_sec, n_dp, n_ten = (mesh.shape[name] for name in ("section", "dp", "tensor"))
    fine = Mesh(
        mesh.devices.reshape(n_sec, n_dp // 2, 2, XS, n_ten // XS), ("section", "y", "core", "x", "low")
    )
    dp, heads = ("y", "core"), ("x", "low")
    return jax.shard_map(
        make_shards(n_sec),
        mesh=fine,
        in_specs=(
            P(dp, "section", None),
            P("section", None, heads),
            P("section", None, heads),
            P("section", dp, None, heads),
            P("section", dp, None, heads),
            P(dp),
            P(dp),
        ),
        out_specs=(
            P("section", dp, None, heads),
            P(dp, "section", None),
            P("section", dp, heads),
            P("section", dp, heads),
        ),
        check_vma=False,
    )
```

```python
import jax
import jax.numpy as jnp
from jax import lax
from jax.experimental import pallas as pl
from jax.experimental.pallas import tpu as pltpu
from jax.sharding import Mesh
from jax.sharding import PartitionSpec as P

HEAD = 256
XS = 4
UNIT = 512
masked_score = -1e30
f32 = jnp.float32
bf16 = jnp.bfloat16
X, SEC, LO, Y, CORE, SRC_LIVE, TGT_LIVE = range(7)


def dot(a, b):
    return jnp.dot(a, b, preferred_element_type=f32)


def dot_t(a, b):
    return lax.dot_general(a, b, (((1,), (1,)), ((), ())), preferred_element_type=f32)


def t_dot(a, b):
    return lax.dot_general(a, b, (((0,), (0,)), ((), ())), preferred_element_type=f32)


def mod4(v):
    return lax.rem(v + 8, 4)


def params(mib):
    return pltpu.CompilerParams(vmem_limit_bytes=mib * 1024 * 1024)


def whole(a):
    return pl.BlockSpec(a.shape, lambda i, info: (0,) * a.ndim)


ANYWHERE = pl.BlockSpec(memory_space=pl.ANY)
LIGHT = pl.CostEstimate(flops=1, bytes_accessed=1, transcendentals=0)


def project(quarters, enc, wk, wv, acc, info, n_sec, after=(), queries=None, first=None):
    blk, width = enc.shape
    quarter = width // XS
    total = n_sec * blk
    cols = wk.shape[1]
    heads = cols // HEAD
    parts = [part for _, some in quarters for part in some]
    extra = ([] if acc is None else [acc]) + list(queries or ())
    n = len(quarters)

    def body(info, *refs):
        refs = list(refs)
        enc_refs = [refs.pop(0) for _ in quarters]
        part_refs = [refs.pop(0) for _ in parts]
        weight_refs = [refs.pop(0) for _ in range(2 * n)]
        acc_ref = refs.pop(0) if acc is not None else None
        step = pl.program_id(0)
        if queries is not None:
            far_refs = refs[-3:]
            del refs[-3:]
        rows_refs = refs[-n:]

        @pl.when(step == 0)
        def _():
            left = list(part_refs)
            for rows_ref, enc_ref, (_, some) in zip(rows_refs, enc_refs, quarters):
                rows_ref[pl.ds(pl.multiple_of(info[SEC] * blk, blk), blk), :] = enc_ref[...]
                for _, pieces in some:
                    ref = left.pop(0)
                    for at, count, block, off in pieces:
                        to = block_of(info, block, n_sec) * blk + off
                        rows_ref[pl.ds(pl.multiple_of(to, count), count), :] = ref[at : at + count, :]

        def head_sums():
            sums = [None if acc_ref is None else acc_ref[:, j * HEAD : (j + 1) * HEAD] for j in range(2)]
            for i, rows_ref in enumerate(rows_refs):
                rows = rows_ref[...]
                for j in range(2):
                    term = dot(rows, weight_refs[2 * i + j][...])
                    sums[j] = term if sums[j] is None else sums[j] + term
            return sums

        if queries is None:
            sums = head_sums()
            refs[-n - 1][:, :HEAD] = sums[0]
            refs[-n - 1][:, HEAD:] = sums[1]
            return
        q_ref, g_ref, wk_ref, wv_ref = refs[:4]
        ctx_ref, act_ref = refs[-n - 2], refs[-n - 1]

        @pl.when(step < heads)
        def _():
            k, v = (one.astype(bf16) for one in head_sums())
            at = pl.multiple_of(step * 2 * HEAD, 2 * HEAD)
            here = act_ref.at[:, pl.ds(at, 2 * HEAD)]
            attend(k, v, q_ref[...], g_ref[...], info, ctx_ref, here)

        @pl.when(step >= heads)
        def _():
            far_terms(act_ref, wk_ref, wv_ref, info, (n_sec, blk, first), *far_refs)

    def head(rows, count):
        return pl.BlockSpec((rows, count * HEAD), lambda h, info: (0, jnp.minimum(h, heads - 1)))

    def enc_block(m):
        return pl.BlockSpec((blk, quarter), lambda h, info: (0, mod4(info[X] - m)))

    def weight(m):
        return pl.BlockSpec((quarter, HEAD), lambda h, info: (mod4(info[X] - m), jnp.minimum(h, heads - 1)))

    rows_out = jax.ShapeDtypeStruct((total, quarter), bf16)
    if queries is None:
        far_shape, far_specs = [], []
        targets = 0
        out_shape, out_specs = [jax.ShapeDtypeStruct((total, 2 * cols), f32)], [head(total, 2)]
    else:
        targets = queries[0].shape[0]
        act_out = jax.ShapeDtypeStruct((total, 2 * cols), bf16)
        out_shape, out_specs = [jax.ShapeDtypeStruct((targets, cols), bf16), act_out], [head(targets, 1), whole(act_out)]
        per = quarter // UNIT

        def unit(h):
            return jnp.maximum(h - heads, 0)

        far_weight = pl.BlockSpec((UNIT, cols), lambda h, info: (mod4(info[X] - 2) * per + unit(h), 0))
        far_rows = (total, blk // 2 * len(first), blk // 2 * len(first))
        far_shape = [jax.ShapeDtypeStruct((r, quarter), bf16) for r in far_rows]
        far_specs = [pl.BlockSpec((r, UNIT), lambda h, info: (0, unit(h))) for r in far_rows]
        extra += [wk, wv]
    return pl.pallas_call(
        body,
        grid_spec=pltpu.PrefetchScalarGridSpec(
            num_scalar_prefetch=1,
            grid=(heads if queries is None else heads + per,),
            in_specs=[enc_block(m) for m, _ in quarters]
            + [whole(p) for p, _ in parts]
            + [weight(m) for m, _ in quarters for _ in range(2)]
            + ([] if acc is None else [head(total, 2)])
            + ([] if queries is None else [head(targets, 1)] * 2 + [far_weight] * 2)
            + [ANYWHERE] * len(after),
            out_specs=out_specs + [whole(rows_out)] * n + far_specs,
        ),
        out_shape=out_shape + [rows_out] * n + far_shape,
        compiler_params=params(28),
        cost_estimate=LIGHT,
    )(info, *[enc] * n, *[p for p, _ in parts], *[wk, wv] * n, *extra, *after)


def attend(k, v, q, g, info, ctx_ref, act_ref):
    scale = HEAD ** (-0.5)
    place = lax.broadcasted_iota(jnp.int32, (k.shape[0], 1), 0)
    scores = jnp.where(place < info[SRC_LIVE], dot_t(k, q), masked_score / scale)
    highest = jnp.max(scores, axis=0, keepdims=True)
    shifted = jnp.exp((scores - highest) * scale)
    weights = shifted * (1.0 / jnp.sum(shifted, axis=0, keepdims=True))
    low = weights.astype(bf16)
    target = lax.broadcasted_iota(jnp.int32, (q.shape[0], 1), 0)
    g = jnp.where(target < info[TGT_LIVE], g.astype(f32), 0.0).astype(bf16)
    prob = dot_t(v, g)
    prob_dot = jnp.sum(weights * prob, axis=0, keepdims=True)
    grad = (weights * (prob - prob_dot)).astype(bf16)
    act_ref[:, :HEAD] = (dot(grad, q) * scale).astype(bf16)
    act_ref[:, HEAD:] = dot(low, g).astype(bf16)
    ctx_ref[...] = t_dot(low, v).astype(bf16)


def block_of(info, which, n_sec):
    back = (0, 1 + 2 * info[LO], 3 - 2 * info[LO], 2)[which]
    return lax.rem(info[SEC] - back + n_sec, n_sec)


def transposed(act_ref, wk_ref, wv_ref):
    sums = None
    for h in range(wk_ref.shape[1] // HEAD):
        for j, w_ref in enumerate((wk_ref, wv_ref)):
            at = (2 * h + j) * HEAD
            term = dot_t(act_ref[:, at : at + HEAD], w_ref[:, h * HEAD : (h + 1) * HEAD])
            sums = term if sums is None else sums + term
    return sums


def far_terms(act_ref, wk_ref, wv_ref, info, first, out_ref, up_ref, down_ref):
    out_ref[...] = transposed(act_ref, wk_ref, wv_ref).astype(out_ref.dtype)
    n_sec, blk, blocks = first
    mid = blk // 2
    for i, which in enumerate(blocks):
        at = block_of(info, which, n_sec) * blk
        up_ref[i * mid : (i + 1) * mid, :] = out_ref[pl.ds(pl.multiple_of(at, blk), mid), :]
        down_ref[i * mid : (i + 1) * mid, :] = out_ref[pl.ds(pl.multiple_of(at + mid, mid), mid), :]


def partial_grad(act, wk, wv, info, quarters, dtype, after=()):
    total, cols = act.shape[0], wk.shape[1]
    width = wk.shape[0]
    per = width // XS // UNIT
    n = per * len(quarters)

    def unit(i, info):
        quarter = i // per
        m = quarters[0]
        for j, other in enumerate(quarters[1:]):
            m = jnp.where(quarter == j + 1, other, m)
        return mod4(info[X] - m) * per + i % per

    def body(info, act_ref, wk_ref, wv_ref, *refs):
        refs[-1][...] = transposed(act_ref, wk_ref, wv_ref).astype(dtype)

    weight = pl.BlockSpec((UNIT, cols), lambda i, info: (unit(i, info), 0))
    block = pl.BlockSpec((total, UNIT), lambda i, info: (0, i))
    out_specs, out_shape = [block], [jax.ShapeDtypeStruct((total, n * UNIT), dtype)]
    return pl.pallas_call(
        body,
        grid_spec=pltpu.PrefetchScalarGridSpec(
            num_scalar_prefetch=1,
            grid=(n,),
            in_specs=[whole(act), weight, weight] + [ANYWHERE] * len(after),
            out_specs=out_specs,
        ),
        out_shape=out_shape,
        compiler_params=params(12),
        cost_estimate=LIGHT,
    )(info, act, wk, wv, *after)


def pair_grads(kept, got, act, act_other, info, blocks, after=()):
    width = act.shape[1]
    half = kept.shape[1] // XS

    def body(info, kept_ref, got_ref, act_ref, other_ref, *refs):
        for ref, group in zip(refs, blocks):
            for j, at in enumerate(group):
                here = slice(at * half, (at + 1) * half)
                term = t_dot(kept_ref[:, here], act_ref[...]) + t_dot(got_ref[:, here], other_ref[...])
                ref[j * half : (j + 1) * half, :] = term.astype(bf16)

    out = [jax.ShapeDtypeStruct((len(group) * half, width), bf16) for group in blocks]
    return small(body, [kept, got, act, act_other], out, info, after)


def small(body, ins, outs, info, after=()):
    ins = [i if isinstance(i, tuple) else (i, whole(i)) for i in ins]
    n = len(ins)

    def run(info, *refs):
        body(info, *refs[:n], *refs[n + len(after) :])

    return pl.pallas_call(
        run,
        grid_spec=pltpu.PrefetchScalarGridSpec(
            num_scalar_prefetch=1,
            grid=(1,),
            in_specs=[s for _, s in ins] + [ANYWHERE] * len(after),
            out_specs=[whole(o) for o in outs],
        ),
        out_shape=[jax.ShapeDtypeStruct(o.shape, o.dtype) for o in outs],
        compiler_params=params(28),
        cost_estimate=LIGHT,
    )(info, *[a for a, _ in ins], *after)


def make_shards(n_sec):

    def shift_x(v, k):
        return lax.ppermute(v, "x", [(i, (i + k) % XS) for i in range(XS)])

    def swap_core(v):
        return lax.ppermute(v, "core", [(0, 1), (1, 0)])

    def swap_low(v):
        return lax.ppermute(v, "low", [(0, 1), (1, 0)])

    def cross(v):
        n = 2 * n_sec
        return lax.ppermute(v, ("section", "low"), [(z, (z + (1 if z % 2 else -1)) % n) for z in range(n)])

    def jump(v, k):
        n = 2 * n_sec
        return lax.ppermute(v, ("section", "low"), [(z, (z + (-2 * k if z % 2 else 2 * k)) % n) for z in range(n)])

    def shift_y(v, change=False):
        n = 2 * XS
        pairs = [(i, (i + (-2 if i % 2 else 2)) % n) for i in range(n)]
        return lax.ppermute(v, ("y", "core"), [(i, j ^ 1 if change else j) for i, j in pairs])

    def shards(enc_out, key_weight, value_weight, queries, ctx_grad, src_pad, tgt_pad):
        enc, wk, wv = enc_out[0], key_weight[0], value_weight[0]
        blk, width = enc.shape
        quarter = width // XS
        local_width = wk.shape[1]
        total_src = n_sec * blk
        x, lo, sec = lax.axis_index("x"), lax.axis_index("low"), lax.axis_index("section")
        info = jnp.stack(
            [
                x,
                sec,
                lo,
                lax.axis_index("y"),
                lax.axis_index("core"),
                total_src - src_pad[0],
                queries.shape[2] - tgt_pad[0],
            ]
        ).astype(jnp.int32)

        mine = lax.dynamic_slice(enc, (0, x * quarter), (blk, quarter))
        mid = blk // 2

        def both(up, down):
            return shift_x(up, 1), shift_x(down, -1)

        def with_halves(block, ups, downs):
            part = jax.ShapeDtypeStruct((mid, quarter), bf16)
            out = jax.ShapeDtypeStruct((mid + mid * len(ups), quarter), bf16)

            def body(info, block_ref, *refs):
                up_out, down_out, top_out, low_out = refs[-4:]
                top_out[...] = block_ref[:mid]
                low_out[...] = block_ref[mid:]
                up_out[:mid] = block_ref[mid:]
                down_out[:mid] = block_ref[:mid]
                for i in range(len(ups)):
                    at = mid + i * mid
                    up_out[at : at + mid] = refs[i][:mid]
                    down_out[at : at + mid] = refs[len(ups) + i][mid:blk]

            return small(body, [block, *ups, *downs], [out, out, part, part], info)

        b1, b2 = cross(mine), jump(mine, -1)
        u1, d1 = both(b1, b1)
        u2, d2 = both(b2, b2)
        b3 = cross(b2)
        out3 = with_halves(b3, (u1, u2), (d1, d2))
        ut, dt = both(*out3[2:])
        u3, d3 = both(*out3[:2])
        rows = [None] * XS

        def parts(*got):
            return [(g, [(0, blk, i + 1, 0)]) for i, g in enumerate(got)]

        acc, rows[0] = project([(0, parts(b1, b2, b3))], enc, wk, wv, None, info, n_sec, out3)

        def pass_on(info, up_ref, down_ref, up_out, down_out):
            up_out[...] = up_ref[...]
            down_out[...] = down_ref[...]

        u4, d4 = both(*small(pass_on, [ut, dt], [ut, dt], info, (acc,)))
        beside = [
            (1, parts(u1, u2) + [(ut, [(0, mid, 3, 0)]), (u3, [(0, mid, 3, mid)])]),
            (3, parts(d1, d2) + [(dt, [(0, mid, 3, mid)]), (d3, [(0, mid, 3, 0)])]),
        ]
        acc, rows[1], rows[3] = project(beside, enc, wk, wv, acc, info, n_sec)
        last = [(u3, [(mid, mid, 1, 0), (blk, mid, 2, 0)]), (d3, [(mid, mid, 1, mid), (blk, mid, 2, mid)])]
        last += [(u4, [(0, mid, 3, 0)]), (d4, [(0, mid, 3, mid)])]
        asked = (queries[0, 0], ctx_grad[0, 0])
        first = (3, 0, 2)
        context, act, rows[2], far, up, down = project(
            [(2, last)], enc, wk, wv, acc, info, n_sec, queries=asked, first=first
        )
        context = context[None, None]
        act_other = swap_core(act)

        half = quarter // 2

        def pack(own, after=()):
            def body(info, *refs):
                side = info[CORE] if own else 1 - info[CORE]
                for m, ref in enumerate(refs[:-1]):
                    step = mod4(info[X] - info[Y] - m)

                    @pl.when(step == 1 + 2 * side)
                    def _():
                        refs[-1][:, :quarter] = ref[...]

                    for place, at in ((2, quarter), (0, quarter + half)):

                        @pl.when(step == place)
                        def _():
                            refs[-1][:, at : at + half] = ref[:, pl.ds(pl.multiple_of(side * half, half), half)]

            return small(body, rows, [jax.ShapeDtypeStruct((total_src, 2 * quarter), bf16)], info, after)[0]

        sent = pack(False)
        got = swap_core(sent)

        halves = both(up, down)
        (near,) = partial_grad(act, wk, wv, info, (3, 1), bf16, (far,))
        kept = pack(True, (near,))
        (far_y,) = pair_grads(kept, got, act, act_other, info, [(2,)], (near,))
        (keep,) = partial_grad(act, wk, wv, info, (0,), f32, (near,))

        def rows_of(v, which):
            return v, pl.BlockSpec((blk, v.shape[1]), lambda i, info: (block_of(info, which, n_sec), 0))

        def stage(done, sent, ahead, after=(), through=()):
            ins, outs = [], []
            for which, (up, down), _, more in done:
                ins += [rows_of(keep, which), up, down, *more]
                outs.append(jax.ShapeDtypeStruct((blk, quarter), bf16))
            for which, (up, down), _ in sent:
                ins += [rows_of(near, which), up, down]
            ins += [rows_of(far, which) for which in ahead] + list(through)
            size = blk * len(sent) + mid * len(ahead)
            outs += [jax.ShapeDtypeStruct((size, quarter), bf16)] * (2 if size else 0) + list(through)

            def body(info, *refs):
                refs, out_refs = list(refs[: len(ins)]), list(refs[len(ins) :])
                for _, _, at, more in done:
                    sums = refs.pop(0)[...]
                    for _ in range(2):
                        sums = sums + refs.pop(0)[at : at + blk].astype(f32)
                    for _ in more:
                        sums = sums + refs.pop(0)[...].astype(f32)
                    out_refs.pop(0)[...] = sums.astype(bf16)
                to = 0
                if size:
                    up_out, down_out = out_refs.pop(0), out_refs.pop(0)
                for _, _, at in sent:
                    near_ref, up_ref, down_ref = (refs.pop(0) for _ in range(3))
                    half_up, half_down = up_ref[at : at + mid].astype(f32), down_ref[at : at + mid].astype(f32)
                    up_out[to : to + mid] = (near_ref[:mid, :quarter].astype(f32) + half_up).astype(bf16)
                    up_out[to + mid : to + blk] = near_ref[mid:, :quarter]
                    down_out[to : to + mid] = near_ref[:mid, quarter:]
                    down_out[to + mid : to + blk] = (near_ref[mid:, quarter:].astype(f32) + half_down).astype(bf16)
                    to += blk
                for _ in ahead:
                    far_ref = refs.pop(0)
                    up_out[to : to + mid] = far_ref[:mid]
                    down_out[to : to + mid] = far_ref[mid:]
                    to += mid
                for ref, out_ref in zip(refs, out_refs):
                    out_ref[...] = ref[...]

            return small(body, ins, outs, info, after)

        up, down, far_y = stage([], [(3, halves, 0)], [1], through=[far_y])
        got_y = shift_y(far_y)
        near_y, keep_y = pair_grads(kept, got, act, act_other, info, [(0, 1), (3,)], (up,))
        side = both(up, down)
        total3, up, down = stage([(3, side, 0, [])], [(2, halves, 2 * mid), (1, side, blk)], [])
        carried = cross(total3)
        side = both(up, down)
        total2, total1, up, down = stage([(2, side, 0, [carried]), (1, side, blk, [])], [(0, halves, mid)], [])

        def add_y(info, near_ref, got_ref, same_ref, other_ref):
            here = pl.ds(pl.multiple_of(info[CORE] * half, half), half)
            there = pl.ds(pl.multiple_of((1 - info[CORE]) * half, half), half)
            same_ref[...] = (near_ref[here, :].astype(f32) + got_ref[...].astype(f32)).astype(bf16)
            other_ref[...] = near_ref[there, :]

        same_y, other_y = small(add_y, [near_y, got_y], [keep_y, keep_y], info, (total1,))
        same_y = shift_y(same_y)
        carried = [jump(total2, 1), cross(total1)]
        side = both(up, down)
        mine, other_y = stage([(0, side, 0, carried)], [], [], through=[other_y])
        in_y = same_y, shift_y(other_y, True)
        other = swap_low(mine)
        part = mine

        def add_two(info, one_ref, two_ref, out_ref, top_ref):
            out_ref[...] = (one_ref[...].astype(f32) + two_ref[...].astype(f32)).astype(bf16)
            top_ref[...] = out_ref[:mid]

        half_part = jax.ShapeDtypeStruct((mid, quarter), bf16)
        final, top = small(add_two, [mine, other], [part, half_part], info)
        below, above = both(final, final)
        far_top = shift_x(top, 2)

        def cut_low(info, in_ref, out_ref):
            out_ref[...] = in_ref[mid:]

        (low,) = small(cut_low, [above], [half_part], info)
        far_low = shift_x(low, -1)

        def finish(info, keep_ref, one_ref, two_ref, key_ref, value_ref, end_ref):
            end_ref[...] = jnp.zeros_like(end_ref)
            sums = keep_ref[...].astype(f32) + one_ref[...].astype(f32) + two_ref[...].astype(f32)
            sums = sums.astype(bf16)
            for h in range(local_width // HEAD):
                at = 2 * h * HEAD
                key_ref[:, h * HEAD : (h + 1) * HEAD] = sums[:, at : at + HEAD]
                value_ref[:, h * HEAD : (h + 1) * HEAD] = sums[:, at + HEAD : at + 2 * HEAD]

        shard = jax.ShapeDtypeStruct((half, local_width), bf16)
        end = jax.ShapeDtypeStruct((16, 128), bf16)
        key_weight_grad, value_weight_grad, end = small(finish, [keep_y, *in_y], [shard, shard, end], info, (low,))

        def place(info, *refs):
            for ref, k in zip(refs[:-1], (0, 1, 3)):
                at = mod4(info[X] - k) * quarter
                refs[-1][:, pl.ds(pl.multiple_of(at, quarter), quarter)] = ref[...]

        whole_rows = jax.ShapeDtypeStruct((blk, width), bf16)
        (enc_grad,) = small(place, [final, below, above], [whole_rows], info, (low,))

        def place_last(info, top_ref, low_ref, _, __, out_ref):
            out_ref[:mid] = top_ref[...]
            out_ref[mid:] = low_ref[...]

        enc_grad = pl.pallas_call(
            place_last,
            grid_spec=pltpu.PrefetchScalarGridSpec(
                num_scalar_prefetch=1,
                grid=(1,),
                in_specs=[whole(half_part), whole(half_part), ANYWHERE, ANYWHERE],
                out_specs=pl.BlockSpec((blk, quarter), lambda i, info: (0, mod4(info[X] - 2))),
            ),
            out_shape=whole_rows,
            input_output_aliases={3: 0},
            compiler_params=params(8),
            cost_estimate=LIGHT,
        )(info, far_top, far_low, enc_grad, end)
        enc_grad = enc_grad[None]

        return (context, enc_grad, key_weight_grad[None], value_weight_grad[None])

    return shards


def solution(mesh):
    n_sec, n_dp, n_ten = (mesh.shape[name] for name in ("section", "dp", "tensor"))
    fine = Mesh(
        mesh.devices.reshape(n_sec, n_dp // 2, 2, XS, n_ten // XS), ("section", "y", "core", "x", "low")
    )
    dp, heads = ("y", "core"), ("x", "low")
    return jax.shard_map(
        make_shards(n_sec),
        mesh=fine,
        in_specs=(
            P(dp, "section", None),
            P("section", None, heads),
            P("section", None, heads),
            P("section", dp, None, heads),
            P("section", dp, None, heads),
            P(dp),
            P(dp),
        ),
        out_specs=(
            P("section", dp, None, heads),
            P(dp, "section", None),
            P("section", dp, heads),
            P("section", dp, heads),
        ),
        check_vma=False,
    )
```
